32 devices in a mesh: ad: 8 (over z, x), bn: 4 (over y, core).
Axes of the slice: x: 2, y: 2, z: 4, core: 2. Of those that a mesh axis runs over, the one named last changes fastest.
Arguments:
- hidden_in: bfloat16 [8192, 768], P(('ad', 'bn')), may hold values from -6 to 6
- lengths: int32 [32], P(('ad', 'bn')), may hold values from 16 to 256, as said below
- cotangent: bfloat16 [8192, 768], P(('ad', 'bn')), may hold values from -6 to 6
- w_qkv: bfloat16 [768, 2304], replicated, may hold values from -0.21875 to 0.21875
- w_out: bfloat16 [768, 768], replicated, may hold values from -1.75 to 1.75
- gain_attn: float32 [768], replicated, may hold values from 0.1 to 1.9
- w_ff_in: bfloat16 [768, 3072], replicated, may hold values from -0.21875 to 0.21875
- w_ff_out: bfloat16 [3072, 768], replicated, may hold values from -0.109375 to 0.109375
- gain_ff: float32 [768], replicated, may hold values from 0.1 to 1.9
- join_query: bfloat16 [768, 768], replicated, may hold values from -0.21875 to 0.21875
- join_key: bfloat16 [768, 768], replicated, may hold values from -0.21875 to 0.21875
- join_value: bfloat16 [768, 768], replicated, may hold values from -0.21875 to 0.21875
- adapt_down: bfloat16 [48, 16, 768], P('bn'), may hold values from -0.21875 to 0.21875
- adapt_up: bfloat16 [48, 16, 768], P('bn'), may hold values from -1.75 to 1.75
- gain_out: float32 [768], replicated, may hold values from 0.1 to 1.9
Outputs:
- output: float32 [8192, 768], P(('ad', 'bn'))
- grad_in: float32 [8192, 768], P(('ad', 'bn'))
- grad_w_qkv: float32 [768, 2304], P('bn', 'ad')
- grad_w_out: float32 [768, 768], P('bn', 'ad')
- grad_gain_attn: float32 [768], P('ad')
- grad_w_ff_in: float32 [768, 3072], P('bn', 'ad')
- grad_w_ff_out: float32 [3072, 768], P('bn', 'ad')
- grad_gain_ff: float32 [768], P('ad')
- grad_join_query: float32 [768, 768], P('bn', 'ad')
- grad_join_key: float32 [768, 768], P('bn', 'ad')
- grad_join_value: float32 [768, 768], P('bn', 'ad')
- grad_adapt_down: float32 [48, 16, 768], P('bn', None, 'ad')
- grad_adapt_up: float32 [48, 16, 768], P('bn', None, 'ad')
- grad_gain_out: float32 [768], P('ad')
The draws below stay inside these ranges and needn't reach their ends.
Inputs may be any that keep to these rules, and one draw needn't show every extreme that they name: Each sequence holds its real tokens in the first lengths slots of its 256; in every draw one sequence, chosen by the seed, fills all its slots.
All inputs are finite; a program needn't handle non-finite values.
Results may differ from the reference program's by a relative error of at most 0.04.
Values may be sent and summed in bfloat16 or wider, within the bound.
A program may use at most 192 MiB of HBM per device.

```python
import math
import jax
import jax.numpy as jnp
from jax import lax

D = 768
H = 12
FF = 3072
R = 48
A = 16
SEQ_LEN = 256
MIN_LEN = 16
SEQS = 32
TOKENS = 8192


def draw_lengths(key, part):
    key_base, key_pick = jax.random.split(jax.random.fold_in(key, 7))
    drawn_lens = jax.random.randint(key_base, (SEQS,), MIN_LEN, SEQ_LEN + 1)
    chosen = jax.random.randint(key_pick, (), 0, SEQS)
    return jnp.where(jnp.arange(SEQS) == chosen, SEQ_LEN, drawn_lens).astype(jnp.int32)


def raised(array, stream_key, source, target, parts, factor):
    owner, partner = [(jnp.arange(array.shape[dim]) // (array.shape[dim] // parts)).reshape([-1 if axis == dim else 1 for axis in range(array.ndim)]) for dim in (source, target)]
    chosen = jax.random.permutation(stream_key, parts)[partner]
    strong = (owner == chosen) | (owner == (partner + parts // 2) % parts)
    return jnp.where(strong, factor * array, array)


def shard_levels(stream_key, extent, pieces, low, high):
    level, own = 1.0, jax.random.fold_in(stream_key, 6)
    for dim, shards_of in pieces:
        steps = jnp.exp(jax.random.uniform(jax.random.fold_in(own, dim), (shards_of,), jnp.float32, low / len(pieces), high / len(pieces)))
        level = level * jnp.repeat(steps, extent[dim] // shards_of).reshape([-1 if axis == dim else 1 for axis in range(len(extent))])
    return level


def noise(own_key, shape, scale, reach, pieces=(), held_as=jnp.bfloat16):
    values = scale * jax.random.normal(own_key, shape, jnp.float32)
    if pieces:
        values = values * shard_levels(own_key, shape, pieces, -0.22, 0.18)
    return jnp.clip(values, -reach, reach).astype(held_as)


def heavy_noise(key, extent, scale, bound, cuts, heavy, held_as=jnp.bfloat16):
    array = scale * jax.random.normal(key, extent, jnp.float32)
    if cuts:
        array = array * shard_levels(key, extent, cuts, -0.22, 0.18)
    return jnp.clip(raised(array, jax.random.fold_in(key, 3), *heavy), -bound, bound).astype(held_as)


def setup_inputs(seed: int = 0) -> dict:
    keys = jax.random.split(jax.random.key(seed), 16)
    hidden_in = noise(keys[0], (TOKENS, D), 1.0, 6.0, ((0, 32),))
    lengths = draw_lengths(jax.random.fold_in(keys[15], 71), 0)
    cotangent = heavy_noise(keys[2], (TOKENS, D), 1.0, 6.0, ((0, 32),), (0, 1, 32, 2.75))
    w_qkv = noise(keys[3], (D, 3 * D), D ** -0.5, 0.21875)
    w_out = noise(keys[4], (D, D), (max(D // 64, 4)) ** -0.5, 1.75)
    gain_attn = jnp.clip(1.0 + 0.18 * jax.random.normal(keys[5], (D,), jnp.float32), 0.1, 1.9)
    w_ff_in = noise(keys[6], (D, FF), D ** -0.5, 0.21875)
    w_ff_out = noise(keys[7], (FF, D), FF ** -0.5, 0.109375)
    gain_ff = jnp.clip(1.0 + 0.18 * jax.random.normal(keys[8], (D,), jnp.float32), 0.1, 1.9)
    join_query = noise(keys[9], (D, D), D ** -0.5, 0.21875)
    join_key = noise(keys[10], (D, D), D ** -0.5, 0.21875)
    join_value = noise(keys[11], (D, D), D ** -0.5, 0.21875)
    adapt_down = noise(keys[12], (R, A, D), D ** -0.5, 0.21875, ((0, 4),))
    adapt_up = noise(keys[13], (R, A, D), (R // 4) ** -0.5, 1.75, ((0, 4),))
    gain_out = jnp.clip(1.0 + 0.18 * jax.random.normal(keys[14], (D,), jnp.float32), 0.1, 1.9)
    return dict(hidden_in=hidden_in, lengths=lengths, cotangent=cotangent, w_qkv=w_qkv, w_out=w_out, gain_attn=gain_attn, w_ff_in=w_ff_in, w_ff_out=w_ff_out, gain_ff=gain_ff, join_query=join_query, join_key=join_key, join_value=join_value, adapt_down=adapt_down, adapt_up=adapt_up, gain_out=gain_out)


@jax.custom_vjp
def low(v):
    return lax.optimization_barrier(v.astype(jnp.bfloat16)).astype(jnp.float32)

@jax.custom_vjp
def low_back(v):
    return v

def low_keep(v):
    return (low(v), None)

def low_pass(kept, grad):
    return (grad,)

def back_keep(v):
    return (v, None)

def back_low(kept, grad):
    return (low(grad),)
low.defvjp(low_keep, low_pass)
low_back.defvjp(back_keep, back_low)
epsilon = 1e-06
masked_value = -1000000000.0
highest = lax.Precision.HIGHEST

def layer_norm(values, gain):
    center = values - lax.optimization_barrier(jnp.mean(values, -1, keepdims=True))
    spread = lax.optimization_barrier(jnp.mean(center * center, -1, keepdims=True))
    return center * lax.rsqrt(spread + epsilon) * gain

def gelu_exact(values):
    return jax.nn.gelu(values, approximate=False)

def matmul(left, right):
    return jnp.dot(left, right, precision=highest)

def matmul_t(left, right):
    return jnp.dot(left, right.T, precision=highest)

def forward(tokens, slot_lens, w_qkv, w_out, gain_attn, w_ff_in, w_ff_out, gain_ff, join_query, join_key, join_value, adapt_down, adapt_up, gain_out):
    seq_count = slot_lens.shape[0]
    model_width = tokens.shape[1]
    row_count = tokens.shape[0]
    slot_len = row_count // seq_count
    head_size = model_width // H
    valid = jnp.arange(slot_len)[None, :] < slot_lens[:, None]
    qkv = low_back(matmul(tokens, w_qkv))
    queries = low(qkv[:, :model_width]).reshape(seq_count, slot_len, H, head_size)
    key_rows = low(qkv[:, model_width:2 * model_width]).reshape(seq_count, slot_len, H, head_size)
    values = low(qkv[:, 2 * model_width:]).reshape(seq_count, slot_len, H, head_size)
    scores = low_back(jnp.einsum('sqhe,skhe->shqk', queries, key_rows, precision=highest) / math.sqrt(head_size))
    scores = jnp.where(valid[:, None, None, :], scores, masked_value)
    probs = low(jax.nn.softmax(scores, -1))
    context = jnp.einsum('shqk,skhe->sqhe', probs, values, precision=highest).reshape(row_count, model_width)
    context = low(low_back(context))
    attn_out = low_back(matmul(context, w_out))
    hidden_one = layer_norm(tokens + attn_out, gain_attn)
    ff_pre = low_back(matmul(low(hidden_one), w_ff_in))
    ff_act = low(gelu_exact(ff_pre))
    ff_out = low_back(matmul(ff_act, w_ff_out))
    hidden_two = layer_norm(hidden_one + ff_out, gain_ff)
    hidden_low = low(hidden_two)
    query_join = low(low_back(matmul(hidden_low, join_query)))
    probe = low(low_back(matmul_t(query_join, join_key)))
    down_flat = adapt_down.reshape(-1, model_width)
    up_flat = adapt_up.reshape(-1, model_width)
    inner = low_back(matmul_t(hidden_low, down_flat))
    active = gelu_exact(inner)
    weigh = low_back(matmul_t(probe, up_flat))
    logits = lax.optimization_barrier(jnp.sum((active * weigh).reshape(row_count, -1, A), 1)) / math.sqrt(model_width)
    shares = jax.nn.softmax(logits, -1)
    mixing = low((shares[:, None, :] * active.reshape(row_count, -1, A)).reshape(row_count, -1))
    mixed = low_back(matmul(mixing, up_flat))
    joined_in = low(hidden_two + mixed)
    joined = low_back(matmul(joined_in, join_value))
    return layer_norm(hidden_two + joined, gain_out)

def reference(hidden_in, lengths, cotangent, w_qkv, w_out, gain_attn, w_ff_in, w_ff_out, gain_ff, join_query, join_key, join_value, adapt_down, adapt_up, gain_out):
    group = math.gcd(SEQS, 16)
    blocks = SEQS // group
    weights = tuple((item.astype(jnp.float32) for item in (w_qkv, w_out, gain_attn, w_ff_in, w_ff_out, gain_ff, join_query, join_key, join_value, adapt_down, adapt_up, gain_out)))
    tokens = hidden_in.astype(jnp.float32).reshape(blocks, group * SEQ_LEN, D)
    slot_lens = lengths.reshape(blocks, group)
    upstream = cotangent.astype(jnp.float32).reshape(blocks, group * SEQ_LEN, D)

    def one_block(carry, item):
        block_tokens, block_lens, block_up = item
        row_ok = (jnp.arange(SEQ_LEN)[None, :] < block_lens[:, None]).reshape(-1, 1).astype(jnp.float32)

        def apply_layer(token_rows, *params):
            return forward(token_rows, block_lens, *params)
        result, backward = jax.vjp(apply_layer, block_tokens, *weights)
        grads = backward(block_up * row_ok)
        summed = tuple((total + grad for total, grad in zip(carry, grads[1:])))
        return (summed, (result, grads[0]))
    initial = tuple((jnp.zeros_like(item) for item in weights))
    totals, (results, input_grads) = lax.scan(one_block, initial, (tokens, slot_lens, upstream))
    output = results.reshape(TOKENS, D)
    grad_in = input_grads.reshape(TOKENS, D)
    return (output, grad_in, totals[0], totals[1], totals[2], totals[3], totals[4], totals[5], totals[6], totals[7], totals[8], totals[9], totals[10], totals[11])
```

```python
import functools
import math

import jax
import jax.numpy as jnp
from jax import lax
from jax.experimental import pallas as pl
from jax.experimental.pallas import tpu as pltpu
from jax.sharding import PartitionSpec as P

H = 12


epsilon = 1e-06
masked_value = -1000000000.0
MESH = pl.DeviceIdType.MESH


def layer_norm(values, gain):
    center = values - jnp.mean(values, -1, keepdims=True)
    spread = jnp.mean(center * center, -1, keepdims=True)
    return center * lax.rsqrt(spread + epsilon) * gain


def gelu_exact(values):
    return jax.nn.gelu(values, approximate=False)


def matmul(left, right):
    return jnp.dot(left, right, preferred_element_type=jnp.float32)


def matmul_t(left, right):
    return lax.dot_general(
        left, right, (((1,), (1,)), ((), ())), preferred_element_type=jnp.float32
    )


def matmul_tn(left, right):
    return lax.dot_general(
        left, right, (((0,), (0,)), ((), ())), preferred_element_type=jnp.float32
    )


def adapter_forward(hidden, probe_rows, down_flat, up_flat, adapters):
    row_count, model_width = hidden.shape
    inner_pre = matmul_t(hidden, down_flat)
    active = gelu_exact(inner_pre)
    weigh_rows = matmul_t(probe_rows, up_flat)
    logits = jnp.sum((active * weigh_rows).reshape(row_count, -1, adapters), 1) / math.sqrt(
        model_width
    )
    shares = jax.nn.softmax(logits, -1)
    mixing = (
        (shares[:, None, :] * active.reshape(row_count, -1, adapters))
        .reshape(row_count, -1)
        .astype(jnp.bfloat16)
    )
    return (mixing, (inner_pre, active, weigh_rows, shares))


def adapter_backward(kept_state, up_flat, mix_grad, adapters):
    inner_pre, active, weigh_rows, shares = kept_state
    row_count, model_width = mix_grad.shape
    score_scale = 1.0 / math.sqrt(model_width)
    mix_in = matmul_t(mix_grad, up_flat).reshape(row_count, -1, adapters)
    active_three = active.reshape(row_count, -1, adapters)
    weigh_three = weigh_rows.reshape(row_count, -1, adapters)
    share_grad = jnp.sum(mix_in * active_three, 1)
    logit_grad = shares * (share_grad - jnp.sum(shares * share_grad, -1, keepdims=True))
    act_grad = mix_in * shares[:, None, :] + logit_grad[:, None, :] * score_scale * weigh_three
    weigh_grad = (
        (logit_grad[:, None, :] * score_scale * active_three)
        .reshape(row_count, -1)
        .astype(jnp.bfloat16)
    )
    unused, gelu_back = jax.vjp(gelu_exact, inner_pre)
    inner_grad = gelu_back(act_grad.reshape(row_count, -1))[0].astype(jnp.bfloat16)
    return (inner_grad, weigh_grad)


def flip(index, bit):
    return index + bit - 2 * bit * ((index // bit) % 2)


def reduce_kernel(
    products,
    rows_ref,
    cols_ref,
    gain_ref,
    out_ref,
    gain_out_ref,
    rows_sib,
    cols_sib,
    part,
    recv_one,
    recv_two,
    recv_three,
    gain_core,
    gain_x,
    gain_y,
    gain_z,
    core_send,
    core_recv,
    colx_send,
    colx_recv,
    one_send,
    one_recv,
    two_send,
    two_recv,
    three_send,
    three_recv,
    last_send,
    last_recv,
    gain_send,
    gain_recv,
):
    ad = lax.axis_index("ad")
    bn = lax.axis_index("bn")
    x, z = ad % 2, ad // 2
    core, y = bn % 2, bn // 2
    sibling = (ad, flip(bn, 1))
    x_mate = (flip(ad, 1), bn)
    y_mate = (ad, flip(bn, 2))
    z_index = [flip(z, 1), flip(z, 2), flip(flip(z, 1), 2)]
    z_mates = [(zz * 2 + x, bn) for zz in z_index]
    other_core, other_x, other_y = 1 - core, 1 - x, 1 - y

    barrier = pltpu.get_barrier_semaphore()
    for mate in [sibling, x_mate, y_mate] + z_mates:
        pl.semaphore_signal(barrier, inc=1, device_id=mate, device_id_type=MESH)
    pl.semaphore_wait(barrier, 6)

    started = []

    def send(source, target, send_sem, recv_sem, mate):
        copy = pltpu.make_async_remote_copy(
            src_ref=source,
            dst_ref=target,
            send_sem=send_sem,
            recv_sem=recv_sem,
            device_id=mate,
            device_id_type=MESH,
        )
        copy.start()
        started.append(copy)
        return copy

    core_copies = {}
    seen = {}
    for terms in products:
        for left, right in terms:
            if left not in core_copies:
                core_copies[left] = send(
                    rows_ref.at[left, other_core],
                    rows_sib.at[left],
                    core_send.at[left],
                    core_recv.at[left],
                    sibling,
                )
            if right not in seen:
                seen[right] = send(
                    cols_ref.at[right],
                    cols_sib.at[right],
                    colx_send.at[right],
                    colx_recv.at[right],
                    sibling,
                )
    gain_copy = send(gain_ref, gain_core, gain_send.at[0], gain_recv.at[0], sibling)
    arrived = set()

    def half(unit, side):
        total = None
        for left, right in products[unit]:
            if (0, left) not in arrived:
                core_copies[left].wait_recv()
                arrived.add((0, left))
            if (1, right) not in arrived:
                seen[right].wait_recv()
                arrived.add((1, right))
            term = matmul(rows_ref[left, core, side], cols_ref[right])
            term += matmul(rows_sib[left, side], cols_sib[right])
            total = term if total is None else total + term
        total = total.astype(jnp.bfloat16).reshape(4, 48, total.shape[1])
        width = total.shape[2] // 2
        part[unit, 0, side] = total[:, :, :width]
        part[unit, 1, side] = total[:, :, width:]

    one = {}
    two = {}
    three = {}
    last = {}
    units = len(products)

    def stage_one(unit):
        if unit % 2 == 0:
            half(unit, other_x)
            one[unit] = send(
                part.at[unit, :, other_x],
                recv_one.at[unit],
                one_send.at[unit],
                one_recv.at[unit],
                x_mate,
            )
            half(unit, x)
        else:
            half(unit, 0)
            half(unit, 1)
            one[unit] = send(
                part.at[unit, other_y],
                recv_one.at[unit],
                one_send.at[unit],
                one_recv.at[unit],
                y_mate,
            )

    def add_low(left, right):
        return (left.astype(jnp.float32) + right.astype(jnp.float32)).astype(jnp.bfloat16)

    def stage_two(unit):
        one[unit].wait_recv()
        if unit % 2 == 0:
            part[unit, other_y, x] = add_low(part[unit, other_y, x], recv_one[unit, other_y])
            two[unit] = send(
                part.at[unit, other_y, x],
                recv_two.at[unit],
                two_send.at[unit],
                two_recv.at[unit],
                y_mate,
            )
            part[unit, y, x] = add_low(part[unit, y, x], recv_one[unit, y])
        else:
            part[unit, y, other_x] = add_low(part[unit, y, other_x], recv_one[unit, other_x])
            two[unit] = send(
                part.at[unit, y, other_x],
                recv_two.at[unit],
                two_send.at[unit],
                two_recv.at[unit],
                x_mate,
            )
            part[unit, y, x] = add_low(part[unit, y, x], recv_one[unit, x])

    def stage_three(unit):
        two[unit].wait_recv()
        part[unit, y, x] = add_low(part[unit, y, x], recv_two[unit])
        three[unit] = [
            send(
                part.at[unit, y, x, z_index[k]],
                recv_three.at[unit, k],
                three_send.at[unit, k],
                three_recv.at[unit, k],
                z_mates[k],
            )
            for k in range(3)
        ]

    def stage_four(unit):
        total = part[unit, y, x, z].astype(jnp.float32)
        for k in range(3):
            three[unit][k].wait_recv()
            total += recv_three[unit, k].astype(jnp.float32)
        out_ref[unit, core] = total.astype(jnp.bfloat16)
        last[unit] = send(
            out_ref.at[unit, core],
            out_ref.at[unit, core],
            last_send.at[unit],
            last_recv.at[unit],
            sibling,
        )

    for step in range(units + 7):
        if step == 4:
            gain_copy.wait_recv()
            gain_core[...] = gain_core[...] + gain_ref[...]
            gain_copy = send(
                gain_core.at[other_x], gain_x, gain_send.at[1], gain_recv.at[1], x_mate
            )
        if step == 6:
            gain_copy.wait_recv()
            gain_x[...] = gain_x[...] + gain_core[x]
            gain_copy = send(gain_x, gain_y, gain_send.at[2], gain_recv.at[2], y_mate)
        if step == 8:
            gain_copy.wait_recv()
            gain_y[...] = gain_y[...] + gain_x[...]
            gain_copies = [
                send(
                    gain_y.at[z_index[k]],
                    gain_z.at[k],
                    gain_send.at[3 + k],
                    gain_recv.at[3 + k],
                    z_mates[k],
                )
                for k in range(3)
            ]
        if step == 10:
            gain_total = gain_y[z]
            for k in range(3):
                gain_copies[k].wait_recv()
                gain_total += gain_z[k]
            gain_out_ref[...] = gain_total
        if step < units:
            stage_one(step)
        if 0 <= step - 3 < units:
            stage_two(step - 3)
        if 0 <= step - 5 < units:
            stage_three(step - 5)
        if 0 <= step - 7 < units:
            stage_four(step - 7)
    for unit in range(units):
        last[unit].wait_recv()
    for copy in started:
        copy.wait_send()


def reduce_units(products, row_factors, col_factors, gain_rows):
    lefts, cores, xs, zs, piece, tokens = row_factors.shape
    rights, tokens, width = col_factors.shape
    units = len(products)
    half_width = width // 2
    low = jnp.bfloat16
    dma = pltpu.SemaphoreType.DMA
    row_factors = row_factors.reshape(lefts, cores, xs, zs * piece, tokens)
    return pl.pallas_call(
        functools.partial(reduce_kernel, products),
        out_shape=(
            jax.ShapeDtypeStruct((units, cores, piece, half_width), low),
            jax.ShapeDtypeStruct(gain_rows.shape[2:], jnp.float32),
        ),
        in_specs=[pl.BlockSpec(memory_space=pltpu.VMEM)] * 3,
        out_specs=[pl.BlockSpec(memory_space=pltpu.VMEM)] * 2,
        scratch_shapes=[
            pltpu.VMEM((lefts, xs, zs * piece, tokens), low),
            pltpu.VMEM(col_factors.shape, low),
            pltpu.VMEM((units, 2, xs, zs, piece, half_width), low),
            pltpu.VMEM((units, 2, zs, piece, half_width), low),
            pltpu.VMEM((units, zs, piece, half_width), low),
            pltpu.VMEM((units, 3, piece, half_width), low),
            pltpu.VMEM(gain_rows.shape, jnp.float32),
            pltpu.VMEM(gain_rows.shape[1:], jnp.float32),
            pltpu.VMEM(gain_rows.shape[1:], jnp.float32),
            pltpu.VMEM((3,) + gain_rows.shape[2:], jnp.float32),
            dma((lefts,)),
            dma((lefts,)),
            dma((rights,)),
            dma((rights,)),
            dma((units,)),
            dma((units,)),
            dma((units,)),
            dma((units,)),
            dma((units, 3)),
            dma((units, 3)),
            dma((units,)),
            dma((units,)),
            dma((6,)),
            dma((6,)),
        ],
        compiler_params=pltpu.CompilerParams(
            collective_id=0, has_side_effects=True, vmem_limit_bytes=60 * 2**20
        ),
    )(row_factors, col_factors, gain_rows)


def row_units(factor, unit_count):
    tokens = factor.shape[0]
    piece = factor.shape[1] // (8 * unit_count * 2)
    cut = factor.reshape(tokens, 4, 2, unit_count, 2, piece)
    return jnp.transpose(cut, (3, 4, 2, 1, 5, 0))


def col_units(factor, unit_count):
    tokens = factor.shape[0]
    cut = factor.reshape(tokens, 2, unit_count, -1)
    return jnp.transpose(cut, (2, 0, 1, 3)).reshape(unit_count, tokens, -1)


def fast_sums(pairs, gains):
    row_parts, col_parts, products = [], [], []
    row_at, col_at = {}, {}
    for terms in pairs:
        unit_terms = None
        for row_name, row_factor, row_count, col_name, col_factor, col_count in terms:
            if row_name not in row_at:
                row_at[row_name] = len(row_parts)
                row_parts += list(row_units(row_factor, row_count))
            if col_name not in col_at:
                col_at[col_name] = len(col_parts)
                col_parts += list(col_units(col_factor, col_count))
            count = max(row_count, col_count)
            entries = [
                (
                    row_at[row_name] + (k if row_count > 1 else 0),
                    col_at[col_name] + (k if col_count > 1 else 0),
                )
                for k in range(count)
            ]
            if unit_terms is None:
                unit_terms = [[entry] for entry in entries]
            else:
                for listed, entry in zip(unit_terms, entries):
                    listed.append(entry)
        products += [tuple(listed) for listed in unit_terms]
    stacked = jnp.stack(gains).reshape(3, 4, 2, -1)
    stacked = jnp.transpose(stacked, (2, 1, 0, 3))
    gain_rows = jnp.pad(stacked, ((0, 0), (0, 0), (0, 5), (0, 128 - stacked.shape[3])))
    sums, gain_sums = reduce_units(
        tuple(products), jnp.stack(row_parts), jnp.stack(col_parts), gain_rows
    )
    units, cores, piece, width = sums.shape
    return sums.reshape(units, cores * piece, width), gain_sums[:3, : stacked.shape[3]]


def local(
    sizes,
    hidden_in,
    lengths,
    cotangent,
    w_qkv,
    w_out,
    gain_attn,
    w_ff_in,
    w_ff_out,
    gain_ff,
    join_query,
    join_key,
    join_value,
    adapt_down,
    adapt_up,
    gain_out,
):
    seq_count = lengths.shape[0]
    tok_rows, model_width = hidden_in.shape
    slot_len = tok_rows // seq_count
    head_count = H
    head_size = model_width // head_count
    score_scale = 1.0 / math.sqrt(head_size)
    adapters = adapt_down.shape[1]
    down_flat = lax.all_gather(adapt_down.reshape(-1, model_width), "bn", axis=0, tiled=True)
    up_flat = lax.all_gather(adapt_up.reshape(-1, model_width), "bn", axis=0, tiled=True)
    valid = lax.broadcasted_iota(jnp.int32, (seq_count, slot_len), 1) < lengths[:, None]
    row_ok = valid.reshape(tok_rows, 1).astype(jnp.float32)
    tokens_wide = hidden_in.astype(jnp.float32)
    qkv = matmul(hidden_in, w_qkv).astype(jnp.bfloat16)
    queries = qkv[:, :model_width].reshape(seq_count, slot_len, head_count, head_size)
    key_rows = qkv[:, model_width : 2 * model_width].reshape(
        seq_count, slot_len, head_count, head_size
    )
    values = qkv[:, 2 * model_width :].reshape(seq_count, slot_len, head_count, head_size)

    def attend_scores():
        raw_scores = (
            jnp.einsum("sqhe,skhe->shqk", queries, key_rows, preferred_element_type=jnp.float32)
            * score_scale
        )
        return jnp.where(valid[:, None, None, :], raw_scores, masked_value)

    scores = attend_scores()
    row_max = jnp.max(scores, -1, keepdims=True)
    log_total = row_max + jnp.log(jnp.sum(jnp.exp(scores - row_max), -1, keepdims=True))
    probs = jnp.exp(scores - log_total).astype(jnp.bfloat16)
    context = (
        jnp.einsum("shqk,skhe->sqhe", probs, values, preferred_element_type=jnp.float32)
        .reshape(tok_rows, model_width)
        .astype(jnp.bfloat16)
    )
    attn_out = matmul(context, w_out)
    hidden_one, norm_one_back = jax.vjp(layer_norm, tokens_wide + attn_out, gain_attn)
    hidden_one_low = hidden_one.astype(jnp.bfloat16)
    ff_pre = matmul(hidden_one_low, w_ff_in)
    ff_act, gelu_ff_back = jax.vjp(gelu_exact, ff_pre)
    ff_low = ff_act.astype(jnp.bfloat16)
    ff_out = matmul(ff_low, w_ff_out)
    hidden_two, norm_two_back = jax.vjp(layer_norm, hidden_one + ff_out, gain_ff)
    hidden_low = hidden_two.astype(jnp.bfloat16)
    query_join = matmul(hidden_low, join_query).astype(jnp.bfloat16)
    probe = matmul_t(query_join, join_key).astype(jnp.bfloat16)
    mixing, kept_state = adapter_forward(hidden_low, probe, down_flat, up_flat, adapters)
    joined_in = (hidden_two + matmul(mixing, up_flat)).astype(jnp.bfloat16)
    joined = matmul(joined_in, join_value)
    output, norm_out_back = jax.vjp(layer_norm, hidden_two + joined, gain_out)
    out_grad = cotangent.astype(jnp.float32) * row_ok
    sum_three, gain_out_grad = norm_out_back(out_grad)
    joined_grad = sum_three.astype(jnp.bfloat16)
    into_joined = matmul_t(joined_grad, join_value)
    mix_grad = into_joined.astype(jnp.bfloat16)
    inner_grad, weigh_grad = adapter_backward(kept_state, up_flat, mix_grad, adapters)
    hidden_back = matmul(inner_grad, down_flat)
    probe_grad = matmul(weigh_grad, up_flat).astype(jnp.bfloat16)
    query_in = matmul(probe_grad, join_key).astype(jnp.bfloat16)
    grad_two = sum_three + into_joined + hidden_back + matmul_t(query_in, join_query)
    sum_two, gain_ff_grad = norm_two_back(grad_two)
    ff_out_grad = sum_two.astype(jnp.bfloat16)
    ff_pre_grad = gelu_ff_back(matmul_t(ff_out_grad, w_ff_out))[0].astype(jnp.bfloat16)
    grad_one = sum_two + matmul_t(ff_pre_grad, w_ff_in)
    sum_one, gain_attn_grad = norm_one_back(grad_one)
    attn_grad = sum_one.astype(jnp.bfloat16)
    context_grad = (
        matmul_t(attn_grad, w_out)
        .astype(jnp.bfloat16)
        .reshape(seq_count, slot_len, head_count, head_size)
    )
    probs_wide = jnp.exp(attend_scores() - log_total)
    prob_grad = jnp.einsum(
        "sqhe,skhe->shqk", context_grad, values, preferred_element_type=jnp.float32
    )
    row_delta = jnp.sum(probs_wide * prob_grad, -1, keepdims=True)
    score_grad = (probs_wide * (prob_grad - row_delta)).astype(jnp.bfloat16)
    query_back = (
        jnp.einsum("shqk,skhe->sqhe", score_grad, key_rows, preferred_element_type=jnp.float32)
        * score_scale
    )
    key_back = (
        jnp.einsum("shqk,sqhe->skhe", score_grad, queries, preferred_element_type=jnp.float32)
        * score_scale
    )
    value_back = jnp.einsum(
        "shqk,sqhe->skhe", probs, context_grad, preferred_element_type=jnp.float32
    )
    qkv_grad = jnp.concatenate(
        [
            query_back.reshape(tok_rows, model_width),
            key_back.reshape(tok_rows, model_width),
            value_back.reshape(tok_rows, model_width),
        ],
        1,
    ).astype(jnp.bfloat16)
    grad_in = sum_one + matmul_t(qkv_grad, w_qkv)
    if sizes == (8, 4):
        pairs = [
            [("joined_grad", joined_grad, 1, "joined_in", joined_in, 1)],
            [
                ("mix_grad", mix_grad, 1, "mixing", mixing, 1),
                ("probe", probe, 1, "weigh_grad", weigh_grad, 1),
            ],
            [("hidden_low", hidden_low, 1, "inner_grad", inner_grad, 1)],
            [("query_join", query_join, 1, "probe_grad", probe_grad, 1)],
            [("query_in", query_in, 1, "hidden_low", hidden_low, 1)],
            [("ff_out_grad", ff_out_grad, 1, "ff_low", ff_low, 4)],
            [("ff_pre_grad", ff_pre_grad, 4, "hidden_one", hidden_one_low, 1)],
            [("attn_grad", attn_grad, 1, "context", context, 1)],
            [("qkv_grad", qkv_grad, 3, "hidden_in", hidden_in, 1)],
        ]
        sums, gain_sums = fast_sums(pairs, (gain_attn_grad, gain_ff_grad, gain_out_grad))
        core = lax.axis_index("bn") % 2
        width = sums.shape[2] // 2
        mine = lax.dynamic_slice_in_dim(sums, core * width, width, 2).astype(jnp.float32)

        def columns(first, count):
            return jnp.transpose(mine[first : first + count], (2, 0, 1)).reshape(width, -1)

        ff_rows = lax.dynamic_slice_in_dim(sums[5:9], core * 2, 2, 0).astype(jnp.float32)
        ff_down_grad = jnp.transpose(ff_rows, (0, 2, 1)).reshape(-1, sums.shape[1])
        bank = (width // adapters, adapters, -1)
        return (
            output,
            grad_in,
            columns(14, 3),
            columns(13, 1),
            gain_sums[0],
            columns(9, 4),
            ff_down_grad,
            gain_sums[1],
            columns(4, 1),
            columns(3, 1),
            columns(0, 1),
            columns(2, 1).reshape(bank),
            columns(1, 1).reshape(bank),
            gain_sums[2],
        )

    def shared_sum(gradient):
        columns = lax.psum_scatter(gradient, "ad", scatter_dimension=1, tiled=True)
        return lax.psum_scatter(
            columns.astype(jnp.bfloat16), "bn", scatter_dimension=0, tiled=True
        ).astype(jnp.float32)

    gains = lax.psum(
        lax.psum_scatter(
            jnp.stack([gain_attn_grad, gain_ff_grad, gain_out_grad]),
            "ad",
            scatter_dimension=1,
            tiled=True,
        ),
        "bn",
    )
    down_grad = shared_sum(matmul_tn(inner_grad, hidden_low))
    up_grad = shared_sum(matmul_tn(mixing, mix_grad) + matmul_tn(weigh_grad, probe))
    bank = adapt_down.shape[:2] + (-1,)
    return (
        output,
        grad_in,
        shared_sum(matmul_tn(hidden_in, qkv_grad)),
        shared_sum(matmul_tn(context, attn_grad)),
        gains[0],
        shared_sum(matmul_tn(hidden_one_low, ff_pre_grad)),
        shared_sum(matmul_tn(ff_low, ff_out_grad)),
        gains[1],
        shared_sum(matmul_tn(hidden_low, query_in)),
        shared_sum(matmul_tn(probe_grad, query_join)),
        shared_sum(matmul_tn(joined_in, joined_grad)),
        down_grad.reshape(bank),
        up_grad.reshape(bank),
        gains[2],
    )


def solution(mesh):
    placed = (
        P(("ad", "bn"), None),
        P(("ad", "bn")),
        P(("ad", "bn"), None),
        P(),
        P(),
        P(),
        P(),
        P(),
        P(),
        P(),
        P(),
        P(),
        P("bn", None, None),
        P("bn", None, None),
        P(),
    )
    sizes = (mesh.shape["ad"], mesh.shape["bn"])
    return jax.shard_map(
        functools.partial(local, sizes),
        mesh=mesh,
        in_specs=placed,
        out_specs=(
            P(("ad", "bn"), None),
            P(("ad", "bn"), None),
            P("bn", "ad"),
            P("bn", "ad"),
            P("ad"),
            P("bn", "ad"),
            P("bn", "ad"),
            P("ad"),
            P("bn", "ad"),
            P("bn", "ad"),
            P("bn", "ad"),
            P("bn", None, "ad"),
            P("bn", None, "ad"),
            P("ad"),
        ),
        check_vma=False,
    )
```

```python
import functools
import math

import jax
import jax.numpy as jnp
from jax import lax
from jax.experimental import pallas as pl
from jax.experimental.pallas import tpu as pltpu
from jax.sharding import PartitionSpec as P

H = 12


epsilon = 1e-06
masked_value = -1000000000.0
MESH = pl.DeviceIdType.MESH


def layer_norm(values, gain):
    center = values - jnp.mean(values, -1, keepdims=True)
    spread = jnp.mean(center * center, -1, keepdims=True)
    return center * lax.rsqrt(spread + epsilon) * gain


def gelu_exact(values):
    return jax.nn.gelu(values, approximate=False)


def matmul(left, right):
    return jnp.dot(left, right, preferred_element_type=jnp.float32)


def matmul_t(left, right):
    return lax.dot_general(
        left, right, (((1,), (1,)), ((), ())), preferred_element_type=jnp.float32
    )


def matmul_tn(left, right):
    return lax.dot_general(
        left, right, (((0,), (0,)), ((), ())), preferred_element_type=jnp.float32
    )


def adapter_forward(hidden, probe_rows, down_flat, up_flat, adapters):
    row_count, model_width = hidden.shape
    inner_pre = matmul_t(hidden, down_flat)
    active = gelu_exact(inner_pre)
    weigh_rows = matmul_t(probe_rows, up_flat)
    logits = jnp.sum((active * weigh_rows).reshape(row_count, -1, adapters), 1) / math.sqrt(
        model_width
    )
    shares = jax.nn.softmax(logits, -1)
    mixing = (
        (shares[:, None, :] * active.reshape(row_count, -1, adapters))
        .reshape(row_count, -1)
        .astype(jnp.bfloat16)
    )
    return (mixing, (inner_pre, active, weigh_rows, shares))


def adapter_backward(kept_state, up_flat, mix_grad, adapters):
    inner_pre, active, weigh_rows, shares = kept_state
    row_count, model_width = mix_grad.shape
    score_scale = 1.0 / math.sqrt(model_width)
    mix_in = matmul_t(mix_grad, up_flat).reshape(row_count, -1, adapters)
    active_three = active.reshape(row_count, -1, adapters)
    weigh_three = weigh_rows.reshape(row_count, -1, adapters)
    share_grad = jnp.sum(mix_in * active_three, 1)
    logit_grad = shares * (share_grad - jnp.sum(shares * share_grad, -1, keepdims=True))
    act_grad = mix_in * shares[:, None, :] + logit_grad[:, None, :] * score_scale * weigh_three
    weigh_grad = (
        (logit_grad[:, None, :] * score_scale * active_three)
        .reshape(row_count, -1)
        .astype(jnp.bfloat16)
    )
    unused, gelu_back = jax.vjp(gelu_exact, inner_pre)
    inner_grad = gelu_back(act_grad.reshape(row_count, -1))[0].astype(jnp.bfloat16)
    return (inner_grad, weigh_grad)


PIECE = 48
SLOTS = 5
LAG_TWO = 4
LAG_THREE = 6
LAG_FOUR = 8
UNITS = (
    ((0, 8),),
    ((1, 9), (2, 10)),
    ((3, 11),),
    ((4, 12),),
    ((5, 7),),
    ((6, 3),),
    ((6, 4),),
    ((6, 5),),
    ((6, 6),),
    ((8, 2),),
    ((9, 2),),
    ((10, 2),),
    ((11, 2),),
    ((7, 1),),
    ((12, 0),),
    ((13, 0),),
    ((14, 0),),
)


def flip(index, bit):
    return index + bit - 2 * bit * ((index // bit) % 2)


def normal_parts(values):
    cdf = 0.5 * (1.0 + lax.erf(values * (1.0 / math.sqrt(2.0))))
    density = jnp.exp(values * values * -0.5) * (1.0 / math.sqrt(2.0 * math.pi))
    return cdf, density


def layer_kernel(
    heads,
    adapters,
    hidden,
    lengths,
    cotangent,
    w_qkv,
    w_out,
    gain_attn,
    w_ff_in,
    w_ff_out,
    gain_ff,
    join_query,
    join_key,
    join_value,
    adapt_down,
    adapt_up,
    gain_out,
    output,
    grad_in,
    sums,
    gain_sums,
    rows,
    rows_ff,
    rows_qkv,
    rows_sib,
    cols,
    cols_sib,
    ring,
    banks,
    acc,
    acc_two,
    wide,
    acc_t,
    acc_t_two,
    active,
    bank_slope,
    second,
    norm_one,
    norm_two,
    slope,
    qkv_t,
    probs,
    low_tmp,
    low_tmp_two,
    stat,
    stat_one,
    stat_two,
    gain_col,
    part,
    recv_one,
    recv_two,
    recv_three,
    gain_sum,
    gain_from,
    ring_sem,
    local_sem,
    bank_send,
    bank_recv,
    row_send,
    row_recv,
    col_send,
    col_recv,
    one_send,
    one_recv,
    two_send,
    two_recv,
    three_send,
    three_recv,
    last_send,
    last_recv,
    gain_send,
    gain_recv,
):
    low = jnp.bfloat16
    tokens, width = hidden.shape
    half_width = width // 2
    blocks = rows.shape[1] * rows.shape[2] * rows.shape[3]
    ad = lax.axis_index("ad")
    bn = lax.axis_index("bn")
    x, z = ad % 2, ad // 2
    core, y = bn % 2, bn // 2
    sibling = (ad, flip(bn, 1))
    x_mate = (flip(ad, 1), bn)
    y_mate = (ad, flip(bn, 2))
    z_index = [flip(z, 1), flip(z, 2), flip(flip(z, 1), 2)]
    z_mates = [(zz * 2 + x, bn) for zz in z_index]
    other_core, other_x, other_y = 1 - core, 1 - x, 1 - y

    loads = [(w_qkv.at[:, pl.ds(k * width, width)]) for k in range(3)] + [w_out]
    for k in range(4):
        loads.append(w_ff_in.at[:, pl.ds(k * width, width)])
        loads.append(w_ff_out.at[pl.ds(k * width, width), :])
    loads += [join_query, join_key, join_value]
    for k in range(4):
        loads.append(w_ff_out.at[pl.ds(k * width, width), :])
        loads.append(w_ff_in.at[:, pl.ds(k * width, width)])
    loads += [w_out] + [w_qkv.at[:, pl.ds(k * width, width)] for k in range(3)]
    free_slots = list(range(SLOTS))
    in_flight = []
    next_load = [0]

    def fill():
        while free_slots and next_load[0] < len(loads):
            slot = free_slots.pop(0)
            copy = pltpu.make_async_copy(loads[next_load[0]], ring.at[slot], ring_sem.at[slot])
            copy.start()
            in_flight.append((slot, copy))
            next_load[0] += 1

    def take():
        slot, copy = in_flight.pop(0)
        copy.wait()
        return slot

    def release(slot):
        free_slots.append(slot)
        fill()

    fill()
    bank_own = []
    for i, bank in enumerate((adapt_down, adapt_up)):
        bank_own.append(pltpu.make_async_copy(bank, banks.at[i, bn], local_sem.at[i]))
        bank_own[i].start()

    barrier = pltpu.get_barrier_semaphore()
    for mate in [sibling, x_mate, y_mate] + z_mates:
        pl.semaphore_signal(barrier, inc=1, device_id=mate, device_id_type=MESH)
    pl.semaphore_wait(barrier, 6)

    started = []

    def send(source, target, send_sem, recv_sem, mate):
        copy = pltpu.make_async_remote_copy(
            src_ref=source,
            dst_ref=target,
            send_sem=send_sem,
            recv_sem=recv_sem,
            device_id=mate,
            device_id_type=MESH,
        )
        copy.start()
        started.append(copy)
        return copy

    bank_sib, bank_y, bank_far = [], [], []
    for i, bank in enumerate((adapt_down, adapt_up)):
        bank_y.append(
            send(bank, banks.at[i, bn], bank_send.at[i, 1], bank_recv.at[i, 1], y_mate)
        )
    for i, bank in enumerate((adapt_down, adapt_up)):
        bank_sib.append(
            send(bank, banks.at[i, bn], bank_send.at[i, 0], bank_recv.at[i, 0], sibling)
        )

    def row_views(index):
        if index < 8:
            return rows.at[index]
        if index < 12:
            return rows_ff.at[:, :, index - 8]
        return rows_qkv.at[:, :, index - 12]

    def row_half(index, side):
        if index < 8:
            piece = rows[index, :, side, core]
        elif index < 12:
            piece = rows_ff[:, side, index - 8, core]
        else:
            piece = rows_qkv[:, side, index - 12, core]
        return piece.reshape(4 * PIECE, tokens)

    def col_ref(index):
        return hidden if index == 0 else cols.at[index - 1]

    row_copies, col_copies = {}, {}
    arrived = set()

    def share_row(index):
        row_copies[index] = send(
            row_views(index).at[:, :, other_core],
            rows_sib.at[index],
            row_send.at[index],
            row_recv.at[index],
            sibling,
        )

    def share_col(index):
        col_copies[index] = send(
            col_ref(index),
            cols_sib.at[index],
            col_send.at[index],
            col_recv.at[index],
            sibling,
        )

    one, two, three, last = {}, {}, {}, {}
    units = len(UNITS)

    def half(unit, side):
        total = None
        for left, right in UNITS[unit]:
            if (0, left) not in arrived:
                row_copies[left].wait_recv()
                arrived.add((0, left))
            if (1, right) not in arrived:
                col_copies[right].wait_recv()
                arrived.add((1, right))
            term = matmul(row_half(left, side), col_ref(right)[...])
            term += matmul(
                rows_sib[left, :, side].reshape(4 * PIECE, tokens), cols_sib[right]
            )
            total = term if total is None else total + term
        total = total.astype(low).reshape(4, PIECE, width)
        part[unit, 0, side] = total[:, :, :half_width]
        part[unit, 1, side] = total[:, :, half_width:]

    def stage_one(unit):
        if unit % 2 == 0:
            half(unit, other_x)
            one[unit] = send(
                part.at[unit, :, other_x],
                recv_one.at[unit],
                one_send.at[unit],
                one_recv.at[unit],
                x_mate,
            )
            half(unit, x)
        else:
            half(unit, 0)
            half(unit, 1)
            one[unit] = send(
                part.at[unit, other_y],
                recv_one.at[unit],
                one_send.at[unit],
                one_recv.at[unit],
                y_mate,
            )

    def add_low(left, right):
        return (left.astype(jnp.float32) + right.astype(jnp.float32)).astype(low)

    def stage_two(unit):
        one[unit].wait_recv()
        if unit % 2 == 0:
            part[unit, other_y, x] = add_low(part[unit, other_y, x], recv_one[unit, other_y])
            two[unit] = send(
                part.at[unit, other_y, x],
                recv_two.at[unit],
                two_send.at[unit],
                two_recv.at[unit],
                y_mate,
            )
            part[unit, y, x] = add_low(part[unit, y, x], recv_one[unit, y])
        else:
            part[unit, y, other_x] = add_low(part[unit, y, other_x], recv_one[unit, other_x])
            two[unit] = send(
                part.at[unit, y, other_x],
                recv_two.at[unit],
                two_send.at[unit],
                two_recv.at[unit],
                x_mate,
            )
            part[unit, y, x] = add_low(part[unit, y, x], recv_one[unit, x])

    def stage_three(unit):
        two[unit].wait_recv()
        part[unit, y, x] = add_low(part[unit, y, x], recv_two[unit])
        three[unit] = [
            send(
                part.at[unit, y, x, z_index[k]],
                recv_three.at[unit, k],
                three_send.at[unit, k],
                three_recv.at[unit, k],
                z_mates[k],
            )
            for k in range(3)
        ]

    def stage_four(unit):
        total = part[unit, y, x, z].astype(jnp.float32)
        for k in range(3):
            three[unit][k].wait_recv()
            total += recv_three[unit, k].astype(jnp.float32)
        sums[unit, core] = total.astype(low)
        last[unit] = send(
            sums.at[unit, core],
            sums.at[unit, core],
            last_send.at[unit],
            last_recv.at[unit],
            sibling,
        )

    def reduce_step(step):
        if step < units:
            stage_one(step)
        if 0 <= step - LAG_TWO < units:
            stage_two(step - LAG_TWO)
        if 0 <= step - LAG_THREE < units:
            stage_three(step - LAG_THREE)
        if 0 <= step - LAG_FOUR < units:
            stage_four(step - LAG_FOUR)

    step_rows = 32
    row_steps = tokens // step_rows

    def over_rows(body, init=0):
        def step(i, carry):
            return body(pl.ds(pl.multiple_of(i * step_rows, step_rows), step_rows), i, carry)

        return lax.fori_loop(0, row_steps, step, init)

    def over_pieces(body, init=0):
        return lax.fori_loop(0, blocks, body, init)

    def spot(p):
        return p // 4, (p // 2) % 2, p % 2

    def put_t(index, value):
        rows[index] = value.reshape(4, 2, 2, PIECE, tokens)

    def get_t(index):
        return rows[index].reshape(width, tokens)

    def fold(value):
        return value.reshape(PIECE // 8, 8, tokens).sum(0)

    share_col(0)
    length = lengths[0]
    for k in range(3):
        slot = take()
        value = matmul(hidden[...], ring[slot])
        release(slot)
        if k == 0:
            value = value * 0.125
        qkv_t[pl.ds(k * width, width), :] = value.astype(low).T
    size = width // heads

    def head_rows(k, head):
        return pl.ds(pl.multiple_of(k * width + head * size, size), size)

    valid_keys = lax.broadcasted_iota(jnp.int32, (tokens, tokens), 0) < length

    def head_forward(head, carry):
        scores = matmul_tn(qkv_t[head_rows(1, head), :], qkv_t[head_rows(0, head), :])
        scores = jnp.where(valid_keys, scores, masked_value)
        scores = jnp.exp(scores - jnp.max(scores, 0, keepdims=True))
        share = (scores * (1.0 / jnp.sum(scores, 0, keepdims=True))).astype(low)
        probs[head] = share
        context = matmul(qkv_t[head_rows(2, head), :], share)
        low_tmp_two[pl.ds(pl.multiple_of(head * size, size), size), :] = context.astype(low)
        return carry

    lax.fori_loop(0, heads, head_forward, 0)
    cols[0] = low_tmp_two[...].T
    share_col(1)
    slot = take()
    acc[...] = matmul(cols[0], ring[slot])
    release(slot)

    def norm_rows(total):
        center = total - jnp.mean(total, -1, keepdims=True)
        rstd = lax.rsqrt(jnp.mean(center * center, -1, keepdims=True) + epsilon)
        return center * rstd, rstd

    def norm_first(r, i, carry):
        normed, rstd = norm_rows(hidden[r, :].astype(jnp.float32) + acc[r, :])
        stat[r, :] = jnp.broadcast_to(rstd, (step_rows, 128))
        low_tmp[r, :] = normed.astype(low)
        one_rows = normed * gain_attn[...]
        wide[r, :] = one_rows
        cols[1, r, :] = one_rows.astype(low)
        return carry

    over_rows(norm_first)
    share_col(2)
    norm_one[...] = low_tmp[...].T.reshape(blocks, PIECE, tokens)
    stat_one[...] = stat[...].T[:8]

    for k in range(4):
        slot = take()
        acc[...] = matmul(cols[1], ring[slot])
        release(slot)
        unit_base = 2 + (k % 2) * 2
        lanes = pl.ds((k // 2) * half_width, half_width)

        def gelu_rows(r, i, carry):
            before = acc[r, :]
            cdf, density = normal_parts(before)
            act = (before * cdf).astype(low)
            low_tmp[r, :] = act
            cols[unit_base, r, lanes] = act[:, :half_width]
            cols[unit_base + 1, r, lanes] = act[:, half_width:]
            cols[9, r, :] = (cdf + before * density).astype(low)
            return carry

        over_rows(gelu_rows)
        slope[pl.ds(k * blocks, blocks)] = cols[9].T.reshape(blocks, PIECE, tokens)
        slot = take()
        value = matmul(low_tmp[...], ring[slot])
        release(slot)
        acc_two[...] = value if k == 0 else acc_two[...] + value
        if k == 1:
            for i in range(2):
                bank_y[i].wait_recv()
                far = flip(bn, 2)
                bank_far.append(
                    send(
                        banks.at[i, far],
                        banks.at[i, far],
                        bank_send.at[i, 2],
                        bank_recv.at[i, 2],
                        sibling,
                    )
                )
    for index in range(3, 7):
        share_col(index)

    def norm_second(r, i, carry):
        normed, rstd = norm_rows(wide[r, :] + acc_two[r, :])
        stat[r, :] = jnp.broadcast_to(rstd, (step_rows, 128))
        low_tmp[r, :] = normed.astype(low)
        two_rows = normed * gain_ff[...]
        wide[r, :] = two_rows
        cols[6, r, :] = two_rows.astype(low)
        return carry

    over_rows(norm_second)
    share_col(7)
    norm_two[...] = low_tmp[...].T.reshape(blocks, PIECE, tokens)
    stat_two[...] = stat[...].T[:8]
    put_t(3, cols[6].T)
    share_row(3)

    slot_query = take()
    low_tmp[...] = matmul(cols[6], ring[slot_query]).astype(low)
    put_t(4, low_tmp[...].T)
    share_row(4)
    slot_key = take()
    put_t(2, matmul(ring[slot_key], get_t(4)).astype(low))
    share_row(2)

    for i in range(2):
        bank_own[i].wait()
        bank_sib[i].wait_recv()
        bank_far[i].wait_recv()
    acc_t[...] = matmul(banks[0].reshape(width, width), get_t(3)).reshape(blocks, PIECE, tokens)
    acc_t_two[...] = matmul(banks[1].reshape(width, width), get_t(2)).reshape(
        blocks, PIECE, tokens
    )
    score_scale = 1.0 / math.sqrt(width)
    groups = PIECE // adapters

    def grouped(value):
        return value.reshape(groups, adapters, tokens)

    def adapter_rows(p, logits):
        inner = acc_t[p]
        cdf, density = normal_parts(inner)
        act = inner * cdf
        active[p] = act
        bank_slope[p] = (cdf + inner * density).astype(low)
        return logits + grouped(act * acc_t_two[p]).sum(0)

    logits = over_pieces(adapter_rows, jnp.zeros((adapters, tokens), jnp.float32)) * score_scale
    logits = jnp.exp(logits - jnp.max(logits, 0, keepdims=True))
    shares = logits / jnp.sum(logits, 0, keepdims=True)

    def spread(value):
        return jnp.concatenate([value] * groups, 0)

    wide_shares = spread(shares)

    def mixing_rows(p, carry):
        low_tmp_two[pl.ds(pl.multiple_of(p * PIECE, PIECE), PIECE), :] = (
            wide_shares * active[p]
        ).astype(low)
        return carry

    over_pieces(mixing_rows)
    cols[8] = low_tmp_two[...].T
    share_col(9)
    acc[...] = matmul(cols[8], banks[1].reshape(width, width))

    def joined_rows(r, i, carry):
        cols[7, r, :] = (wide[r, :] + acc[r, :]).astype(low)
        return carry

    over_rows(joined_rows)
    share_col(8)
    slot_value = take()
    acc[...] = matmul(cols[7], ring[slot_value])

    def norm_third(r, i, gain_part):
        normed, rstd = norm_rows(wide[r, :] + acc[r, :])
        gain = gain_out[...]
        acc_two[r, :] = normed * gain
        token = lax.broadcasted_iota(jnp.int32, (step_rows, 1), 0) + i * step_rows
        upstream = jnp.where(token < length, cotangent[r, :].astype(jnp.float32), 0.0)
        product = upstream * normed
        gained = upstream * gain
        third = rstd * (
            gained
            - jnp.mean(gained, -1, keepdims=True)
            - normed * jnp.mean(gained * normed, -1, keepdims=True)
        )
        low_tmp[r, :] = third.astype(low)
        return gain_part + product.reshape(step_rows // 8, 8, width).sum(0)

    gain_part = over_rows(norm_third, jnp.zeros((8, width), jnp.float32))
    out_copy = pltpu.make_async_copy(acc_two, output, local_sem.at[2])
    out_copy.start()
    gain_sum[0] = jnp.broadcast_to(jnp.sum(gain_part, 0, keepdims=True), (8, width))
    put_t(0, low_tmp[...].T)
    share_row(0)

    second[...] = matmul(ring[slot_value], get_t(0)).reshape(blocks, PIECE, tokens)
    release(slot_value)

    def mix_rows(p, carry):
        zz, xx, cc = spot(p)
        rows[1, zz, xx, cc] = second[p].astype(low)
        return carry

    over_pieces(mix_rows)
    share_row(1)

    acc_t[...] = matmul(banks[1].reshape(width, width), get_t(1)).reshape(blocks, PIECE, tokens)
    reduce_step(0)

    def share_rows(p, total):
        return total + grouped(acc_t[p] * active[p]).sum(0)

    share_grad = over_pieces(share_rows, jnp.zeros((adapters, tokens), jnp.float32))
    logit_grad = shares * (share_grad - jnp.sum(shares * share_grad, 0, keepdims=True))
    wide_logit = spread(logit_grad * score_scale)

    def adapter_back(p, carry):
        act_grad = acc_t[p] * wide_shares + wide_logit * acc_t_two[p]
        where = pl.ds(pl.multiple_of(p * PIECE, PIECE), PIECE)
        low_tmp_two[where, :] = (wide_logit * active[p]).astype(low)
        bank_slope[p] = (bank_slope[p].astype(jnp.float32) * act_grad).astype(low)
        return carry

    over_pieces(adapter_back)
    cols[9] = low_tmp_two[...].T
    share_col(10)
    cols[10] = bank_slope[...].reshape(width, tokens).T
    share_col(11)
    cols[11] = matmul(cols[9], banks[1].reshape(width, width)).astype(low)
    share_col(12)
    low_tmp[...] = matmul(cols[11], ring[slot_key]).astype(low)
    release(slot_key)
    put_t(5, low_tmp[...].T)
    share_row(5)
    low_tmp[...] = matmul(cols[10], banks[0].reshape(width, width)).astype(low)
    low_tmp_two[...] = low_tmp[...].T
    acc_t[...] = matmul(ring[slot_query], get_t(5)).reshape(blocks, PIECE, tokens)
    release(slot_query)
    reduce_step(1)

    reduce_step(2)

    def norm_back(index, gain, normed_ref, stat_ref, upstream_of, factor):
        gain_col[...] = jnp.broadcast_to(gain[...], (128, width)).T.reshape(blocks, PIECE, 128)

        def gained(p):
            column = gain_col[p]
            return acc_t[p] * jnp.concatenate([column] * (tokens // 128), 1)

        def first_pass(p, carry):
            upstream = upstream_of(p)
            acc_t[p] = upstream
            normed = normed_ref[p].astype(jnp.float32)
            gain_of = jnp.sum(upstream * normed, -1, keepdims=True)
            weighted = gained(p)
            gain_col[p] = jnp.broadcast_to(gain_of, (PIECE, 128))
            acc_t[p] = weighted
            return carry[0] + fold(weighted), carry[1] + fold(weighted * normed)

        zeros = jnp.zeros((8, tokens), jnp.float32)
        plain, tilted = over_pieces(first_pass, (zeros, zeros))
        mean_plain = jnp.sum(plain, 0, keepdims=True) * (1.0 / width)
        mean_tilted = jnp.sum(tilted, 0, keepdims=True) * (1.0 / width)
        rstd = stat_ref[0:1, :]

        def second_pass(p, carry):
            value = rstd * (acc_t[p] - mean_plain - normed_ref[p].astype(jnp.float32) * mean_tilted)
            second[p] = value
            zz, xx, cc = spot(p)
            rows[factor, zz, xx, cc] = value.astype(low)
            return carry

        over_pieces(second_pass)
        gain_sum[0, index : index + 1, :] = gain_col[...].reshape(width, 128).T[:1]

    def upstream_two(p):
        zz, xx, cc = spot(p)
        where = pl.ds(pl.multiple_of(p * PIECE, PIECE), PIECE)
        total = rows[0, zz, xx, cc].astype(jnp.float32) + second[p]
        return total + low_tmp_two[where, :].astype(jnp.float32) + acc_t[p]

    norm_back(1, gain_ff, norm_two, stat_two, upstream_two, 6)
    share_row(6)
    reduce_step(3)
    reduce_step(4)

    for k in range(4):
        slot = take()
        acc_t_two[...] = matmul(ring[slot], get_t(6)).reshape(blocks, PIECE, tokens)
        release(slot)

        def slope_rows(p, carry):
            value = acc_t_two[p] * slope[k * blocks + p].astype(jnp.float32)
            rows_ff[k, p // 8, (p % 8) // 2, p % 2] = value.astype(low)
            return carry

        over_pieces(slope_rows)
        slot = take()
        value = matmul(ring[slot], rows_ff[k].reshape(width, tokens))
        value = value.reshape(blocks, PIECE, tokens)
        release(slot)
        acc_t[...] = value if k == 0 else acc_t[...] + value
        reduce_step(5 + k)
    for index in range(8, 12):
        share_row(index)

    def upstream_one(p):
        return second[p] + acc_t[p]

    norm_back(0, gain_attn, norm_one, stat_one, upstream_one, 7)
    share_row(7)
    gain_copy = send(gain_sum.at[0], gain_from.at[0], gain_send.at[0], gain_recv.at[0], sibling)
    slot = take()
    low_tmp_two[...] = matmul(ring[slot], get_t(7)).astype(low)
    release(slot)
    reduce_step(9)

    heads_step = 3
    step_pieces = heads_step * size // PIECE

    def head_backward(group, carry):
        grads = [[], [], []]
        for i in range(heads_step):
            head = group * heads_step + i
            query, key, value = [qkv_t[head_rows(k, head), :] for k in range(3)]
            upstream = low_tmp_two[pl.ds(pl.multiple_of(head * size, size), size), :]
            share = probs[head]
            share_wide = share.astype(jnp.float32)
            prob_grad = matmul_tn(value, upstream)
            delta = jnp.sum(share_wide * prob_grad, 0, keepdims=True)
            score_grad = (share_wide * (prob_grad - delta)).astype(low)
            grads[0].append((matmul(key, score_grad) * 0.125).astype(low))
            grads[1].append(matmul_t(query, score_grad).astype(low))
            grads[2].append(matmul_t(upstream, share).astype(low))
        for k in range(3):
            stacked = jnp.concatenate(grads[k], 0).reshape(step_pieces, PIECE, tokens)
            for i in range(step_pieces):
                p = k * blocks + group * step_pieces + i
                rows_qkv[p // 12, (p // 6) % 2, (p % 6) // 2, p % 2] = stacked[i]
        return carry

    lax.fori_loop(0, heads // heads_step, head_backward, 0)
    for index in range(12, 15):
        share_row(index)
    for step in range(10, 14):
        reduce_step(step)
    gain_copy.wait_recv()
    gain_sum[1] = gain_sum[0] + gain_from[0]
    gain_copy = send(gain_sum.at[1], gain_from.at[1], gain_send.at[1], gain_recv.at[1], x_mate)
    reduce_step(14)
    reduce_step(15)
    reduce_step(16)
    for k in range(3):
        slot = take()
        block = rows_qkv[...].reshape(3 * blocks, PIECE, tokens)[k * blocks : (k + 1) * blocks]
        value = matmul(ring[slot], block.reshape(width, tokens)).reshape(blocks, PIECE, tokens)
        release(slot)
        second[...] = second[...] + value
    acc[...] = second[...].reshape(width, tokens).T
    in_copy = pltpu.make_async_copy(acc, grad_in, local_sem.at[3])
    in_copy.start()

    for step in range(units, units + LAG_FOUR):
        reduce_step(step)
        if step == units:
            gain_copy.wait_recv()
            gain_sum[2] = gain_sum[1] + gain_from[1]
            gain_copy = send(
                gain_sum.at[2], gain_from.at[2], gain_send.at[2], gain_recv.at[2], y_mate
            )
        if step == units + 2:
            gain_copy.wait_recv()
            gain_sum[3] = gain_sum[2] + gain_from[2]
            gain_copies = [
                send(
                    gain_sum.at[3],
                    gain_from.at[3 + k],
                    gain_send.at[3 + k],
                    gain_recv.at[3 + k],
                    z_mates[k],
                )
                for k in range(3)
            ]
        if step == units + 5:
            total = gain_sum[3]
            for k in range(3):
                gain_copies[k].wait_recv()
                total += gain_from[3 + k]
            gain_sums[...] = total
    for unit in range(units):
        last[unit].wait_recv()
    for copy in started:
        copy.wait_send()
    out_copy.wait()
    in_copy.wait()


def run_layer(heads, adapters, arrays):
    hidden = arrays[0]
    tokens, width = hidden.shape
    low, wide = jnp.bfloat16, jnp.float32
    blocks = width // PIECE
    units = len(UNITS)
    dma = pltpu.SemaphoreType.DMA
    vmem = pl.BlockSpec(memory_space=pltpu.VMEM)
    smem = pl.BlockSpec(memory_space=pltpu.SMEM)
    far = pl.BlockSpec(memory_space=pl.ANY)
    half_width = width // 2
    pair = lambda shape: [dma(shape), dma(shape)]
    return pl.pallas_call(
        functools.partial(layer_kernel, heads, adapters),
        out_shape=(
            jax.ShapeDtypeStruct((tokens, width), wide),
            jax.ShapeDtypeStruct((tokens, width), wide),
            jax.ShapeDtypeStruct((units, 2, PIECE, half_width), low),
            jax.ShapeDtypeStruct((8, width), wide),
        ),
        in_specs=[
            vmem, smem, vmem, far, far, vmem, far, far, vmem, far, far, far, far, far, vmem,
        ],
        out_specs=[far, far, vmem, vmem],
        scratch_shapes=[
            pltpu.VMEM((8, 4, 2, 2, PIECE, tokens), low),
            pltpu.VMEM((4, 2, 4, 2, PIECE, tokens), low),
            pltpu.VMEM((4, 2, 3, 2, PIECE, tokens), low),
            pltpu.VMEM((15, 4, 2, PIECE, tokens), low),
            pltpu.VMEM((12, tokens, width), low),
            pltpu.VMEM((13, tokens, width), low),
            pltpu.VMEM((SLOTS, width, width), low),
            pltpu.VMEM((2, 4, width // 4, width), low),
            pltpu.VMEM((tokens, width), wide),
            pltpu.VMEM((tokens, width), wide),
            pltpu.VMEM((tokens, width), wide),
            pltpu.VMEM((blocks, PIECE, tokens), wide),
            pltpu.VMEM((blocks, PIECE, tokens), wide),
            pltpu.VMEM((blocks, PIECE, tokens), wide),
            pltpu.VMEM((blocks, PIECE, tokens), low),
            pltpu.VMEM((blocks, PIECE, tokens), wide),
            pltpu.VMEM((blocks, PIECE, tokens), low),
            pltpu.VMEM((blocks, PIECE, tokens), low),
            pltpu.VMEM((4 * blocks, PIECE, tokens), low),
            pltpu.VMEM((3 * width, tokens), low),
            pltpu.VMEM((heads, tokens, tokens), low),
            pltpu.VMEM((tokens, width), low),
            pltpu.VMEM((width, tokens), low),
            pltpu.VMEM((tokens, 128), wide),
            pltpu.VMEM((8, tokens), wide),
            pltpu.VMEM((8, tokens), wide),
            pltpu.VMEM((blocks, PIECE, 128), wide),
            pltpu.VMEM((units, 2, 2, 4, PIECE, half_width), low),
            pltpu.VMEM((units, 2, 4, PIECE, half_width), low),
            pltpu.VMEM((units, 4, PIECE, half_width), low),
            pltpu.VMEM((units, 3, PIECE, half_width), low),
            pltpu.VMEM((4, 8, width), wide),
            pltpu.VMEM((6, 8, width), wide),
            dma((SLOTS,)),
            dma((4,)),
        ]
        + pair((2, 3))
        + pair((15,))
        + pair((13,))
        + pair((units,))
        + pair((units,))
        + pair((units, 3))
        + pair((units,))
        + pair((6,)),
        compiler_params=pltpu.CompilerParams(
            collective_id=0, has_side_effects=True, vmem_limit_bytes=63 * 2**20
        ),
    )(*arrays)


def finish_kernel(
    sums,
    gain_sums,
    out_qkv,
    out_proj,
    out_gain_attn,
    out_ff_in,
    out_ff_out,
    out_gain_ff,
    out_query,
    out_key,
    out_value,
    out_down,
    out_up,
    out_gain_out,
    turned,
):
    ad = lax.axis_index("ad")
    core = lax.axis_index("bn") % 2
    width = sums.shape[3]
    own = pl.ds(pl.multiple_of(core * (width // 2), width // 2), width // 2)

    def columns(out, slot, first, count):
        value = sums[first : first + count].reshape(count * 2 * PIECE, width)
        extent = pl.ds(0, count * 2 * PIECE)
        turned[slot, :, extent] = value.astype(jnp.float32).T
        out[...] = turned[slot, own, extent]

    columns(out_value, 0, 0, 1)
    columns(out_up, 1, 1, 1)
    columns(out_down, 2, 2, 1)
    columns(out_key, 0, 3, 1)
    columns(out_query, 1, 4, 1)
    columns(out_ff_in, 2, 9, 4)
    columns(out_proj, 0, 13, 1)
    columns(out_qkv, 1, 14, 3)
    for i in range(2):
        value = sums[5 + 2 * core + i].reshape(2 * PIECE, width)
        out_ff_out[pl.ds(i * width, width), :] = value.astype(jnp.float32).T
    total = gain_sums.shape[1]
    piece = out_gain_attn.shape[1]
    rolled = pltpu.roll(gain_sums[...], lax.rem(total - ad * piece, total), 1)[:, :piece]
    out_gain_attn[...] = rolled[0:1]
    out_gain_ff[...] = rolled[1:2]
    out_gain_out[...] = rolled[2:3]


def finish(sums, gain_sums, width):
    quarter, eighth = width // 4, width // 8
    shapes = [
        (quarter, 3 * eighth),
        (quarter, eighth),
        (1, eighth),
        (quarter, 4 * eighth),
        (4 * quarter, eighth),
        (1, eighth),
    ]
    shapes += [(quarter, eighth)] * 5 + [(1, eighth)]
    return pl.pallas_call(
        finish_kernel,
        out_shape=tuple(jax.ShapeDtypeStruct(shape, jnp.float32) for shape in shapes),
        in_specs=[pl.BlockSpec(memory_space=pltpu.VMEM)] * 2,
        out_specs=[pl.BlockSpec(memory_space=pltpu.VMEM)] * 12,
        scratch_shapes=[pltpu.VMEM((3, width // 2, 4 * eighth), jnp.float32)],
        compiler_params=pltpu.CompilerParams(vmem_limit_bytes=32 * 2**20),
    )(sums, gain_sums)


def fast_local(*arrays):
    arrays = list(arrays)
    width = arrays[0].shape[1]
    adapters = arrays[12].shape[1]
    for i in (5, 8, 14):
        arrays[i] = arrays[i].reshape(1, width)
    bank_shape = arrays[12].shape[:2] + (-1,)
    for i in (12, 13):
        arrays[i] = arrays[i].reshape(-1, width)
    output, grad_in, sums, gain_sums = run_layer(H, adapters, arrays)
    grads = list(finish(sums, gain_sums, width))
    for i in (2, 5, 11):
        grads[i] = grads[i].reshape(-1)
    for i in (9, 10):
        grads[i] = grads[i].reshape(bank_shape)
    return (output, grad_in, *grads)


def local(
    hidden_in,
    lengths,
    cotangent,
    w_qkv,
    w_out,
    gain_attn,
    w_ff_in,
    w_ff_out,
    gain_ff,
    join_query,
    join_key,
    join_value,
    adapt_down,
    adapt_up,
    gain_out,
):
    seq_count = lengths.shape[0]
    tok_rows, model_width = hidden_in.shape
    slot_len = tok_rows // seq_count
    head_count = H
    head_size = model_width // head_count
    score_scale = 1.0 / math.sqrt(head_size)
    adapters = adapt_down.shape[1]
    down_flat = lax.all_gather(adapt_down.reshape(-1, model_width), "bn", axis=0, tiled=True)
    up_flat = lax.all_gather(adapt_up.reshape(-1, model_width), "bn", axis=0, tiled=True)
    valid = lax.broadcasted_iota(jnp.int32, (seq_count, slot_len), 1) < lengths[:, None]
    row_ok = valid.reshape(tok_rows, 1).astype(jnp.float32)
    tokens_wide = hidden_in.astype(jnp.float32)
    qkv = matmul(hidden_in, w_qkv).astype(jnp.bfloat16)
    queries = qkv[:, :model_width].reshape(seq_count, slot_len, head_count, head_size)
    key_rows = qkv[:, model_width : 2 * model_width].reshape(
        seq_count, slot_len, head_count, head_size
    )
    values = qkv[:, 2 * model_width :].reshape(seq_count, slot_len, head_count, head_size)

    def attend_scores():
        raw_scores = (
            jnp.einsum("sqhe,skhe->shqk", queries, key_rows, preferred_element_type=jnp.float32)
            * score_scale
        )
        return jnp.where(valid[:, None, None, :], raw_scores, masked_value)

    scores = attend_scores()
    row_max = jnp.max(scores, -1, keepdims=True)
    log_total = row_max + jnp.log(jnp.sum(jnp.exp(scores - row_max), -1, keepdims=True))
    probs = jnp.exp(scores - log_total).astype(jnp.bfloat16)
    context = (
        jnp.einsum("shqk,skhe->sqhe", probs, values, preferred_element_type=jnp.float32)
        .reshape(tok_rows, model_width)
        .astype(jnp.bfloat16)
    )
    attn_out = matmul(context, w_out)
    hidden_one, norm_one_back = jax.vjp(layer_norm, tokens_wide + attn_out, gain_attn)
    hidden_one_low = hidden_one.astype(jnp.bfloat16)
    ff_pre = matmul(hidden_one_low, w_ff_in)
    ff_act, gelu_ff_back = jax.vjp(gelu_exact, ff_pre)
    ff_low = ff_act.astype(jnp.bfloat16)
    ff_out = matmul(ff_low, w_ff_out)
    hidden_two, norm_two_back = jax.vjp(layer_norm, hidden_one + ff_out, gain_ff)
    hidden_low = hidden_two.astype(jnp.bfloat16)
    query_join = matmul(hidden_low, join_query).astype(jnp.bfloat16)
    probe = matmul_t(query_join, join_key).astype(jnp.bfloat16)
    mixing, kept_state = adapter_forward(hidden_low, probe, down_flat, up_flat, adapters)
    joined_in = (hidden_two + matmul(mixing, up_flat)).astype(jnp.bfloat16)
    joined = matmul(joined_in, join_value)
    output, norm_out_back = jax.vjp(layer_norm, hidden_two + joined, gain_out)
    out_grad = cotangent.astype(jnp.float32) * row_ok
    sum_three, gain_out_grad = norm_out_back(out_grad)
    joined_grad = sum_three.astype(jnp.bfloat16)
    into_joined = matmul_t(joined_grad, join_value)
    mix_grad = into_joined.astype(jnp.bfloat16)
    inner_grad, weigh_grad = adapter_backward(kept_state, up_flat, mix_grad, adapters)
    hidden_back = matmul(inner_grad, down_flat)
    probe_grad = matmul(weigh_grad, up_flat).astype(jnp.bfloat16)
    query_in = matmul(probe_grad, join_key).astype(jnp.bfloat16)
    grad_two = sum_three + into_joined + hidden_back + matmul_t(query_in, join_query)
    sum_two, gain_ff_grad = norm_two_back(grad_two)
    ff_out_grad = sum_two.astype(jnp.bfloat16)
    ff_pre_grad = gelu_ff_back(matmul_t(ff_out_grad, w_ff_out))[0].astype(jnp.bfloat16)
    grad_one = sum_two + matmul_t(ff_pre_grad, w_ff_in)
    sum_one, gain_attn_grad = norm_one_back(grad_one)
    attn_grad = sum_one.astype(jnp.bfloat16)
    context_grad = (
        matmul_t(attn_grad, w_out)
        .astype(jnp.bfloat16)
        .reshape(seq_count, slot_len, head_count, head_size)
    )
    probs_wide = jnp.exp(attend_scores() - log_total)
    prob_grad = jnp.einsum(
        "sqhe,skhe->shqk", context_grad, values, preferred_element_type=jnp.float32
    )
    row_delta = jnp.sum(probs_wide * prob_grad, -1, keepdims=True)
    score_grad = (probs_wide * (prob_grad - row_delta)).astype(jnp.bfloat16)
    query_back = (
        jnp.einsum("shqk,skhe->sqhe", score_grad, key_rows, preferred_element_type=jnp.float32)
        * score_scale
    )
    key_back = (
        jnp.einsum("shqk,sqhe->skhe", score_grad, queries, preferred_element_type=jnp.float32)
        * score_scale
    )
    value_back = jnp.einsum(
        "shqk,sqhe->skhe", probs, context_grad, preferred_element_type=jnp.float32
    )
    qkv_grad = jnp.concatenate(
        [
            query_back.reshape(tok_rows, model_width),
            key_back.reshape(tok_rows, model_width),
            value_back.reshape(tok_rows, model_width),
        ],
        1,
    ).astype(jnp.bfloat16)
    grad_in = sum_one + matmul_t(qkv_grad, w_qkv)
    def shared_sum(gradient):
        columns = lax.psum_scatter(gradient, "ad", scatter_dimension=1, tiled=True)
        return lax.psum_scatter(
            columns.astype(jnp.bfloat16), "bn", scatter_dimension=0, tiled=True
        ).astype(jnp.float32)

    gains = lax.psum(
        lax.psum_scatter(
            jnp.stack([gain_attn_grad, gain_ff_grad, gain_out_grad]),
            "ad",
            scatter_dimension=1,
            tiled=True,
        ),
        "bn",
    )
    down_grad = shared_sum(matmul_tn(inner_grad, hidden_low))
    up_grad = shared_sum(matmul_tn(mixing, mix_grad) + matmul_tn(weigh_grad, probe))
    bank = adapt_down.shape[:2] + (-1,)
    return (
        output,
        grad_in,
        shared_sum(matmul_tn(hidden_in, qkv_grad)),
        shared_sum(matmul_tn(context, attn_grad)),
        gains[0],
        shared_sum(matmul_tn(hidden_one_low, ff_pre_grad)),
        shared_sum(matmul_tn(ff_low, ff_out_grad)),
        gains[1],
        shared_sum(matmul_tn(hidden_low, query_in)),
        shared_sum(matmul_tn(probe_grad, query_join)),
        shared_sum(matmul_tn(joined_in, joined_grad)),
        down_grad.reshape(bank),
        up_grad.reshape(bank),
        gains[2],
    )


def solution(mesh):
    placed = (
        P(("ad", "bn"), None),
        P(("ad", "bn")),
        P(("ad", "bn"), None),
        P(),
        P(),
        P(),
        P(),
        P(),
        P(),
        P(),
        P(),
        P(),
        P("bn", None, None),
        P("bn", None, None),
        P(),
    )
    sizes = (mesh.shape["ad"], mesh.shape["bn"])
    return jax.shard_map(
        fast_local if sizes == (8, 4) else local,
        mesh=mesh,
        in_specs=placed,
        out_specs=(
            P(("ad", "bn"), None),
            P(("ad", "bn"), None),
            P("bn", "ad"),
            P("bn", "ad"),
            P("ad"),
            P("bn", "ad"),
            P("bn", "ad"),
            P("ad"),
            P("bn", "ad"),
            P("bn", "ad"),
            P("bn", "ad"),
            P("bn", None, "ad"),
            P("bn", None, "ad"),
            P("ad"),
        ),
        check_vma=False,
    )
```

```python
import functools
import math

import jax
import jax.numpy as jnp
from jax import lax
from jax.experimental import pallas as pl
from jax.experimental.pallas import tpu as pltpu
from jax.sharding import PartitionSpec as P

H = 12


epsilon = 1e-06
masked_value = -1000000000.0
MESH = pl.DeviceIdType.MESH


def layer_norm(values, gain):
    center = values - jnp.mean(values, -1, keepdims=True)
    spread = jnp.mean(center * center, -1, keepdims=True)
    return center * lax.rsqrt(spread + epsilon) * gain


def gelu_exact(values):
    return jax.nn.gelu(values, approximate=False)


def matmul(left, right):
    return jnp.dot(left, right, preferred_element_type=jnp.float32)


def matmul_t(left, right):
    return lax.dot_general(
        left, right, (((1,), (1,)), ((), ())), preferred_element_type=jnp.float32
    )


def matmul_tn(left, right):
    return lax.dot_general(
        left, right, (((0,), (0,)), ((), ())), preferred_element_type=jnp.float32
    )


def adapter_forward(hidden, probe_rows, down_flat, up_flat, adapters):
    row_count, model_width = hidden.shape
    inner_pre = matmul_t(hidden, down_flat)
    active = gelu_exact(inner_pre)
    weigh_rows = matmul_t(probe_rows, up_flat)
    logits = jnp.sum((active * weigh_rows).reshape(row_count, -1, adapters), 1) / math.sqrt(
        model_width
    )
    shares = jax.nn.softmax(logits, -1)
    mixing = (
        (shares[:, None, :] * active.reshape(row_count, -1, adapters))
        .reshape(row_count, -1)
        .astype(jnp.bfloat16)
    )
    return (mixing, (inner_pre, active, weigh_rows, shares))


def adapter_backward(kept_state, up_flat, mix_grad, adapters):
    inner_pre, active, weigh_rows, shares = kept_state
    row_count, model_width = mix_grad.shape
    score_scale = 1.0 / math.sqrt(model_width)
    mix_in = matmul_t(mix_grad, up_flat).reshape(row_count, -1, adapters)
    active_three = active.reshape(row_count, -1, adapters)
    weigh_three = weigh_rows.reshape(row_count, -1, adapters)
    share_grad = jnp.sum(mix_in * active_three, 1)
    logit_grad = shares * (share_grad - jnp.sum(shares * share_grad, -1, keepdims=True))
    act_grad = mix_in * shares[:, None, :] + logit_grad[:, None, :] * score_scale * weigh_three
    weigh_grad = (
        (logit_grad[:, None, :] * score_scale * active_three)
        .reshape(row_count, -1)
        .astype(jnp.bfloat16)
    )
    unused, gelu_back = jax.vjp(gelu_exact, inner_pre)
    inner_grad = gelu_back(act_grad.reshape(row_count, -1))[0].astype(jnp.bfloat16)
    return (inner_grad, weigh_grad)


PIECE = 48
SLOTS = 5
UNITS = (
    ((0, 8),),
    ((1, 9), (2, 10)),
    ((3, 11),),
    ((4, 12),),
    ((5, 7),),
    ((6, 3),),
    ((6, 4),),
    ((6, 5),),
    ((6, 6),),
    ((8, 2),),
    ((9, 2),),
    ((10, 2),),
    ((11, 2),),
    ((7, 1),),
    ((12, 0),),
    ((13, 0),),
    ((14, 0),),
)


ORDERS = (
    ("y", "x", "l", "h"),
    ("l", "y", "x", "h"),
    ("x", "l", "h", "y"),
    ("y", "x", "l", "h"),
    ("y", "l", "x", "h"),
    ("y", "l", "x", "h"),
    ("l", "x", "y", "h"),
    ("x", "l", "h", "y"),
    ("y", "x", "l", "h"),
    ("x", "l", "h", "y"),
    ("x", "l", "y", "h"),
    ("l", "x", "h", "y"),
    ("y", "x", "l", "h"),
    ("x", "y", "l", "h"),
    ("y", "x", "l", "h"),
    ("y", "l", "x", "h"),
    ("x", "y", "l", "h"),
)
SEQUENCE = (
    -1, -1, 0, -1, 2, 1, -1, 3, -1, 7, 6, 8, -1, -1, -1, 0, -1, 2, 9, 11, 4, -1, 13, 5,
    -1, 2, 16, 0, 15, 7, 9, 10, 14, 0, 4, 7, 5, 12, 0, 3, 9, 15, 4, 11, 10, 5, 2, 7, 3,
    8, 9, 16, 4, 15, 13, 11, 14, 2, 5, 3, 7, 4, 9, 10, 6, 1, 8, 16, 5, 15, 12, 11, 3, 8,
    13, 16, 14, 15, 10, 8, 13, 6, 16, 1, 11, 14, 10, 12, 6, 13, 1, 14, 12, 6, 1, 12,
)

def flip(index, bit):
    return index + bit - 2 * bit * ((index // bit) % 2)


def normal_parts(values):
    cdf = 0.5 * (1.0 + lax.erf(values * (1.0 / math.sqrt(2.0))))
    density = jnp.exp(values * values * -0.5) * (1.0 / math.sqrt(2.0 * math.pi))
    return cdf, density


def layer_kernel(
    heads,
    adapters,
    hidden,
    lengths,
    cotangent,
    w_qkv,
    w_out,
    gain_attn,
    w_ff_in,
    w_ff_out,
    gain_ff,
    join_query,
    join_key,
    join_value,
    adapt_down,
    adapt_up,
    gain_out,
    output,
    grad_in,
    sums,
    gain_sums,
    rows,
    rows_ff,
    rows_qkv,
    rows_sib,
    cols,
    cols_sib,
    ring,
    banks,
    acc,
    acc_two,
    wide,
    acc_t,
    acc_t_two,
    active,
    bank_slope,
    second,
    norm_one,
    norm_two,
    slope,
    qkv_t,
    probs,
    low_tmp,
    low_tmp_two,
    stat,
    stat_one,
    stat_two,
    gain_col,
    part,
    recv_one,
    recv_two,
    recv_three,
    recv_four,
    gain_sum,
    gain_from,
    ring_sem,
    local_sem,
    bank_send,
    bank_recv,
    row_send,
    row_recv,
    col_send,
    col_recv,
    stage_send,
    stage_recv,
    last_send,
    last_recv,
    gain_send,
    gain_recv,
):
    low = jnp.bfloat16
    tokens, width = hidden.shape
    half_width = width // 2
    gain_attn, gain_ff, gain_out = [
        gain[...].reshape(1, width) for gain in (gain_attn, gain_ff, gain_out)
    ]
    blocks = rows.shape[1] * rows.shape[2] * rows.shape[3]
    ad = lax.axis_index("ad")
    bn = lax.axis_index("bn")
    x, z = ad % 2, ad // 2
    core, y = bn % 2, bn // 2
    sibling = (ad, flip(bn, 1))
    x_mate = (flip(ad, 1), bn)
    y_mate = (ad, flip(bn, 2))
    own = {"y": y, "x": x, "h": z // 2, "l": z % 2}
    mates = {"y": y_mate, "x": x_mate, "h": (flip(ad, 4), bn), "l": (flip(ad, 2), bn)}
    other_core = 1 - core

    loads = [(w_qkv.at[:, pl.ds(k * width, width)]) for k in range(3)] + [w_out]
    for k in range(4):
        loads.append(w_ff_in.at[:, pl.ds(k * width, width)])
        loads.append(w_ff_out.at[pl.ds(k * width, width), :])
    loads += [join_query, join_key, join_value]
    for k in range(4):
        loads.append(w_ff_out.at[pl.ds(k * width, width), :])
        loads.append(w_ff_in.at[:, pl.ds(k * width, width)])
    loads += [w_out] + [w_qkv.at[:, pl.ds(k * width, width)] for k in range(3)]
    free_slots = list(range(SLOTS))
    in_flight = []
    next_load = [0]

    def fill():
        while free_slots and next_load[0] < len(loads):
            slot = free_slots.pop(0)
            copy = pltpu.make_async_copy(loads[next_load[0]], ring.at[slot], ring_sem.at[slot])
            copy.start()
            in_flight.append((slot, copy))
            next_load[0] += 1

    def take():
        slot, copy = in_flight.pop(0)
        copy.wait()
        return slot

    def release(slot):
        free_slots.append(slot)
        fill()

    fill()
    bank_own = []
    for i, bank in enumerate((adapt_down, adapt_up)):
        bank_own.append(pltpu.make_async_copy(bank, banks.at[i, bn], local_sem.at[i]))
        bank_own[i].start()

    barrier = pltpu.get_barrier_semaphore()
    for mate in [sibling, *mates.values()]:
        pl.semaphore_signal(barrier, inc=1, device_id=mate, device_id_type=MESH)

    started = []

    def send(source, target, send_sem, recv_sem, mate):
        copy = pltpu.make_async_remote_copy(
            src_ref=source,
            dst_ref=target,
            send_sem=send_sem,
            recv_sem=recv_sem,
            device_id=mate,
            device_id_type=MESH,
        )
        copy.start()
        started.append(copy)
        return copy

    def row_views(index):
        if index < 8:
            return rows.at[index]
        if index < 12:
            return rows_ff.at[:, :, index - 8]
        return rows_qkv.at[:, :, index - 12]

    def row_half(index, side):
        if index < 8:
            piece = rows[index, :, side, core]
        elif index < 12:
            piece = rows_ff[:, side, index - 8, core]
        else:
            piece = rows_qkv[:, side, index - 12, core]
        return piece.reshape(4 * PIECE, tokens)

    def col_ref(index):
        return hidden if index == 0 else cols.at[index - 1]

    row_copies, col_copies = {}, {}
    arrived = set()

    def share_row(index):
        row_copies[index] = send(
            row_views(index).at[:, :, other_core],
            rows_sib.at[index],
            row_send.at[index],
            row_recv.at[index],
            sibling,
        )

    def share_col(index):
        col_copies[index] = send(
            col_ref(index),
            cols_sib.at[index],
            col_send.at[index],
            col_recv.at[index],
            sibling,
        )

    axes = ("y", "x", "h", "l")
    recvs = (recv_one, recv_two, recv_three, recv_four)
    copies, last = {}, {}
    units = len(UNITS)

    def half(unit, side):
        total = None
        for left, right in UNITS[unit]:
            if (0, left) not in arrived:
                row_copies[left].wait_recv()
                arrived.add((0, left))
            if (1, right) not in arrived:
                col_copies[right].wait_recv()
                arrived.add((1, right))
            term = matmul(row_half(left, side), col_ref(right)[...])
            term += matmul(
                rows_sib[left, :, side].reshape(4 * PIECE, tokens), cols_sib[right]
            )
            total = term if total is None else total + term
        total = total.astype(low).reshape(2, 2, PIECE, width)
        part[unit, 0, side] = total[..., :half_width]
        part[unit, 1, side] = total[..., half_width:]

    def place(done, axis, index):
        fixed = {name: own[name] for name in done}
        fixed[axis] = index
        left = [name for name in axes if name not in done]
        inside = tuple(index if name == axis else slice(None) for name in left)
        return tuple(fixed.get(name, slice(None)) for name in axes), inside

    def push(unit, stage):
        order = ORDERS[unit]
        axis = order[stage]
        where, _ = place(order[:stage], axis, 1 - own[axis])
        copies[unit, stage] = send(
            part.at[(unit, *where)],
            recvs[stage].at[unit],
            stage_send.at[stage, unit],
            stage_recv.at[stage, unit],
            mates[axis],
        )

    def start(unit):
        if ORDERS[unit][0] == "x":
            half(unit, 1 - x)
            push(unit, 0)
            half(unit, x)
        else:
            half(unit, 0)
            half(unit, 1)
            push(unit, 0)

    def add(unit, stage, axis, index):
        where, inside = place(ORDERS[unit][: stage + 1], axis, index)
        mine = part[(unit, *where)].astype(jnp.float32)
        part[(unit, *where)] = (mine + recvs[stage][(unit, *inside)].astype(jnp.float32)).astype(low)

    def advance(unit, stage):
        copies[unit, stage].wait_recv()
        axis = ORDERS[unit][stage + 1]
        add(unit, stage, axis, 1 - own[axis])
        push(unit, stage + 1)
        add(unit, stage, axis, own[axis])

    def close(unit):
        copies[unit, 3].wait_recv()
        total = part[(unit, *(own[name] for name in axes))].astype(jnp.float32)
        sums[unit, core] = (total + recv_four[unit].astype(jnp.float32)).astype(low)
        last[unit] = send(
            sums.at[unit, core],
            sums.at[unit, core],
            last_send.at[unit],
            last_recv.at[unit],
            sibling,
        )

    step_rows = tokens

    def over_rows(body, init=0):
        return body(slice(None), 0, init)

    def over_pieces(body, init=0):
        for p in range(blocks):
            init = body(p, init)
        return init

    def spot(p):
        return p // 4, (p // 2) % 2, p % 2

    def put_t(index, value):
        rows[index] = value.reshape(4, 2, 2, PIECE, tokens)

    def get_t(index):
        return rows[index].reshape(width, tokens)

    def fold(value):
        return value.reshape(PIECE // 8, 8, tokens).sum(0)

    length = lengths[0]
    for k in range(3):
        slot = take()
        value = matmul(hidden[...], ring[slot])
        release(slot)
        if k == 0:
            value = value * 0.125
        qkv_t[pl.ds(k * width, width), :] = value.astype(low).T
    pl.semaphore_wait(barrier, 1 + len(mates))
    bank_sib, bank_y, bank_far = [], [], []
    for i, bank in enumerate((adapt_down, adapt_up)):
        bank_y.append(
            send(bank, banks.at[i, bn], bank_send.at[i, 1], bank_recv.at[i, 1], y_mate)
        )
    for i, bank in enumerate((adapt_down, adapt_up)):
        bank_sib.append(
            send(bank, banks.at[i, bn], bank_send.at[i, 0], bank_recv.at[i, 0], sibling)
        )
    share_col(0)
    size = width // heads

    def head_rows(k, head):
        return pl.ds(pl.multiple_of(k * width + head * size, size), size)

    valid_keys = lax.broadcasted_iota(jnp.int32, (tokens, tokens), 0) < length

    def head_forward(head, carry):
        scores = matmul_tn(qkv_t[head_rows(1, head), :], qkv_t[head_rows(0, head), :])
        scores = jnp.where(valid_keys, scores, masked_value)
        scores = jnp.exp(scores - jnp.max(scores, 0, keepdims=True))
        share = (scores * (1.0 / jnp.sum(scores, 0, keepdims=True))).astype(low)
        probs[head] = share
        context = matmul(qkv_t[head_rows(2, head), :], share)
        low_tmp_two[pl.ds(pl.multiple_of(head * size, size), size), :] = context.astype(low)
        return carry

    lax.fori_loop(0, heads, head_forward, 0, unroll=3)
    cols[0] = low_tmp_two[...].T
    share_col(1)
    slot = take()
    acc[...] = matmul(cols[0], ring[slot])
    release(slot)

    def norm_rows(total):
        center = total - jnp.mean(total, -1, keepdims=True)
        rstd = lax.rsqrt(jnp.mean(center * center, -1, keepdims=True) + epsilon)
        return center * rstd, rstd

    def norm_first(r, i, carry):
        normed, rstd = norm_rows(hidden[r, :].astype(jnp.float32) + acc[r, :])
        stat[r, :] = jnp.broadcast_to(rstd, (step_rows, 128))
        low_tmp[r, :] = normed.astype(low)
        one_rows = normed * gain_attn
        wide[r, :] = one_rows
        cols[1, r, :] = one_rows.astype(low)
        return carry

    over_rows(norm_first)
    share_col(2)
    norm_one[...] = low_tmp[...].T.reshape(blocks, PIECE, tokens)
    stat_one[...] = stat[...].T[:8]

    for k in range(4):
        slot = take()
        acc[...] = matmul(cols[1], ring[slot])
        release(slot)
        unit_base = 2 + (k % 2) * 2
        lanes = pl.ds((k // 2) * half_width, half_width)

        def gelu_rows(r, i, carry):
            before = acc[r, :]
            cdf, density = normal_parts(before)
            act = (before * cdf).astype(low)
            low_tmp[r, :] = act
            cols[unit_base, r, lanes] = act[:, :half_width]
            cols[unit_base + 1, r, lanes] = act[:, half_width:]
            cols[9, r, :] = (cdf + before * density).astype(low)
            return carry

        over_rows(gelu_rows)
        slope[pl.ds(k * blocks, blocks)] = cols[9].T.reshape(blocks, PIECE, tokens)
        slot = take()
        value = matmul(low_tmp[...], ring[slot])
        release(slot)
        acc_two[...] = value if k == 0 else acc_two[...] + value
        if k == 1:
            for i in range(2):
                bank_y[i].wait_recv()
                far = flip(bn, 2)
                bank_far.append(
                    send(
                        banks.at[i, far],
                        banks.at[i, far],
                        bank_send.at[i, 2],
                        bank_recv.at[i, 2],
                        sibling,
                    )
                )
    for index in range(3, 7):
        share_col(index)

    def norm_second(r, i, carry):
        normed, rstd = norm_rows(wide[r, :] + acc_two[r, :])
        stat[r, :] = jnp.broadcast_to(rstd, (step_rows, 128))
        low_tmp[r, :] = normed.astype(low)
        two_rows = normed * gain_ff
        wide[r, :] = two_rows
        cols[6, r, :] = two_rows.astype(low)
        return carry

    over_rows(norm_second)
    share_col(7)
    norm_two[...] = low_tmp[...].T.reshape(blocks, PIECE, tokens)
    stat_two[...] = stat[...].T[:8]
    put_t(3, cols[6].T)
    share_row(3)

    slot_query = take()
    low_tmp[...] = matmul(cols[6], ring[slot_query]).astype(low)
    put_t(4, low_tmp[...].T)
    share_row(4)
    slot_key = take()
    put_t(2, matmul(ring[slot_key], get_t(4)).astype(low))
    share_row(2)

    for i in range(2):
        bank_own[i].wait()
        bank_sib[i].wait_recv()
        bank_far[i].wait_recv()
    acc_t[...] = matmul(banks[0].reshape(width, width), get_t(3)).reshape(blocks, PIECE, tokens)
    acc_t_two[...] = matmul(banks[1].reshape(width, width), get_t(2)).reshape(
        blocks, PIECE, tokens
    )
    score_scale = 1.0 / math.sqrt(width)
    groups = PIECE // adapters

    def grouped(value):
        return value.reshape(groups, adapters, tokens)

    def adapter_rows(p, logits):
        inner = acc_t[p]
        cdf, density = normal_parts(inner)
        act = inner * cdf
        active[p] = act
        bank_slope[p] = (cdf + inner * density).astype(low)
        return logits + grouped(act * acc_t_two[p]).sum(0)

    logits = over_pieces(adapter_rows, jnp.zeros((adapters, tokens), jnp.float32)) * score_scale
    logits = jnp.exp(logits - jnp.max(logits, 0, keepdims=True))
    shares = logits / jnp.sum(logits, 0, keepdims=True)

    def spread(value):
        return jnp.concatenate([value] * groups, 0)

    wide_shares = spread(shares)

    def mixing_rows(p, carry):
        low_tmp_two[pl.ds(p * PIECE, PIECE), :] = (
            wide_shares * active[p]
        ).astype(low)
        return carry

    over_pieces(mixing_rows)
    cols[8] = low_tmp_two[...].T
    share_col(9)
    acc[...] = matmul(cols[8], banks[1].reshape(width, width))

    def joined_rows(r, i, carry):
        cols[7, r, :] = (wide[r, :] + acc[r, :]).astype(low)
        return carry

    over_rows(joined_rows)
    share_col(8)
    slot_value = take()
    acc[...] = matmul(cols[7], ring[slot_value])

    def norm_third(r, i, gain_part):
        normed, rstd = norm_rows(wide[r, :] + acc[r, :])
        gain = gain_out
        acc_two[r, :] = normed * gain
        token = lax.broadcasted_iota(jnp.int32, (step_rows, 1), 0) + i * step_rows
        upstream = jnp.where(token < length, cotangent[r, :].astype(jnp.float32), 0.0)
        product = upstream * normed
        gained = upstream * gain
        third = rstd * (
            gained
            - jnp.mean(gained, -1, keepdims=True)
            - normed * jnp.mean(gained * normed, -1, keepdims=True)
        )
        low_tmp[r, :] = third.astype(low)
        return gain_part + product.reshape(step_rows // 8, 8, width).sum(0)

    gain_part = over_rows(norm_third, jnp.zeros((8, width), jnp.float32))
    out_copy = pltpu.make_async_copy(acc_two, output, local_sem.at[2])
    out_copy.start()
    gain_sum[0] = jnp.broadcast_to(jnp.sum(gain_part, 0, keepdims=True), (8, width))
    put_t(0, low_tmp[...].T)
    share_row(0)

    state = {}

    def value_back():
        second[...] = matmul(ring[slot_value], get_t(0)).reshape(blocks, PIECE, tokens)
        release(slot_value)

        def mix_rows(p, carry):
            zz, xx, cc = spot(p)
            rows[1, zz, xx, cc] = second[p].astype(low)
            return carry

        over_pieces(mix_rows)
        share_row(1)
        acc_t[...] = matmul(banks[1].reshape(width, width), get_t(1)).reshape(blocks, PIECE, tokens)

    def adapter_grads():
        def share_rows(p, total):
            return total + grouped(acc_t[p] * active[p]).sum(0)

        share_grad = over_pieces(share_rows, jnp.zeros((adapters, tokens), jnp.float32))
        logit_grad = shares * (share_grad - jnp.sum(shares * share_grad, 0, keepdims=True))
        wide_logit = spread(logit_grad * score_scale)

        def adapter_back(p, carry):
            act_grad = acc_t[p] * wide_shares + wide_logit * acc_t_two[p]
            where = pl.ds(p * PIECE, PIECE)
            low_tmp_two[where, :] = (wide_logit * active[p]).astype(low)
            bank_slope[p] = (bank_slope[p].astype(jnp.float32) * act_grad).astype(low)
            return carry

        over_pieces(adapter_back)
        cols[9] = low_tmp_two[...].T
        share_col(10)
        cols[10] = bank_slope[...].reshape(width, tokens).T
        share_col(11)

    def probe_back():
        cols[11] = matmul(cols[9], banks[1].reshape(width, width)).astype(low)
        share_col(12)
        low_tmp[...] = matmul(cols[11], ring[slot_key]).astype(low)
        release(slot_key)
        put_t(5, low_tmp[...].T)
        share_row(5)
        low_tmp[...] = matmul(cols[10], banks[0].reshape(width, width)).astype(low)
        low_tmp_two[...] = low_tmp[...].T
        acc_t[...] = matmul(ring[slot_query], get_t(5)).reshape(blocks, PIECE, tokens)
        release(slot_query)

    def norm_back(index, gain, normed_ref, stat_ref, upstream_of, factor):
        gain_col[...] = jnp.broadcast_to(gain, (128, width)).T.reshape(blocks, PIECE, 128)

        def gained(p):
            column = gain_col[p]
            return acc_t[p] * jnp.concatenate([column] * (tokens // 128), 1)

        def first_pass(p, carry):
            upstream = upstream_of(p)
            acc_t[p] = upstream
            normed = normed_ref[p].astype(jnp.float32)
            gain_of = jnp.sum(upstream * normed, -1, keepdims=True)
            weighted = gained(p)
            gain_col[p] = jnp.broadcast_to(gain_of, (PIECE, 128))
            acc_t[p] = weighted
            return carry[0] + fold(weighted), carry[1] + fold(weighted * normed)

        zeros = jnp.zeros((8, tokens), jnp.float32)
        plain, tilted = over_pieces(first_pass, (zeros, zeros))
        mean_plain = jnp.sum(plain, 0, keepdims=True) * (1.0 / width)
        mean_tilted = jnp.sum(tilted, 0, keepdims=True) * (1.0 / width)
        rstd = stat_ref[0:1, :]

        def second_pass(p, carry):
            value = rstd * (acc_t[p] - mean_plain - normed_ref[p].astype(jnp.float32) * mean_tilted)
            second[p] = value
            zz, xx, cc = spot(p)
            rows[factor, zz, xx, cc] = value.astype(low)
            return carry

        over_pieces(second_pass)
        gain_sum[0, index : index + 1, :] = gain_col[...].reshape(width, 128).T[:1]

    def upstream_two(p):
        zz, xx, cc = spot(p)
        where = pl.ds(p * PIECE, PIECE)
        total = rows[0, zz, xx, cc].astype(jnp.float32) + second[p]
        return total + low_tmp_two[where, :].astype(jnp.float32) + acc_t[p]

    def norm_two_back():
        norm_back(1, gain_ff, norm_two, stat_two, upstream_two, 6)
        share_row(6)

    def ff_back(k):
        slot = take()
        acc_t_two[...] = matmul(ring[slot], get_t(6)).reshape(blocks, PIECE, tokens)
        release(slot)

        def slope_rows(p, carry):
            value = acc_t_two[p] * slope[k * blocks + p].astype(jnp.float32)
            rows_ff[k, p // 8, (p % 8) // 2, p % 2] = value.astype(low)
            return carry

        over_pieces(slope_rows)
        slot = take()
        value = matmul(ring[slot], rows_ff[k].reshape(width, tokens))
        value = value.reshape(blocks, PIECE, tokens)
        release(slot)
        acc_t[...] = value if k == 0 else acc_t[...] + value
        if k == 3:
            for index in range(8, 12):
                share_row(index)

    def upstream_one(p):
        return second[p] + acc_t[p]

    def norm_one_back():
        norm_back(0, gain_attn, norm_one, stat_one, upstream_one, 7)
        share_row(7)
        slot = take()
        low_tmp_two[...] = matmul(ring[slot], get_t(7)).astype(low)
        release(slot)

    heads_step = 3
    step_pieces = heads_step * size // PIECE

    def head_backward(group, carry):
        grads = [[], [], []]
        for i in range(heads_step):
            head = group * heads_step + i
            query, key, value = [qkv_t[head_rows(k, head), :] for k in range(3)]
            upstream = low_tmp_two[pl.ds(pl.multiple_of(head * size, size), size), :]
            share = probs[head]
            share_wide = share.astype(jnp.float32)
            prob_grad = matmul_tn(value, upstream)
            delta = jnp.sum(share_wide * prob_grad, 0, keepdims=True)
            score_grad = (share_wide * (prob_grad - delta)).astype(low)
            grads[0].append((matmul(key, score_grad) * 0.125).astype(low))
            grads[1].append(matmul_t(query, score_grad).astype(low))
            grads[2].append(matmul_t(upstream, share).astype(low))
        for k in range(3):
            stacked = jnp.concatenate(grads[k], 0).reshape(step_pieces, PIECE, tokens)
            for i in range(step_pieces):
                p = k * blocks + group * step_pieces + i
                rows_qkv[p // 12, (p // 6) % 2, (p % 6) // 2, p % 2] = stacked[i]
        return carry

    def attention_back():
        lax.fori_loop(0, heads // heads_step, head_backward, 0)
        for index in range(12, 15):
            share_row(index)

    def input_back():
        for k in range(3):
            slot = take()
            block = rows_qkv[...].reshape(3 * blocks, PIECE, tokens)[k * blocks : (k + 1) * blocks]
            value = matmul(ring[slot], block.reshape(width, tokens)).reshape(blocks, PIECE, tokens)
            release(slot)
            second[...] = second[...] + value
        acc[...] = second[...].reshape(width, tokens).T
        state["in"] = pltpu.make_async_copy(acc, grad_in, local_sem.at[3])
        state["in"].start()

    gain_mates = (sibling, x_mate, y_mate, mates["l"], mates["h"])

    def gain_step(stage):
        if stage > 0:
            state["gain"].wait_recv()
            total = gain_sum[stage - 1] + gain_from[stage - 1]
            if stage == 5:
                gain_sums[...] = total
                return
            gain_sum[stage] = total
        state["gain"] = send(
            gain_sum.at[stage],
            gain_from.at[stage],
            gain_send.at[stage],
            gain_recv.at[stage],
            gain_mates[stage],
        )

    chain = [value_back, adapter_grads, probe_back, norm_two_back]
    chain += [functools.partial(ff_back, k) for k in range(4)]
    chain += [norm_one_back, attention_back, input_back]
    progress = [0] * units
    since_chain, gain_stage = 0, 0
    for action in SEQUENCE:
        if action < 0:
            chain.pop(0)()
        elif progress[action] == 0:
            start(action)
        elif progress[action] < 4:
            advance(action, progress[action] - 1)
        else:
            close(action)
        if action >= 0:
            progress[action] += 1
        if not chain:
            if since_chain % 4 == 0 and gain_stage < 6:
                gain_step(gain_stage)
                gain_stage += 1
            since_chain += 1
    for stage in range(gain_stage, 6):
        gain_step(stage)
    for unit in range(units):
        last[unit].wait_recv()
    for copy in started:
        copy.wait_send()
    out_copy.wait()
    state["in"].wait()


def run_layer(heads, adapters, arrays):
    hidden = arrays[0]
    tokens, width = hidden.shape
    low, wide = jnp.bfloat16, jnp.float32
    blocks = width // PIECE
    units = len(UNITS)
    dma = pltpu.SemaphoreType.DMA
    vmem = pl.BlockSpec(memory_space=pltpu.VMEM)
    smem = pl.BlockSpec(memory_space=pltpu.SMEM)
    far = pl.BlockSpec(memory_space=pl.ANY)
    half_width = width // 2
    pair = lambda shape: [dma(shape), dma(shape)]
    return pl.pallas_call(
        functools.partial(layer_kernel, heads, adapters),
        out_shape=(
            jax.ShapeDtypeStruct((tokens, width), wide),
            jax.ShapeDtypeStruct((tokens, width), wide),
            jax.ShapeDtypeStruct((units, 2, PIECE, half_width), low),
            jax.ShapeDtypeStruct((8, width), wide),
        ),
        in_specs=[
            vmem, smem, vmem, far, far, vmem, far, far, vmem, far, far, far, far, far, vmem,
        ],
        out_specs=[far, far, vmem, vmem],
        scratch_shapes=[
            pltpu.VMEM((8, 4, 2, 2, PIECE, tokens), low),
            pltpu.VMEM((4, 2, 4, 2, PIECE, tokens), low),
            pltpu.VMEM((4, 2, 3, 2, PIECE, tokens), low),
            pltpu.VMEM((15, 4, 2, PIECE, tokens), low),
            pltpu.VMEM((12, tokens, width), low),
            pltpu.VMEM((13, tokens, width), low),
            pltpu.VMEM((SLOTS, width, width), low),
            pltpu.VMEM((2, 4, width // 4, width), low),
            pltpu.VMEM((tokens, width), wide),
            pltpu.VMEM((tokens, width), wide),
            pltpu.VMEM((tokens, width), wide),
            pltpu.VMEM((blocks, PIECE, tokens), wide),
            pltpu.VMEM((blocks, PIECE, tokens), wide),
            pltpu.VMEM((blocks, PIECE, tokens), wide),
            pltpu.VMEM((blocks, PIECE, tokens), low),
            pltpu.VMEM((blocks, PIECE, tokens), wide),
            pltpu.VMEM((blocks, PIECE, tokens), low),
            pltpu.VMEM((blocks, PIECE, tokens), low),
            pltpu.VMEM((4 * blocks, PIECE, tokens), low),
            pltpu.VMEM((3 * width, tokens), low),
            pltpu.VMEM((heads, tokens, tokens), low),
            pltpu.VMEM((tokens, width), low),
            pltpu.VMEM((width, tokens), low),
            pltpu.VMEM((tokens, 128), wide),
            pltpu.VMEM((8, tokens), wide),
            pltpu.VMEM((8, tokens), wide),
            pltpu.VMEM((blocks, PIECE, 128), wide),
            pltpu.VMEM((units, 2, 2, 2, 2, PIECE, half_width), low),
            pltpu.VMEM((units, 2, 2, 2, PIECE, half_width), low),
            pltpu.VMEM((units, 2, 2, PIECE, half_width), low),
            pltpu.VMEM((units, 2, PIECE, half_width), low),
            pltpu.VMEM((units, PIECE, half_width), low),
            pltpu.VMEM((5, 8, width), wide),
            pltpu.VMEM((5, 8, width), wide),
            dma((SLOTS,)),
            dma((4,)),
        ]
        + pair((2, 3))
        + pair((15,))
        + pair((13,))
        + pair((4, units))
        + pair((units,))
        + pair((5,)),
        compiler_params=pltpu.CompilerParams(
            collective_id=0, has_side_effects=True, vmem_limit_bytes=63 * 2**20
        ),
    )(*arrays)


def finish_kernel(
    sums,
    gain_sums,
    output,
    grad_in,
    out_output,
    out_grad_in,
    out_qkv,
    out_proj,
    out_gain_attn,
    out_ff_in,
    out_ff_out,
    out_gain_ff,
    out_query,
    out_key,
    out_value,
    out_down,
    out_up,
    out_gain_out,
    turned,
    copy_sem,
):
    passed = [
        pltpu.make_async_copy(output, out_output, copy_sem.at[0]),
        pltpu.make_async_copy(grad_in, out_grad_in, copy_sem.at[1]),
    ]
    for copy in passed:
        copy.start()
    ad = lax.axis_index("ad")
    core = lax.axis_index("bn") % 2
    width = sums.shape[3]
    own = pl.ds(pl.multiple_of(core * (width // 2), width // 2), width // 2)

    def columns(out, slot, first, count):
        value = sums[first : first + count].reshape(count * 2 * PIECE, width)
        extent = pl.ds(0, count * 2 * PIECE)
        turned[slot, :, extent] = value.astype(jnp.float32).T
        out[...] = turned[slot, own, extent]

    columns(out_value, 0, 0, 1)
    columns(out_up, 1, 1, 1)
    columns(out_down, 2, 2, 1)
    columns(out_key, 0, 3, 1)
    columns(out_query, 1, 4, 1)
    columns(out_ff_in, 2, 9, 4)
    columns(out_proj, 0, 13, 1)
    columns(out_qkv, 1, 14, 3)
    for i in range(2):
        value = sums[5 + 2 * core + i].reshape(2 * PIECE, width)
        out_ff_out[:, pl.ds(i * width, width)] = value.astype(jnp.float32)
    total = gain_sums.shape[1]
    piece = out_gain_attn.shape[0]
    rolled = pltpu.roll(gain_sums[...], lax.rem(total - ad * piece, total), 1)[:, :piece]
    for index, out in enumerate((out_gain_attn, out_gain_ff, out_gain_out)):
        out[...] = rolled[index : index + 1].reshape(piece)
    for copy in passed:
        copy.wait()


def finish(sums, gain_sums, output, grad_in, width):
    quarter, eighth = width // 4, width // 8
    far = pl.BlockSpec(memory_space=pl.ANY)
    shapes = [
        output.shape,
        grad_in.shape,
        (quarter, 3 * eighth),
        (quarter, eighth),
        (eighth,),
        (quarter, 4 * eighth),
        (eighth, 4 * quarter),
        (eighth,),
    ]
    shapes += [(quarter, eighth)] * 5 + [(eighth,)]
    return pl.pallas_call(
        finish_kernel,
        out_shape=tuple(jax.ShapeDtypeStruct(shape, jnp.float32) for shape in shapes),
        in_specs=[pl.BlockSpec(memory_space=pltpu.VMEM)] * 2 + [far] * 2,
        out_specs=[far] * 2 + [pl.BlockSpec(memory_space=pltpu.VMEM)] * 12,
        scratch_shapes=[
            pltpu.VMEM((3, width // 2, 4 * eighth), jnp.float32),
            pltpu.SemaphoreType.DMA((2,)),
        ],
        compiler_params=pltpu.CompilerParams(vmem_limit_bytes=32 * 2**20),
    )(sums, gain_sums, output, grad_in)


def fast_local(*arrays):
    arrays = list(arrays)
    width = arrays[0].shape[1]
    adapters = arrays[12].shape[1]
    bank_shape = arrays[12].shape[:2] + (-1,)
    for i in (12, 13):
        arrays[i] = arrays[i].reshape(-1, width)
    output, grad_in, sums, gain_sums = run_layer(H, adapters, arrays)
    results = list(finish(sums, gain_sums, output, grad_in, width))
    results[6] = results[6].T
    for i in (11, 12):
        results[i] = results[i].reshape(bank_shape)
    return tuple(results)


def local(
    hidden_in,
    lengths,
    cotangent,
    w_qkv,
    w_out,
    gain_attn,
    w_ff_in,
    w_ff_out,
    gain_ff,
    join_query,
    join_key,
    join_value,
    adapt_down,
    adapt_up,
    gain_out,
):
    seq_count = lengths.shape[0]
    tok_rows, model_width = hidden_in.shape
    slot_len = tok_rows // seq_count
    head_count = H
    head_size = model_width // head_count
    score_scale = 1.0 / math.sqrt(head_size)
    adapters = adapt_down.shape[1]
    down_flat = lax.all_gather(adapt_down.reshape(-1, model_width), "bn", axis=0, tiled=True)
    up_flat = lax.all_gather(adapt_up.reshape(-1, model_width), "bn", axis=0, tiled=True)
    valid = lax.broadcasted_iota(jnp.int32, (seq_count, slot_len), 1) < lengths[:, None]
    row_ok = valid.reshape(tok_rows, 1).astype(jnp.float32)
    tokens_wide = hidden_in.astype(jnp.float32)
    qkv = matmul(hidden_in, w_qkv).astype(jnp.bfloat16)
    queries = qkv[:, :model_width].reshape(seq_count, slot_len, head_count, head_size)
    key_rows = qkv[:, model_width : 2 * model_width].reshape(
        seq_count, slot_len, head_count, head_size
    )
    values = qkv[:, 2 * model_width :].reshape(seq_count, slot_len, head_count, head_size)

    def attend_scores():
        raw_scores = (
            jnp.einsum("sqhe,skhe->shqk", queries, key_rows, preferred_element_type=jnp.float32)
            * score_scale
        )
        return jnp.where(valid[:, None, None, :], raw_scores, masked_value)

    scores = attend_scores()
    row_max = jnp.max(scores, -1, keepdims=True)
    log_total = row_max + jnp.log(jnp.sum(jnp.exp(scores - row_max), -1, keepdims=True))
    probs = jnp.exp(scores - log_total).astype(jnp.bfloat16)
    context = (
        jnp.einsum("shqk,skhe->sqhe", probs, values, preferred_element_type=jnp.float32)
        .reshape(tok_rows, model_width)
        .astype(jnp.bfloat16)
    )
    attn_out = matmul(context, w_out)
    hidden_one, norm_one_back = jax.vjp(layer_norm, tokens_wide + attn_out, gain_attn)
    hidden_one_low = hidden_one.astype(jnp.bfloat16)
    ff_pre = matmul(hidden_one_low, w_ff_in)
    ff_act, gelu_ff_back = jax.vjp(gelu_exact, ff_pre)
    ff_low = ff_act.astype(jnp.bfloat16)
    ff_out = matmul(ff_low, w_ff_out)
    hidden_two, norm_two_back = jax.vjp(layer_norm, hidden_one + ff_out, gain_ff)
    hidden_low = hidden_two.astype(jnp.bfloat16)
    query_join = matmul(hidden_low, join_query).astype(jnp.bfloat16)
    probe = matmul_t(query_join, join_key).astype(jnp.bfloat16)
    mixing, kept_state = adapter_forward(hidden_low, probe, down_flat, up_flat, adapters)
    joined_in = (hidden_two + matmul(mixing, up_flat)).astype(jnp.bfloat16)
    joined = matmul(joined_in, join_value)
    output, norm_out_back = jax.vjp(layer_norm, hidden_two + joined, gain_out)
    out_grad = cotangent.astype(jnp.float32) * row_ok
    sum_three, gain_out_grad = norm_out_back(out_grad)
    joined_grad = sum_three.astype(jnp.bfloat16)
    into_joined = matmul_t(joined_grad, join_value)
    mix_grad = into_joined.astype(jnp.bfloat16)
    inner_grad, weigh_grad = adapter_backward(kept_state, up_flat, mix_grad, adapters)
    hidden_back = matmul(inner_grad, down_flat)
    probe_grad = matmul(weigh_grad, up_flat).astype(jnp.bfloat16)
    query_in = matmul(probe_grad, join_key).astype(jnp.bfloat16)
    grad_two = sum_three + into_joined + hidden_back + matmul_t(query_in, join_query)
    sum_two, gain_ff_grad = norm_two_back(grad_two)
    ff_out_grad = sum_two.astype(jnp.bfloat16)
    ff_pre_grad = gelu_ff_back(matmul_t(ff_out_grad, w_ff_out))[0].astype(jnp.bfloat16)
    grad_one = sum_two + matmul_t(ff_pre_grad, w_ff_in)
    sum_one, gain_attn_grad = norm_one_back(grad_one)
    attn_grad = sum_one.astype(jnp.bfloat16)
    context_grad = (
        matmul_t(attn_grad, w_out)
        .astype(jnp.bfloat16)
        .reshape(seq_count, slot_len, head_count, head_size)
    )
    probs_wide = jnp.exp(attend_scores() - log_total)
    prob_grad = jnp.einsum(
        "sqhe,skhe->shqk", context_grad, values, preferred_element_type=jnp.float32
    )
    row_delta = jnp.sum(probs_wide * prob_grad, -1, keepdims=True)
    score_grad = (probs_wide * (prob_grad - row_delta)).astype(jnp.bfloat16)
    query_back = (
        jnp.einsum("shqk,skhe->sqhe", score_grad, key_rows, preferred_element_type=jnp.float32)
        * score_scale
    )
    key_back = (
        jnp.einsum("shqk,sqhe->skhe", score_grad, queries, preferred_element_type=jnp.float32)
        * score_scale
    )
    value_back = jnp.einsum(
        "shqk,sqhe->skhe", probs, context_grad, preferred_element_type=jnp.float32
    )
    qkv_grad = jnp.concatenate(
        [
            query_back.reshape(tok_rows, model_width),
            key_back.reshape(tok_rows, model_width),
            value_back.reshape(tok_rows, model_width),
        ],
        1,
    ).astype(jnp.bfloat16)
    grad_in = sum_one + matmul_t(qkv_grad, w_qkv)
    def shared_sum(gradient):
        columns = lax.psum_scatter(gradient, "ad", scatter_dimension=1, tiled=True)
        return lax.psum_scatter(
            columns.astype(jnp.bfloat16), "bn", scatter_dimension=0, tiled=True
        ).astype(jnp.float32)

    gains = lax.psum(
        lax.psum_scatter(
            jnp.stack([gain_attn_grad, gain_ff_grad, gain_out_grad]),
            "ad",
            scatter_dimension=1,
            tiled=True,
        ),
        "bn",
    )
    down_grad = shared_sum(matmul_tn(inner_grad, hidden_low))
    up_grad = shared_sum(matmul_tn(mixing, mix_grad) + matmul_tn(weigh_grad, probe))
    bank = adapt_down.shape[:2] + (-1,)
    return (
        output,
        grad_in,
        shared_sum(matmul_tn(hidden_in, qkv_grad)),
        shared_sum(matmul_tn(context, attn_grad)),
        gains[0],
        shared_sum(matmul_tn(hidden_one_low, ff_pre_grad)),
        shared_sum(matmul_tn(ff_low, ff_out_grad)),
        gains[1],
        shared_sum(matmul_tn(hidden_low, query_in)),
        shared_sum(matmul_tn(probe_grad, query_join)),
        shared_sum(matmul_tn(joined_in, joined_grad)),
        down_grad.reshape(bank),
        up_grad.reshape(bank),
        gains[2],
    )


def solution(mesh):
    placed = (
        P(("ad", "bn"), None),
        P(("ad", "bn")),
        P(("ad", "bn"), None),
        P(),
        P(),
        P(),
        P(),
        P(),
        P(),
        P(),
        P(),
        P(),
        P("bn", None, None),
        P("bn", None, None),
        P(),
    )
    sizes = (mesh.shape["ad"], mesh.shape["bn"])
    return jax.shard_map(
        fast_local if sizes == (8, 4) else local,
        mesh=mesh,
        in_specs=placed,
        out_specs=(
            P(("ad", "bn"), None),
            P(("ad", "bn"), None),
            P("bn", "ad"),
            P("bn", "ad"),
            P("ad"),
            P("bn", "ad"),
            P("bn", "ad"),
            P("ad"),
            P("bn", "ad"),
            P("bn", "ad"),
            P("bn", "ad"),
            P("bn", None, "ad"),
            P("bn", None, "ad"),
            P("ad"),
        ),
        check_vma=False,
    )
```

```python
import functools
import math

import jax
import jax.numpy as jnp
from jax import lax
from jax.experimental import pallas as pl
from jax.experimental.pallas import tpu as pltpu
from jax.sharding import PartitionSpec as P

H = 12


epsilon = 1e-06
masked_value = -1000000000.0
MESH = pl.DeviceIdType.MESH


def layer_norm(values, gain):
    center = values - jnp.mean(values, -1, keepdims=True)
    spread = jnp.mean(center * center, -1, keepdims=True)
    return center * lax.rsqrt(spread + epsilon) * gain


def gelu_exact(values):
    return jax.nn.gelu(values, approximate=False)


def matmul(left, right):
    return jnp.dot(left, right, preferred_element_type=jnp.float32)


def matmul_t(left, right):
    return lax.dot_general(
        left, right, (((1,), (1,)), ((), ())), preferred_element_type=jnp.float32
    )


def matmul_tn(left, right):
    return lax.dot_general(
        left, right, (((0,), (0,)), ((), ())), preferred_element_type=jnp.float32
    )


def adapter_forward(hidden, probe_rows, down_flat, up_flat, adapters):
    row_count, model_width = hidden.shape
    inner_pre = matmul_t(hidden, down_flat)
    active = gelu_exact(inner_pre)
    weigh_rows = matmul_t(probe_rows, up_flat)
    logits = jnp.sum((active * weigh_rows).reshape(row_count, -1, adapters), 1) / math.sqrt(
        model_width
    )
    shares = jax.nn.softmax(logits, -1)
    mixing = (
        (shares[:, None, :] * active.reshape(row_count, -1, adapters))
        .reshape(row_count, -1)
        .astype(jnp.bfloat16)
    )
    return (mixing, (inner_pre, active, weigh_rows, shares))


def adapter_backward(kept_state, up_flat, mix_grad, adapters):
    inner_pre, active, weigh_rows, shares = kept_state
    row_count, model_width = mix_grad.shape
    score_scale = 1.0 / math.sqrt(model_width)
    mix_in = matmul_t(mix_grad, up_flat).reshape(row_count, -1, adapters)
    active_three = active.reshape(row_count, -1, adapters)
    weigh_three = weigh_rows.reshape(row_count, -1, adapters)
    share_grad = jnp.sum(mix_in * active_three, 1)
    logit_grad = shares * (share_grad - jnp.sum(shares * share_grad, -1, keepdims=True))
    act_grad = mix_in * shares[:, None, :] + logit_grad[:, None, :] * score_scale * weigh_three
    weigh_grad = (
        (logit_grad[:, None, :] * score_scale * active_three)
        .reshape(row_count, -1)
        .astype(jnp.bfloat16)
    )
    unused, gelu_back = jax.vjp(gelu_exact, inner_pre)
    inner_grad = gelu_back(act_grad.reshape(row_count, -1))[0].astype(jnp.bfloat16)
    return (inner_grad, weigh_grad)


PIECE = 48
SLOTS = 5
SENDS = 48
UNITS = (
    ((0, 8),),
    ((1, 9), (2, 10)),
    ((3, 11),),
    ((4, 12),),
    ((5, 7),),
    ((6, 3),),
    ((6, 4),),
    ((6, 5),),
    ((6, 6),),
    ((8, 2),),
    ((9, 2),),
    ((10, 2),),
    ((11, 2),),
    ((7, 1),),
    ((12, 0),),
    ((13, 0),),
    ((14, 0),),
)


CROSS_X = (9, 10, 11, 12, 14, 15, 16)
CROSS_Y = (5, 6, 7, 8)
WHOLE = tuple(unit for unit in range(len(UNITS)) if unit not in CROSS_X + CROSS_Y)
ORDERS = (
    ("x", "y", "l", "h"),
    ("l", "y", "x", "h"),
    ("l", "h", "x", "y"),
    ("y", "l", "x", "h"),
    ("x", "y", "l", "h"),
    ("y", "l", "h", "x"),
    ("y", "x", "l", "h"),
    ("y", "l", "h", "x"),
    ("y", "l", "x", "h"),
    ("x", "l", "h", "y"),
    ("x", "y", "l", "h"),
    ("x", "y", "l", "h"),
    ("x", "y", "l", "h"),
    ("y", "x", "l", "h"),
    ("x", "y", "l", "h"),
    ("x", "y", "l", "h"),
    ("x", "y", "l", "h"),
)
SEQUENCE = (
    -1, -1, 0, -1, 2, -1, 1, 3, 4, -1, -1, 8, 6, 7, 5, -1, -1, -1, 2, 9, 10, -1, 4, 3,
    12, -1, 0, 14, 9, 13, 8, 7, 16, 5, 10, 15, 4, 9, 12, 0, 11, 7, 14, 5, 16, 8, 4, 10,
    2, 9, 3, 0, 15, 12, 6, 1, 4, 14, 7, 5, 10, 8, 13, 0, 11, 16, 12, 9, 3, 14, 2, 10,
    15, 8, 6, 16, 7, 12, 5, 1, 3, 14, 15, 13, 11, 6, 2, 1, 16, 15, 13, 11, 6, 1, 13, 11,
)

def flip(index, bit):
    return index + bit - 2 * bit * ((index // bit) % 2)


def normal_parts(values):
    cdf = 0.5 * (1.0 + lax.erf(values * (1.0 / math.sqrt(2.0))))
    density = jnp.exp(values * values * -0.5) * (1.0 / math.sqrt(2.0 * math.pi))
    return cdf, density


def layer_kernel(
    heads,
    adapters,
    hidden,
    lengths,
    cotangent_far,
    w_qkv,
    w_out,
    gain_attn,
    w_ff_in,
    w_ff_out,
    gain_ff,
    join_query,
    join_key,
    join_value,
    adapt_down,
    adapt_up,
    gain_out,
    output,
    grad_in,
    sums,
    gain_sums,
    rows,
    rows_ff,
    rows_qkv,
    rows_sib,
    cols,
    cols_sib,
    rows_x,
    cols_x,
    rows_y,
    cols_y,
    ring,
    banks,
    acc,
    acc_two,
    wide,
    acc_t,
    acc_t_two,
    active,
    bank_slope,
    second,
    norm_one,
    norm_two,
    slope,
    qkv_t,
    probs,
    low_tmp,
    low_tmp_two,
    stat,
    stat_one,
    stat_two,
    gain_col,
    cotangent,
    part,
    recv_one,
    recv_two,
    recv_three,
    recv_four,
    gain_sum,
    gain_from,
    ring_sem,
    local_sem,
    send_sem,
    bank_recv,
    row_recv,
    col_recv,
    row_x_recv,
    col_x_recv,
    row_y_recv,
    col_y_recv,
    stage_recv,
    last_recv,
    gain_recv,
):
    low = jnp.bfloat16
    tokens, width = hidden.shape
    half_width = width // 2
    gain_attn, gain_ff, gain_out = [
        gain[...].reshape(1, width) for gain in (gain_attn, gain_ff, gain_out)
    ]
    blocks = rows.shape[1] * rows.shape[2] * rows.shape[3]
    ad = lax.axis_index("ad")
    bn = lax.axis_index("bn")
    x, z = ad % 2, ad // 2
    core, y = bn % 2, bn // 2
    sibling = (ad, flip(bn, 1))
    x_mate = (flip(ad, 1), bn)
    y_mate = (ad, flip(bn, 2))
    own = {"y": y, "x": x, "h": z // 2, "l": z % 2}
    mates = {"y": y_mate, "x": x_mate, "h": (flip(ad, 4), bn), "l": (flip(ad, 2), bn)}
    other_core = 1 - core

    loads = [(w_qkv.at[:, pl.ds(k * width, width)]) for k in range(3)] + [w_out]
    for k in range(4):
        loads.append(w_ff_in.at[:, pl.ds(k * width, width)])
        loads.append(w_ff_out.at[pl.ds(k * width, width), :])
    loads += [join_query, join_key, join_value]
    for k in range(4):
        loads.append(w_ff_out.at[pl.ds(k * width, width), :])
        loads.append(w_ff_in.at[:, pl.ds(k * width, width)])
    loads += [w_out] + [w_qkv.at[:, pl.ds(k * width, width)] for k in range(3)]
    free_slots = list(range(SLOTS))
    in_flight = []
    next_load = [0]

    def fill():
        while free_slots and next_load[0] < len(loads):
            slot = free_slots.pop(0)
            copy = pltpu.make_async_copy(loads[next_load[0]], ring.at[slot], ring_sem.at[slot])
            copy.start()
            in_flight.append((slot, copy))
            next_load[0] += 1

    def take():
        slot, copy = in_flight.pop(0)
        copy.wait()
        return slot

    def release(slot):
        free_slots.append(slot)
        fill()

    fill()
    upstream_copy = pltpu.make_async_copy(cotangent_far, cotangent, local_sem.at[6])
    upstream_copy.start()
    bank_own = []
    for i, bank in enumerate((adapt_down, adapt_up)):
        for side in range(2):
            bank_own.append(
                pltpu.make_async_copy(
                    bank.at[pl.ds(side * (width // 8), width // 8), :],
                    banks.at[i, bn, side],
                    local_sem.at[2 + 2 * i + side],
                )
            )
            bank_own[-1].start()

    barrier = pltpu.get_barrier_semaphore()
    for mate in [sibling, *mates.values()]:
        pl.semaphore_signal(barrier, inc=1, device_id=mate, device_id_type=MESH)

    started = []

    def send(source, target, recv_sem, mate):
        slot = len(started) % SENDS
        if len(started) >= SENDS:
            started[-SENDS].wait_send()
        copy = pltpu.make_async_remote_copy(
            src_ref=source,
            dst_ref=target,
            send_sem=send_sem.at[slot],
            recv_sem=recv_sem,
            device_id=mate,
            device_id_type=MESH,
        )
        copy.start()
        started.append(copy)
        return copy

    def row_views(index):
        if index < 8:
            return rows.at[index]
        if index < 12:
            return rows_ff.at[:, :, index - 8]
        return rows_qkv.at[:, :, index - 12]

    def row_half(index, side):
        if index < 8:
            piece = rows[index, :, side, core]
        elif index < 12:
            piece = rows_ff[:, side, index - 8, core]
        else:
            piece = rows_qkv[:, side, index - 12, core]
        return piece.reshape(4 * PIECE, tokens)

    def col_ref(index):
        return hidden if index == 0 else cols.at[index - 1]

    row_copies, col_copies = {}, {}
    arrived = set()

    def share_row(index):
        row_copies[index] = send(
            row_views(index).at[:, :, other_core],
            rows_sib.at[index],
            row_recv.at[index],
            sibling,
        )

    def share_col(index):
        col_copies[index] = send(
            col_ref(index),
            cols_sib.at[index],
            col_recv.at[index],
            sibling,
        )

    cross = {}
    lanes_of = [
        pl.ds(pl.multiple_of(side * half_width, half_width), half_width) for side in (y, 1 - y)
    ]

    def cross_send(key, source, target, sem, index, mate):
        cross[key] = send(source, target, sem.at[index], mate)

    def col_over_x(i):
        cross_send(("cx", i), col_ref(2 * i), cols_x.at[0, i], col_x_recv, (0, i), x_mate)

    def col_over_y(k):
        source = cols.at[2 + k, :, lanes_of[1]]
        cross_send(("cy", k), source, cols_y.at[0, k], col_y_recv, (0, k), y_mate)

    def need(copy_key, table=cross):
        if (id(table), copy_key) not in arrived:
            table[copy_key].wait_recv()
            arrived.add((id(table), copy_key))

    def pass_col_x(i):
        if ("fx", i) not in cross:
            need(("cx", i))
            cross_send(
                ("fx", i), cols_x.at[0, i], cols_x.at[1, i], col_x_recv, (1, i), sibling
            )

    def pass_col_y(k):
        need(("cy", k))
        cross_send(
            ("fy", k), cols_y.at[0, k], cols_y.at[1, k], col_y_recv, (1, k), sibling
        )

    def start_x(unit):
        left, right = UNITS[unit][0]
        n = left - 8
        sem = row_x_recv
        source = row_views(left).at[:, 1 - x, core]
        cross_send(("rx", n, 0), source, rows_x.at[0, n], sem, (0, n), x_mate)
        pass_col_x(right // 2)
        need(left, row_copies)
        cross_send(
            ("rx", n, 1), rows_sib.at[left, :, 1 - x], rows_x.at[1, n], sem, (1, n), x_mate
        )

    def product_x(unit):
        left, right = UNITS[unit][0]
        n, i = left - 8, right // 2
        need(right, col_copies)
        need(("fx", i))
        flat = (4 * PIECE, tokens)
        total = matmul(row_half(left, x), col_ref(right)[...])
        total += matmul(rows_sib[left, :, x].reshape(flat), cols_sib[right])
        for k in range(2):
            need(("rx", n, k))
            total += matmul(rows_x[k, n].reshape(flat), cols_x[k, i])
        total = total.astype(low).reshape(2, 2, PIECE, width)
        part[unit, 0, x] = total[..., :half_width]
        part[unit, 1, x] = total[..., half_width:]

    def start_y(unit):
        if ("ry", 0) not in cross:
            sem = row_y_recv
            cross_send(("ry", 0), rows.at[6, :, :, core], rows_y.at[0], sem, 0, y_mate)
            for k in range(4):
                pass_col_y(k)
            need(6, row_copies)
            cross_send(("ry", 1), rows_sib.at[6], rows_y.at[1], sem, 1, y_mate)

    def product_y(unit):
        left, right = UNITS[unit][0]
        k = right - 3
        need(right, col_copies)
        need(("fy", k))
        flat = (4 * PIECE, tokens)
        for i in range(2):
            need(("ry", i))
        for side in range(2):
            total = matmul(row_half(left, side), cols[2 + k, :, lanes_of[0]])
            total += matmul(
                rows_sib[left, :, side].reshape(flat), cols_sib[right, :, lanes_of[0]]
            )
            for i in range(2):
                total += matmul(rows_y[i, :, side].reshape(flat), cols_y[i, k])
            part[unit, y, side] = total.astype(low).reshape(2, 2, PIECE, half_width)

    axes = ("y", "x", "h", "l")
    recvs = (recv_one, recv_two, recv_three, recv_four)
    copies, last = {}, {}
    units = len(UNITS)

    def half(unit, side):
        total = None
        for left, right in UNITS[unit]:
            need(left, row_copies)
            need(right, col_copies)
            term = matmul(row_half(left, side), col_ref(right)[...])
            term += matmul(
                rows_sib[left, :, side].reshape(4 * PIECE, tokens), cols_sib[right]
            )
            total = term if total is None else total + term
        total = total.astype(low).reshape(2, 2, PIECE, width)
        part[unit, 0, side] = total[..., :half_width]
        part[unit, 1, side] = total[..., half_width:]

    def place(done, axis, index):
        fixed = {name: own[name] for name in done}
        fixed[axis] = index
        left = [name for name in axes if name not in done]
        inside = tuple(index if name == axis else slice(None) for name in left)
        return tuple(fixed.get(name, slice(None)) for name in axes), inside

    def landing(unit, stage):
        return WHOLE.index(unit) if stage == 0 else unit

    def push(unit, stage):
        order = ORDERS[unit]
        axis = order[stage]
        where, _ = place(order[:stage], axis, 1 - own[axis])
        copies[unit, stage] = send(
            part.at[(unit, *where)],
            recvs[stage].at[landing(unit, stage)],
            stage_recv.at[stage, unit],
            mates[axis],
        )

    def start(unit):
        if unit in CROSS_X:
            start_x(unit)
        elif unit in CROSS_Y:
            start_y(unit)
        elif ORDERS[unit][0] == "x":
            half(unit, 1 - x)
            push(unit, 0)
            half(unit, x)
        else:
            half(unit, 0)
            half(unit, 1)
            push(unit, 0)

    def add(unit, stage, axis, index):
        where, inside = place(ORDERS[unit][: stage + 1], axis, index)
        mine = part[(unit, *where)].astype(jnp.float32)
        part[(unit, *where)] = (mine + recvs[stage][(landing(unit, stage), *inside)].astype(jnp.float32)).astype(low)

    def advance(unit, stage):
        if stage == 0 and unit not in WHOLE:
            if unit in CROSS_X:
                product_x(unit)
            else:
                product_y(unit)
            push(unit, 1)
            return
        copies[unit, stage].wait_recv()
        axis = ORDERS[unit][stage + 1]
        add(unit, stage, axis, 1 - own[axis])
        push(unit, stage + 1)
        add(unit, stage, axis, own[axis])

    def close(unit):
        copies[unit, 3].wait_recv()
        total = part[(unit, *(own[name] for name in axes))].astype(jnp.float32)
        sums[unit, core] = (total + recv_four[unit].astype(jnp.float32)).astype(low)
        last[unit] = send(
            sums.at[unit, core],
            sums.at[unit, core],
            last_recv.at[unit],
            sibling,
        )

    step_rows = tokens

    def over_rows(body, init=0):
        return body(slice(None), 0, init)

    def over_pieces(body, init=0):
        for p in range(blocks):
            init = body(p, init)
        return init

    def spot(p):
        return p // 4, (p // 2) % 2, p % 2

    def put_t(index, value):
        rows[index] = value.reshape(4, 2, 2, PIECE, tokens)

    def get_t(index):
        return rows[index].reshape(width, tokens)

    def fold(value):
        return value.reshape(PIECE // 8, 8, tokens).sum(0)

    length = lengths[0]
    for k in range(3):
        slot = take()
        value = matmul(hidden[...], ring[slot])
        release(slot)
        if k == 0:
            value = value * 0.125
        qkv_t[pl.ds(k * width, width), :] = value.astype(low).T
    pl.semaphore_wait(barrier, 1 + len(mates))
    banks_in = (adapt_down, adapt_up)
    half_bank = width // 8
    far = flip(bn, 2)

    def bank_half(bank, side):
        return bank.at[pl.ds(pl.multiple_of(side * half_bank, half_bank), half_bank), :]

    bank_y, bank_x, bank_sib = [], [], []

    def send_bank(source, i, where, kind, mate):
        return send(
            source, banks.at[(i, *where)], bank_recv.at[i, kind], mate
        )

    for i in range(2):
        bank_y.append(send_bank(bank_half(banks_in[i], x), i, (bn, x), 0, y_mate))
    for i in range(2):
        for side in range(2):
            source = bank_half(banks_in[i], side)
            bank_sib.append(send_bank(source, i, (bn, side), 1 + side, sibling))

    def pass_from_y(i):
        bank_y[i].wait_recv()
        source = banks.at[i, far, x]
        bank_x.append(send_bank(source, i, (far, x), 3, x_mate))
        bank_sib.append(send_bank(source, i, (far, x), 4, sibling))

    def pass_from_x(i):
        bank_x[i].wait_recv()
        source = banks.at[i, far, 1 - x]
        bank_sib.append(send_bank(source, i, (far, 1 - x), 5, sibling))

    share_col(0)
    size = width // heads

    def head_rows(k, head):
        return pl.ds(pl.multiple_of(k * width + head * size, size), size)

    valid_keys = lax.broadcasted_iota(jnp.int32, (tokens, tokens), 0) < length

    def head_forward(head, carry):
        scores = matmul_tn(qkv_t[head_rows(1, head), :], qkv_t[head_rows(0, head), :])
        scores = jnp.where(valid_keys, scores, masked_value)
        scores = jnp.exp(scores - jnp.max(scores, 0, keepdims=True))
        share = (scores * (1.0 / jnp.sum(scores, 0, keepdims=True))).astype(low)
        probs[head] = share
        context = matmul(qkv_t[head_rows(2, head), :], share)
        low_tmp_two[pl.ds(pl.multiple_of(head * size, size), size), :] = context.astype(low)
        return carry

    lax.fori_loop(0, heads, head_forward, 0, unroll=3)
    pass_from_y(0)
    cols[0] = low_tmp_two[...].T
    share_col(1)
    slot = take()
    acc[...] = matmul(cols[0], ring[slot])
    release(slot)

    def norm_rows(total):
        center = total - jnp.mean(total, -1, keepdims=True)
        rstd = lax.rsqrt(jnp.mean(center * center, -1, keepdims=True) + epsilon)
        return center * rstd, rstd

    def norm_first(r, i, carry):
        normed, rstd = norm_rows(hidden[r, :].astype(jnp.float32) + acc[r, :])
        stat[r, :] = jnp.broadcast_to(rstd, (step_rows, 128))
        low_tmp[r, :] = normed.astype(low)
        one_rows = normed * gain_attn
        wide[r, :] = one_rows
        cols[1, r, :] = one_rows.astype(low)
        return carry

    over_rows(norm_first)
    share_col(2)
    norm_one[...] = low_tmp[...].T.reshape(blocks, PIECE, tokens)
    stat_one[...] = stat[...].T[:8]

    for k in range(4):
        slot = take()
        acc[...] = matmul(cols[1], ring[slot])
        release(slot)
        unit_base = 2 + (k % 2) * 2
        lanes = pl.ds((k // 2) * half_width, half_width)

        def gelu_rows(r, i, carry):
            before = acc[r, :]
            cdf, density = normal_parts(before)
            act = (before * cdf).astype(low)
            low_tmp[r, :] = act
            cols[unit_base, r, lanes] = act[:, :half_width]
            cols[unit_base + 1, r, lanes] = act[:, half_width:]
            cols[9, r, :] = (cdf + before * density).astype(low)
            return carry

        over_rows(gelu_rows)
        slope[pl.ds(k * blocks, blocks)] = cols[9].T.reshape(blocks, PIECE, tokens)
        slot = take()
        value = matmul(low_tmp[...], ring[slot])
        release(slot)
        acc_two[...] = value if k == 0 else acc_two[...] + value
        if k == 0:
            pass_from_y(1)
            for i in range(2):
                col_over_x(i)
        if k == 2:
            pass_from_x(0)
    for k in range(4):
        col_over_y(k)
    for index in range(3, 7):
        share_col(index)

    def norm_second(r, i, carry):
        normed, rstd = norm_rows(wide[r, :] + acc_two[r, :])
        stat[r, :] = jnp.broadcast_to(rstd, (step_rows, 128))
        low_tmp[r, :] = normed.astype(low)
        two_rows = normed * gain_ff
        wide[r, :] = two_rows
        cols[6, r, :] = two_rows.astype(low)
        return carry

    over_rows(norm_second)
    share_col(7)
    norm_two[...] = low_tmp[...].T.reshape(blocks, PIECE, tokens)
    stat_two[...] = stat[...].T[:8]
    put_t(3, cols[6].T)
    share_row(3)

    pass_from_x(1)
    slot_query = take()
    low_tmp[...] = matmul(cols[6], ring[slot_query]).astype(low)
    put_t(4, low_tmp[...].T)
    share_row(4)
    slot_key = take()
    put_t(2, matmul(ring[slot_key], get_t(4)).astype(low))
    share_row(2)

    for copy in bank_own:
        copy.wait()
    for copy in bank_sib:
        copy.wait_recv()
    acc_t[...] = matmul(banks[0].reshape(width, width), get_t(3)).reshape(blocks, PIECE, tokens)
    acc_t_two[...] = matmul(banks[1].reshape(width, width), get_t(2)).reshape(
        blocks, PIECE, tokens
    )
    score_scale = 1.0 / math.sqrt(width)
    groups = PIECE // adapters

    def grouped(value):
        return value.reshape(groups, adapters, tokens)

    def adapter_rows(p, logits):
        inner = acc_t[p]
        cdf, density = normal_parts(inner)
        act = inner * cdf
        active[p] = act
        bank_slope[p] = (cdf + inner * density).astype(low)
        return logits + grouped(act * acc_t_two[p]).sum(0)

    logits = over_pieces(adapter_rows, jnp.zeros((adapters, tokens), jnp.float32)) * score_scale
    logits = jnp.exp(logits - jnp.max(logits, 0, keepdims=True))
    shares = logits / jnp.sum(logits, 0, keepdims=True)

    def spread(value):
        return jnp.concatenate([value] * groups, 0)

    wide_shares = spread(shares)

    def mixing_rows(p, carry):
        low_tmp_two[pl.ds(p * PIECE, PIECE), :] = (
            wide_shares * active[p]
        ).astype(low)
        return carry

    over_pieces(mixing_rows)
    cols[8] = low_tmp_two[...].T
    share_col(9)
    acc[...] = matmul(cols[8], banks[1].reshape(width, width))

    def joined_rows(r, i, carry):
        cols[7, r, :] = (wide[r, :] + acc[r, :]).astype(low)
        return carry

    over_rows(joined_rows)
    share_col(8)
    slot_value = take()
    acc[...] = matmul(cols[7], ring[slot_value])

    upstream_copy.wait()

    def norm_third(r, i, gain_part):
        normed, rstd = norm_rows(wide[r, :] + acc[r, :])
        gain = gain_out
        acc_two[r, :] = normed * gain
        token = lax.broadcasted_iota(jnp.int32, (step_rows, 1), 0) + i * step_rows
        upstream = jnp.where(token < length, cotangent[r, :].astype(jnp.float32), 0.0)
        product = upstream * normed
        gained = upstream * gain
        third = rstd * (
            gained
            - jnp.mean(gained, -1, keepdims=True)
            - normed * jnp.mean(gained * normed, -1, keepdims=True)
        )
        low_tmp[r, :] = third.astype(low)
        return gain_part + product.reshape(step_rows // 8, 8, width).sum(0)

    gain_part = over_rows(norm_third, jnp.zeros((8, width), jnp.float32))
    out_copy = pltpu.make_async_copy(acc_two, output, local_sem.at[0])
    out_copy.start()
    gain_sum[0] = jnp.broadcast_to(jnp.sum(gain_part, 0, keepdims=True), (8, width))
    put_t(0, low_tmp[...].T)
    share_row(0)

    state = {}

    def value_back():
        second[...] = matmul(ring[slot_value], get_t(0)).reshape(blocks, PIECE, tokens)
        release(slot_value)

        def mix_rows(p, carry):
            zz, xx, cc = spot(p)
            rows[1, zz, xx, cc] = second[p].astype(low)
            return carry

        over_pieces(mix_rows)
        share_row(1)
        acc_t[...] = matmul(banks[1].reshape(width, width), get_t(1)).reshape(blocks, PIECE, tokens)

    def adapter_grads():
        def share_rows(p, total):
            return total + grouped(acc_t[p] * active[p]).sum(0)

        share_grad = over_pieces(share_rows, jnp.zeros((adapters, tokens), jnp.float32))
        logit_grad = shares * (share_grad - jnp.sum(shares * share_grad, 0, keepdims=True))
        wide_logit = spread(logit_grad * score_scale)

        def adapter_back(p, carry):
            act_grad = acc_t[p] * wide_shares + wide_logit * acc_t_two[p]
            where = pl.ds(p * PIECE, PIECE)
            low_tmp_two[where, :] = (wide_logit * active[p]).astype(low)
            bank_slope[p] = (bank_slope[p].astype(jnp.float32) * act_grad).astype(low)
            return carry

        over_pieces(adapter_back)
        cols[9] = low_tmp_two[...].T
        share_col(10)
        cols[10] = bank_slope[...].reshape(width, tokens).T
        share_col(11)

    def probe_back():
        cols[11] = matmul(cols[9], banks[1].reshape(width, width)).astype(low)
        share_col(12)
        low_tmp[...] = matmul(cols[11], ring[slot_key]).astype(low)
        release(slot_key)
        put_t(5, low_tmp[...].T)
        share_row(5)
        low_tmp[...] = matmul(cols[10], banks[0].reshape(width, width)).astype(low)
        low_tmp_two[...] = low_tmp[...].T
        acc_t[...] = matmul(ring[slot_query], get_t(5)).reshape(blocks, PIECE, tokens)
        release(slot_query)

    def norm_back(index, gain, normed_ref, stat_ref, upstream_of, factor):
        gain_col[...] = jnp.broadcast_to(gain, (128, width)).T.reshape(blocks, PIECE, 128)

        def gained(p):
            column = gain_col[p]
            return acc_t[p] * jnp.concatenate([column] * (tokens // 128), 1)

        def first_pass(p, carry):
            upstream = upstream_of(p)
            acc_t[p] = upstream
            normed = normed_ref[p].astype(jnp.float32)
            gain_of = jnp.sum(upstream * normed, -1, keepdims=True)
            weighted = gained(p)
            gain_col[p] = jnp.broadcast_to(gain_of, (PIECE, 128))
            acc_t[p] = weighted
            return carry[0] + fold(weighted), carry[1] + fold(weighted * normed)

        zeros = jnp.zeros((8, tokens), jnp.float32)
        plain, tilted = over_pieces(first_pass, (zeros, zeros))
        mean_plain = jnp.sum(plain, 0, keepdims=True) * (1.0 / width)
        mean_tilted = jnp.sum(tilted, 0, keepdims=True) * (1.0 / width)
        rstd = stat_ref[0:1, :]

        def second_pass(p, carry):
            value = rstd * (acc_t[p] - mean_plain - normed_ref[p].astype(jnp.float32) * mean_tilted)
            second[p] = value
            zz, xx, cc = spot(p)
            rows[factor, zz, xx, cc] = value.astype(low)
            return carry

        over_pieces(second_pass)
        gain_sum[0, index : index + 1, :] = gain_col[...].reshape(width, 128).T[:1]

    def upstream_two(p):
        zz, xx, cc = spot(p)
        where = pl.ds(p * PIECE, PIECE)
        total = rows[0, zz, xx, cc].astype(jnp.float32) + second[p]
        return total + low_tmp_two[where, :].astype(jnp.float32) + acc_t[p]

    def norm_two_back():
        norm_back(1, gain_ff, norm_two, stat_two, upstream_two, 6)
        share_row(6)

    def ff_back(k):
        slot = take()
        acc_t_two[...] = matmul(ring[slot], get_t(6)).reshape(blocks, PIECE, tokens)
        release(slot)

        def slope_rows(p, carry):
            value = acc_t_two[p] * slope[k * blocks + p].astype(jnp.float32)
            rows_ff[k, p // 8, (p % 8) // 2, p % 2] = value.astype(low)
            return carry

        over_pieces(slope_rows)
        slot = take()
        value = matmul(ring[slot], rows_ff[k].reshape(width, tokens))
        value = value.reshape(blocks, PIECE, tokens)
        release(slot)
        acc_t[...] = value if k == 0 else acc_t[...] + value
        if k == 3:
            for index in range(8, 12):
                share_row(index)

    def upstream_one(p):
        return second[p] + acc_t[p]

    def norm_one_back():
        norm_back(0, gain_attn, norm_one, stat_one, upstream_one, 7)
        share_row(7)
        slot = take()
        low_tmp_two[...] = matmul(ring[slot], get_t(7)).astype(low)
        release(slot)

    heads_step = 3
    step_pieces = heads_step * size // PIECE

    def head_backward(group, carry):
        grads = [[], [], []]
        for i in range(heads_step):
            head = group * heads_step + i
            query, key, value = [qkv_t[head_rows(k, head), :] for k in range(3)]
            upstream = low_tmp_two[pl.ds(pl.multiple_of(head * size, size), size), :]
            share = probs[head]
            share_wide = share.astype(jnp.float32)
            prob_grad = matmul_tn(value, upstream)
            delta = jnp.sum(share_wide * prob_grad, 0, keepdims=True)
            score_grad = (share_wide * (prob_grad - delta)).astype(low)
            grads[0].append((matmul(key, score_grad) * 0.125).astype(low))
            grads[1].append(matmul_t(query, score_grad).astype(low))
            grads[2].append(matmul_t(upstream, share).astype(low))
        for k in range(3):
            stacked = jnp.concatenate(grads[k], 0).reshape(step_pieces, PIECE, tokens)
            for i in range(step_pieces):
                p = k * blocks + group * step_pieces + i
                rows_qkv[p // 12, (p // 6) % 2, (p % 6) // 2, p % 2] = stacked[i]
        return carry

    def attention_back():
        lax.fori_loop(0, heads // heads_step, head_backward, 0)
        for index in range(12, 15):
            share_row(index)

    def input_back():
        for k in range(3):
            slot = take()
            block = rows_qkv[...].reshape(3 * blocks, PIECE, tokens)[k * blocks : (k + 1) * blocks]
            value = matmul(ring[slot], block.reshape(width, tokens)).reshape(blocks, PIECE, tokens)
            release(slot)
            second[...] = second[...] + value
        acc[...] = second[...].reshape(width, tokens).T
        state["in"] = pltpu.make_async_copy(acc, grad_in, local_sem.at[1])
        state["in"].start()

    gain_mates = (sibling, x_mate, y_mate, mates["l"], mates["h"])

    def gain_step(stage):
        if stage > 0:
            state["gain"].wait_recv()
            total = gain_sum[stage - 1] + gain_from[stage - 1]
            if stage == 5:
                gain_sums[...] = total
                return
            gain_sum[stage] = total
        state["gain"] = send(
            gain_sum.at[stage],
            gain_from.at[stage],
            gain_recv.at[stage],
            gain_mates[stage],
        )

    chain = [value_back, adapter_grads, probe_back, norm_two_back]
    chain += [functools.partial(ff_back, k) for k in range(4)]
    chain += [norm_one_back, attention_back, input_back]
    progress = [0] * units
    since_chain, gain_stage = 0, 0
    for action in SEQUENCE:
        if action < 0:
            chain.pop(0)()
        elif progress[action] == 0:
            start(action)
        elif progress[action] < 4:
            advance(action, progress[action] - 1)
        else:
            close(action)
        if action >= 0:
            progress[action] += 1
        if not chain:
            if since_chain % 4 == 0 and gain_stage < 6:
                gain_step(gain_stage)
                gain_stage += 1
            since_chain += 1
    for stage in range(gain_stage, 6):
        gain_step(stage)
    for unit in range(units):
        last[unit].wait_recv()
    for copy in started[-SENDS:]:
        copy.wait_send()
    out_copy.wait()
    state["in"].wait()


def run_layer(heads, adapters, arrays):
    hidden = arrays[0]
    tokens, width = hidden.shape
    low, wide = jnp.bfloat16, jnp.float32
    blocks = width // PIECE
    units = len(UNITS)
    dma = pltpu.SemaphoreType.DMA
    vmem = pl.BlockSpec(memory_space=pltpu.VMEM)
    smem = pl.BlockSpec(memory_space=pltpu.SMEM)
    far = pl.BlockSpec(memory_space=pl.ANY)
    half_width = width // 2
    return pl.pallas_call(
        functools.partial(layer_kernel, heads, adapters),
        out_shape=(
            jax.ShapeDtypeStruct((tokens, width), wide),
            jax.ShapeDtypeStruct((tokens, width), wide),
            jax.ShapeDtypeStruct((units, 2, PIECE, half_width), low),
            jax.ShapeDtypeStruct((8, width), wide),
        ),
        in_specs=[
            vmem, smem, far, far, far, vmem, far, far, vmem, far, far, far, far, far, vmem,
        ],
        out_specs=[far, far, vmem, vmem],
        scratch_shapes=[
            pltpu.VMEM((8, 4, 2, 2, PIECE, tokens), low),
            pltpu.VMEM((4, 2, 4, 2, PIECE, tokens), low),
            pltpu.VMEM((4, 2, 3, 2, PIECE, tokens), low),
            pltpu.VMEM((15, 4, 2, PIECE, tokens), low),
            pltpu.VMEM((12, tokens, width), low),
            pltpu.VMEM((13, tokens, width), low),
            pltpu.VMEM((2, 7, 4, PIECE, tokens), low),
            pltpu.VMEM((2, 2, tokens, width), low),
            pltpu.VMEM((2, 4, 2, PIECE, tokens), low),
            pltpu.VMEM((2, 4, tokens, half_width), low),
            pltpu.VMEM((SLOTS, width, width), low),
            pltpu.VMEM((2, 4, 2, width // 8, width), low),
            pltpu.VMEM((tokens, width), wide),
            pltpu.VMEM((tokens, width), wide),
            pltpu.VMEM((tokens, width), wide),
            pltpu.VMEM((blocks, PIECE, tokens), wide),
            pltpu.VMEM((blocks, PIECE, tokens), wide),
            pltpu.VMEM((blocks, PIECE, tokens), wide),
            pltpu.VMEM((blocks, PIECE, tokens), low),
            pltpu.VMEM((blocks, PIECE, tokens), wide),
            pltpu.VMEM((blocks, PIECE, tokens), low),
            pltpu.VMEM((blocks, PIECE, tokens), low),
            pltpu.VMEM((4 * blocks, PIECE, tokens), low),
            pltpu.VMEM((3 * width, tokens), low),
            pltpu.VMEM((heads, tokens, tokens), low),
            pltpu.VMEM((tokens, width), low),
            pltpu.VMEM((width, tokens), low),
            pltpu.VMEM((tokens, 128), wide),
            pltpu.VMEM((8, tokens), wide),
            pltpu.VMEM((8, tokens), wide),
            pltpu.VMEM((blocks, PIECE, 128), wide),
            pltpu.VMEM((tokens, width), low),
            pltpu.VMEM((units, 2, 2, 2, 2, PIECE, half_width), low),
            pltpu.VMEM((len(WHOLE), 2, 2, 2, PIECE, half_width), low),
            pltpu.VMEM((units, 2, 2, PIECE, half_width), low),
            pltpu.VMEM((units, 2, PIECE, half_width), low),
            pltpu.VMEM((units, PIECE, half_width), low),
            pltpu.VMEM((5, 8, width), wide),
            pltpu.VMEM((5, 8, width), wide),
            dma((SLOTS,)),
            dma((7,)),
            dma((SENDS,)),
            dma((2, 6)),
            dma((15,)),
            dma((13,)),
            dma((2, 7)),
            dma((2, 2)),
            dma((2,)),
            dma((2, 4)),
            dma((4, units)),
            dma((units,)),
            dma((5,)),
        ],
        compiler_params=pltpu.CompilerParams(
            collective_id=0, has_side_effects=True, vmem_limit_bytes=63 * 2**20
        ),
    )(*arrays)


def finish_kernel(
    sums_far,
    gain_sums_far,
    output,
    grad_in,
    out_output,
    out_grad_in,
    out_qkv,
    out_proj,
    out_gain_attn,
    out_ff_in,
    out_ff_out,
    out_gain_ff,
    out_query,
    out_key,
    out_value,
    out_down,
    out_up,
    out_gain_out,
    turned,
    sums,
    gain_sums,
    held,
    copy_sem,
):
    fetched = [
        pltpu.make_async_copy(sums_far, sums, copy_sem.at[2]),
        pltpu.make_async_copy(gain_sums_far, gain_sums, copy_sem.at[3]),
    ]
    through = [
        pltpu.make_async_copy(output, held.at[0], copy_sem.at[0]),
        pltpu.make_async_copy(grad_in, held.at[1], copy_sem.at[1]),
    ]
    for copy in fetched + through:
        copy.start()
    for copy in fetched:
        copy.wait()
    ad = lax.axis_index("ad")
    core = lax.axis_index("bn") % 2
    width = sums.shape[3]
    own = pl.ds(pl.multiple_of(core * (width // 2), width // 2), width // 2)

    def columns(out, slot, first, count):
        value = sums[first : first + count].reshape(count * 2 * PIECE, width)
        extent = pl.ds(0, count * 2 * PIECE)
        turned[slot, :, extent] = value.astype(jnp.float32).T
        out[...] = turned[slot, own, extent]

    columns(out_value, 0, 0, 1)
    columns(out_up, 1, 1, 1)
    columns(out_down, 2, 2, 1)
    columns(out_key, 0, 3, 1)
    columns(out_query, 1, 4, 1)
    for copy in through:
        copy.wait()
    passed = [
        pltpu.make_async_copy(held.at[0], out_output, copy_sem.at[0]),
        pltpu.make_async_copy(held.at[1], out_grad_in, copy_sem.at[1]),
    ]
    for copy in passed:
        copy.start()
    columns(out_ff_in, 2, 9, 4)
    columns(out_proj, 0, 13, 1)
    columns(out_qkv, 1, 14, 3)
    for i in range(2):
        value = sums[5 + 2 * core + i].reshape(2 * PIECE, width)
        out_ff_out[:, pl.ds(i * width, width)] = value.astype(jnp.float32)
    total = gain_sums.shape[1]
    piece = out_gain_attn.shape[0]
    rolled = pltpu.roll(gain_sums[...], lax.rem(total - ad * piece, total), 1)[:, :piece]
    for index, out in enumerate((out_gain_attn, out_gain_ff, out_gain_out)):
        out[...] = rolled[index : index + 1].reshape(piece)
    for copy in passed:
        copy.wait()


def finish(sums, gain_sums, output, grad_in, width):
    quarter, eighth = width // 4, width // 8
    far = pl.BlockSpec(memory_space=pl.ANY)
    shapes = [
        output.shape,
        grad_in.shape,
        (quarter, 3 * eighth),
        (quarter, eighth),
        (eighth,),
        (quarter, 4 * eighth),
        (eighth, 4 * quarter),
        (eighth,),
    ]
    shapes += [(quarter, eighth)] * 5 + [(eighth,)]
    return pl.pallas_call(
        finish_kernel,
        out_shape=tuple(jax.ShapeDtypeStruct(shape, jnp.float32) for shape in shapes),
        in_specs=[far] * 4,
        out_specs=[far] * 2 + [pl.BlockSpec(memory_space=pltpu.VMEM)] * 12,
        scratch_shapes=[
            pltpu.VMEM((3, width // 2, 4 * eighth), jnp.float32),
            pltpu.VMEM(sums.shape, sums.dtype),
            pltpu.VMEM(gain_sums.shape, gain_sums.dtype),
            pltpu.VMEM((2, *output.shape), output.dtype),
            pltpu.SemaphoreType.DMA((4,)),
        ],
        compiler_params=pltpu.CompilerParams(vmem_limit_bytes=62 * 2**20),
    )(sums, gain_sums, output, grad_in)


def fast_local(*arrays):
    arrays = list(arrays)
    width = arrays[0].shape[1]
    adapters = arrays[12].shape[1]
    bank_shape = arrays[12].shape[:2] + (-1,)
    for i in (12, 13):
        arrays[i] = arrays[i].reshape(-1, width)
    output, grad_in, sums, gain_sums = run_layer(H, adapters, arrays)
    results = list(finish(sums, gain_sums, output, grad_in, width))
    results[6] = results[6].T
    for i in (11, 12):
        results[i] = results[i].reshape(bank_shape)
    return tuple(results)


def local(
    hidden_in,
    lengths,
    cotangent,
    w_qkv,
    w_out,
    gain_attn,
    w_ff_in,
    w_ff_out,
    gain_ff,
    join_query,
    join_key,
    join_value,
    adapt_down,
    adapt_up,
    gain_out,
):
    seq_count = lengths.shape[0]
    tok_rows, model_width = hidden_in.shape
    slot_len = tok_rows // seq_count
    head_count = H
    head_size = model_width // head_count
    score_scale = 1.0 / math.sqrt(head_size)
    adapters = adapt_down.shape[1]
    down_flat = lax.all_gather(adapt_down.reshape(-1, model_width), "bn", axis=0, tiled=True)
    up_flat = lax.all_gather(adapt_up.reshape(-1, model_width), "bn", axis=0, tiled=True)
    valid = lax.broadcasted_iota(jnp.int32, (seq_count, slot_len), 1) < lengths[:, None]
    row_ok = valid.reshape(tok_rows, 1).astype(jnp.float32)
    tokens_wide = hidden_in.astype(jnp.float32)
    qkv = matmul(hidden_in, w_qkv).astype(jnp.bfloat16)
    queries = qkv[:, :model_width].reshape(seq_count, slot_len, head_count, head_size)
    key_rows = qkv[:, model_width : 2 * model_width].reshape(
        seq_count, slot_len, head_count, head_size
    )
    values = qkv[:, 2 * model_width :].reshape(seq_count, slot_len, head_count, head_size)

    def attend_scores():
        raw_scores = (
            jnp.einsum("sqhe,skhe->shqk", queries, key_rows, preferred_element_type=jnp.float32)
            * score_scale
        )
        return jnp.where(valid[:, None, None, :], raw_scores, masked_value)

    scores = attend_scores()
    row_max = jnp.max(scores, -1, keepdims=True)
    log_total = row_max + jnp.log(jnp.sum(jnp.exp(scores - row_max), -1, keepdims=True))
    probs = jnp.exp(scores - log_total).astype(jnp.bfloat16)
    context = (
        jnp.einsum("shqk,skhe->sqhe", probs, values, preferred_element_type=jnp.float32)
        .reshape(tok_rows, model_width)
        .astype(jnp.bfloat16)
    )
    attn_out = matmul(context, w_out)
    hidden_one, norm_one_back = jax.vjp(layer_norm, tokens_wide + attn_out, gain_attn)
    hidden_one_low = hidden_one.astype(jnp.bfloat16)
    ff_pre = matmul(hidden_one_low, w_ff_in)
    ff_act, gelu_ff_back = jax.vjp(gelu_exact, ff_pre)
    ff_low = ff_act.astype(jnp.bfloat16)
    ff_out = matmul(ff_low, w_ff_out)
    hidden_two, norm_two_back = jax.vjp(layer_norm, hidden_one + ff_out, gain_ff)
    hidden_low = hidden_two.astype(jnp.bfloat16)
    query_join = matmul(hidden_low, join_query).astype(jnp.bfloat16)
    probe = matmul_t(query_join, join_key).astype(jnp.bfloat16)
    mixing, kept_state = adapter_forward(hidden_low, probe, down_flat, up_flat, adapters)
    joined_in = (hidden_two + matmul(mixing, up_flat)).astype(jnp.bfloat16)
    joined = matmul(joined_in, join_value)
    output, norm_out_back = jax.vjp(layer_norm, hidden_two + joined, gain_out)
    out_grad = cotangent.astype(jnp.float32) * row_ok
    sum_three, gain_out_grad = norm_out_back(out_grad)
    joined_grad = sum_three.astype(jnp.bfloat16)
    into_joined = matmul_t(joined_grad, join_value)
    mix_grad = into_joined.astype(jnp.bfloat16)
    inner_grad, weigh_grad = adapter_backward(kept_state, up_flat, mix_grad, adapters)
    hidden_back = matmul(inner_grad, down_flat)
    probe_grad = matmul(weigh_grad, up_flat).astype(jnp.bfloat16)
    query_in = matmul(probe_grad, join_key).astype(jnp.bfloat16)
    grad_two = sum_three + into_joined + hidden_back + matmul_t(query_in, join_query)
    sum_two, gain_ff_grad = norm_two_back(grad_two)
    ff_out_grad = sum_two.astype(jnp.bfloat16)
    ff_pre_grad = gelu_ff_back(matmul_t(ff_out_grad, w_ff_out))[0].astype(jnp.bfloat16)
    grad_one = sum_two + matmul_t(ff_pre_grad, w_ff_in)
    sum_one, gain_attn_grad = norm_one_back(grad_one)
    attn_grad = sum_one.astype(jnp.bfloat16)
    context_grad = (
        matmul_t(attn_grad, w_out)
        .astype(jnp.bfloat16)
        .reshape(seq_count, slot_len, head_count, head_size)
    )
    probs_wide = jnp.exp(attend_scores() - log_total)
    prob_grad = jnp.einsum(
        "sqhe,skhe->shqk", context_grad, values, preferred_element_type=jnp.float32
    )
    row_delta = jnp.sum(probs_wide * prob_grad, -1, keepdims=True)
    score_grad = (probs_wide * (prob_grad - row_delta)).astype(jnp.bfloat16)
    query_back = (
        jnp.einsum("shqk,skhe->sqhe", score_grad, key_rows, preferred_element_type=jnp.float32)
        * score_scale
    )
    key_back = (
        jnp.einsum("shqk,sqhe->skhe", score_grad, queries, preferred_element_type=jnp.float32)
        * score_scale
    )
    value_back = jnp.einsum(
        "shqk,sqhe->skhe", probs, context_grad, preferred_element_type=jnp.float32
    )
    qkv_grad = jnp.concatenate(
        [
            query_back.reshape(tok_rows, model_width),
            key_back.reshape(tok_rows, model_width),
            value_back.reshape(tok_rows, model_width),
        ],
        1,
    ).astype(jnp.bfloat16)
    grad_in = sum_one + matmul_t(qkv_grad, w_qkv)
    def shared_sum(gradient):
        columns = lax.psum_scatter(gradient, "ad", scatter_dimension=1, tiled=True)
        return lax.psum_scatter(
            columns.astype(jnp.bfloat16), "bn", scatter_dimension=0, tiled=True
        ).astype(jnp.float32)

    gains = lax.psum(
        lax.psum_scatter(
            jnp.stack([gain_attn_grad, gain_ff_grad, gain_out_grad]),
            "ad",
            scatter_dimension=1,
            tiled=True,
        ),
        "bn",
    )
    down_grad = shared_sum(matmul_tn(inner_grad, hidden_low))
    up_grad = shared_sum(matmul_tn(mixing, mix_grad) + matmul_tn(weigh_grad, probe))
    bank = adapt_down.shape[:2] + (-1,)
    return (
        output,
        grad_in,
        shared_sum(matmul_tn(hidden_in, qkv_grad)),
        shared_sum(matmul_tn(context, attn_grad)),
        gains[0],
        shared_sum(matmul_tn(hidden_one_low, ff_pre_grad)),
        shared_sum(matmul_tn(ff_low, ff_out_grad)),
        gains[1],
        shared_sum(matmul_tn(hidden_low, query_in)),
        shared_sum(matmul_tn(probe_grad, query_join)),
        shared_sum(matmul_tn(joined_in, joined_grad)),
        down_grad.reshape(bank),
        up_grad.reshape(bank),
        gains[2],
    )


def solution(mesh):
    placed = (
        P(("ad", "bn"), None),
        P(("ad", "bn")),
        P(("ad", "bn"), None),
        P(),
        P(),
        P(),
        P(),
        P(),
        P(),
        P(),
        P(),
        P(),
        P("bn", None, None),
        P("bn", None, None),
        P(),
    )
    sizes = (mesh.shape["ad"], mesh.shape["bn"])
    return jax.shard_map(
        fast_local if sizes == (8, 4) else local,
        mesh=mesh,
        in_specs=placed,
        out_specs=(
            P(("ad", "bn"), None),
            P(("ad", "bn"), None),
            P("bn", "ad"),
            P("bn", "ad"),
            P("ad"),
            P("bn", "ad"),
            P("bn", "ad"),
            P("ad"),
            P("bn", "ad"),
            P("bn", "ad"),
            P("bn", "ad"),
            P("bn", None, "ad"),
            P("bn", None, "ad"),
            P("ad"),
        ),
        check_vma=False,
    )
```

```python
import functools
import math

import jax
import jax.numpy as jnp
from jax import lax
from jax.experimental import pallas as pl
from jax.experimental.pallas import tpu as pltpu
from jax.sharding import PartitionSpec as P

H = 12


epsilon = 1e-06
masked_value = -1000000000.0
MESH = pl.DeviceIdType.MESH


def layer_norm(values, gain):
    center = values - jnp.mean(values, -1, keepdims=True)
    spread = jnp.mean(center * center, -1, keepdims=True)
    return center * lax.rsqrt(spread + epsilon) * gain


def gelu_exact(values):
    return jax.nn.gelu(values, approximate=False)


def matmul(left, right):
    return jnp.dot(left, right, preferred_element_type=jnp.float32)


def matmul_t(left, right):
    return lax.dot_general(
        left, right, (((1,), (1,)), ((), ())), preferred_element_type=jnp.float32
    )


def matmul_tn(left, right):
    return lax.dot_general(
        left, right, (((0,), (0,)), ((), ())), preferred_element_type=jnp.float32
    )


def adapter_forward(hidden, probe_rows, down_flat, up_flat, adapters):
    row_count, model_width = hidden.shape
    inner_pre = matmul_t(hidden, down_flat)
    active = gelu_exact(inner_pre)
    weigh_rows = matmul_t(probe_rows, up_flat)
    logits = jnp.sum((active * weigh_rows).reshape(row_count, -1, adapters), 1) / math.sqrt(
        model_width
    )
    shares = jax.nn.softmax(logits, -1)
    mixing = (
        (shares[:, None, :] * active.reshape(row_count, -1, adapters))
        .reshape(row_count, -1)
        .astype(jnp.bfloat16)
    )
    return (mixing, (inner_pre, active, weigh_rows, shares))


def adapter_backward(kept_state, up_flat, mix_grad, adapters):
    inner_pre, active, weigh_rows, shares = kept_state
    row_count, model_width = mix_grad.shape
    score_scale = 1.0 / math.sqrt(model_width)
    mix_in = matmul_t(mix_grad, up_flat).reshape(row_count, -1, adapters)
    active_three = active.reshape(row_count, -1, adapters)
    weigh_three = weigh_rows.reshape(row_count, -1, adapters)
    share_grad = jnp.sum(mix_in * active_three, 1)
    logit_grad = shares * (share_grad - jnp.sum(shares * share_grad, -1, keepdims=True))
    act_grad = mix_in * shares[:, None, :] + logit_grad[:, None, :] * score_scale * weigh_three
    weigh_grad = (
        (logit_grad[:, None, :] * score_scale * active_three)
        .reshape(row_count, -1)
        .astype(jnp.bfloat16)
    )
    unused, gelu_back = jax.vjp(gelu_exact, inner_pre)
    inner_grad = gelu_back(act_grad.reshape(row_count, -1))[0].astype(jnp.bfloat16)
    return (inner_grad, weigh_grad)


PIECE = 48
SLOTS = 5
SENDS = 48
UNITS = (
    ((0, 8),),
    ((1, 9), (2, 10)),
    ((3, 11),),
    ((4, 12),),
    ((5, 7),),
    ((6, 3),),
    ((6, 4),),
    ((6, 5),),
    ((6, 6),),
    ((8, 2),),
    ((9, 2),),
    ((10, 2),),
    ((11, 2),),
    ((7, 1),),
    ((12, 0),),
    ((13, 0),),
    ((14, 0),),
)


CROSS_X = (9, 10, 11, 12, 14, 15, 16)
CROSS_Y = (5, 6, 7, 8)
WHOLE = tuple(unit for unit in range(len(UNITS)) if unit not in CROSS_X + CROSS_Y)
ORDERS = (
    ("l", "y", "x", "h"),
    ("y", "l", "x", "h"),
    ("l", "y", "x", "h"),
    ("x", "l", "y", "h"),
    ("l", "x", "y", "h"),
    ("y", "l", "x", "h"),
    ("y", "l", "x", "h"),
    ("y", "x", "l", "h"),
    ("y", "x", "l", "h"),
    ("x", "y", "l", "h"),
    ("x", "l", "y", "h"),
    ("x", "y", "l", "h"),
    ("x", "y", "l", "h"),
    ("y", "l", "x", "h"),
    ("x", "y", "l", "h"),
    ("x", "y", "l", "h"),
    ("x", "y", "l", "h"),
)
SEQUENCE = (
    -1, -1, -1, 0, 1, -1, 3, 2, -1, 6, 7, 5, 8, -1, -1, -1, 4, -1, 9, 12, -1, 0, 11, -1,
    1, 9, 16, 3, 13, 6, 14, 5, 10, 12, 9, 3, 15, 16, 13, 11, 1, 12, 9, 6, 14, 3, 10, 0,
    13, 2, 16, 12, 5, 9, 3, 7, 15, 1, 11, 6, 4, 10, 0, 14, 16, 12, 13, 1, 8, 5, 11, 6,
    0, 2, 7, 15, 14, 16, 10, 13, 5, 4, 11, 7, 8, 15, 4, 14, 2, 10, 7, 8, 15, 4, 2, 8,
)

def flip(index, bit):
    return index + bit - 2 * bit * ((index // bit) % 2)


def normal_parts(values):
    cdf = 0.5 * (1.0 + lax.erf(values * (1.0 / math.sqrt(2.0))))
    density = jnp.exp(values * values * -0.5) * (1.0 / math.sqrt(2.0 * math.pi))
    return cdf, density


def layer_kernel(
    heads,
    adapters,
    hidden,
    lengths,
    cotangent_far,
    w_qkv,
    w_out,
    gain_attn,
    w_ff_in,
    w_ff_out,
    gain_ff,
    join_query,
    join_key,
    join_value,
    adapt_down,
    adapt_up,
    gain_out,
    output,
    grad_in,
    sums,
    gain_sums,
    rows,
    rows_ff,
    rows_qkv,
    rows_sib,
    cols,
    cols_sib,
    rows_x,
    cols_x,
    rows_y,
    cols_y,
    ring,
    banks,
    acc,
    acc_two,
    wide,
    acc_t,
    acc_t_two,
    active,
    bank_slope,
    second,
    norm_one,
    norm_two,
    slope,
    qkv_t,
    probs,
    low_tmp,
    low_tmp_two,
    stat,
    stat_one,
    stat_two,
    gain_col,
    cotangent,
    part,
    recv_one,
    recv_two,
    recv_three,
    recv_four,
    gain_sum,
    gain_from,
    ring_sem,
    local_sem,
    send_sem,
    bank_recv,
    row_recv,
    col_recv,
    row_x_recv,
    col_x_recv,
    hidden_x_recv,
    row_y_recv,
    col_y_recv,
    stage_recv,
    last_recv,
    gain_recv,
):
    low = jnp.bfloat16
    tokens, width = hidden.shape
    half_width = width // 2
    gain_attn, gain_ff, gain_out = [
        gain[...].reshape(1, width) for gain in (gain_attn, gain_ff, gain_out)
    ]
    blocks = rows.shape[1] * rows.shape[2] * rows.shape[3]
    ad = lax.axis_index("ad")
    bn = lax.axis_index("bn")
    x, z = ad % 2, ad // 2
    core, y = bn % 2, bn // 2
    sibling = (ad, flip(bn, 1))
    x_mate = (flip(ad, 1), bn)
    y_mate = (ad, flip(bn, 2))
    own = {"y": y, "x": x, "h": z // 2, "l": z % 2}
    mates = {"y": y_mate, "x": x_mate, "h": (flip(ad, 4), bn), "l": (flip(ad, 2), bn)}
    other_core = 1 - core

    loads = [(w_qkv.at[:, pl.ds(k * width, width)]) for k in range(3)] + [w_out]
    ff_blocks = [2 * (1 - y), 2 * (1 - y) + 1, 2 * y, 2 * y + 1]
    for block in ff_blocks:
        where = pl.ds(pl.multiple_of(block * width, width), width)
        loads.append(w_ff_in.at[:, where])
        loads.append(w_ff_out.at[where, :])
    loads += [join_query, join_key, join_value]
    for k in range(4):
        loads.append(w_ff_out.at[pl.ds(k * width, width), :])
        loads.append(w_ff_in.at[:, pl.ds(k * width, width)])
    loads += [w_out] + [w_qkv.at[:, pl.ds(k * width, width)] for k in range(3)]
    free_slots = list(range(SLOTS))
    in_flight = []
    next_load = [0]

    def fill():
        while free_slots and next_load[0] < len(loads):
            slot = free_slots.pop(0)
            copy = pltpu.make_async_copy(loads[next_load[0]], ring.at[slot], ring_sem.at[slot])
            copy.start()
            in_flight.append((slot, copy))
            next_load[0] += 1

    def take():
        slot, copy = in_flight.pop(0)
        copy.wait()
        return slot

    def release(slot):
        free_slots.append(slot)
        fill()

    fill()
    upstream_copy = pltpu.make_async_copy(cotangent_far, cotangent, local_sem.at[6])
    upstream_copy.start()
    bank_own = []
    for i, bank in enumerate((adapt_down, adapt_up)):
        for side in range(2):
            bank_own.append(
                pltpu.make_async_copy(
                    bank.at[pl.ds(side * (width // 8), width // 8), :],
                    banks.at[i, bn, side],
                    local_sem.at[2 + 2 * i + side],
                )
            )
            bank_own[-1].start()

    barrier = pltpu.get_barrier_semaphore()
    for mate in [sibling, *mates.values()]:
        pl.semaphore_signal(barrier, inc=1, device_id=mate, device_id_type=MESH)

    started = []

    def send(source, target, recv_sem, mate):
        slot = len(started) % SENDS
        if len(started) >= SENDS:
            started[-SENDS].wait_send()
        copy = pltpu.make_async_remote_copy(
            src_ref=source,
            dst_ref=target,
            send_sem=send_sem.at[slot],
            recv_sem=recv_sem,
            device_id=mate,
            device_id_type=MESH,
        )
        copy.start()
        started.append(copy)
        return copy

    def row_views(index):
        if index < 8:
            return rows.at[index]
        if index < 12:
            return rows_ff.at[:, :, index - 8]
        return rows_qkv.at[:, :, index - 12]

    def row_half(index, side):
        if index < 8:
            piece = rows[index, :, side, core]
        elif index < 12:
            piece = rows_ff[:, side, index - 8, core]
        else:
            piece = rows_qkv[:, side, index - 12, core]
        return piece.reshape(4 * PIECE, tokens)

    def col_ref(index):
        return hidden if index == 0 else cols.at[index - 1]

    row_copies, col_copies = {}, {}
    arrived = set()

    def share_row(index):
        row_copies[index] = send(
            row_views(index).at[:, :, other_core],
            rows_sib.at[index],
            row_recv.at[index],
            sibling,
        )

    def share_col(index):
        col_copies[index] = send(
            col_ref(index),
            cols_sib.at[index],
            col_recv.at[index],
            sibling,
        )

    cross = {}
    lanes_of = [
        pl.ds(pl.multiple_of(side * half_width, half_width), half_width) for side in (y, 1 - y)
    ]

    def cross_send(key, source, target, sem, index, mate):
        cross[key] = send(source, target, sem.at[index], mate)

    def col_over_x(i):
        cross_send(("cx", i), col_ref(2 * i), cols_x.at[0, i], col_x_recv, (0, i), x_mate)

    def half_hidden_over_x(side):
        where = pl.ds(side * (tokens // 2), tokens // 2)
        cross_send(
            ("hx", side), hidden.at[where], cols_x.at[0, 0, where], hidden_x_recv, side, x_mate
        )

    def col_over_y(k):
        source = cols.at[2 + k, :, lanes_of[1]]
        cross_send(("cy", k), source, cols_y.at[0, k], col_y_recv, (0, k), y_mate)

    def need(copy_key, table=cross):
        if (id(table), copy_key) not in arrived:
            table[copy_key].wait_recv()
            arrived.add((id(table), copy_key))

    def pass_col_x(i):
        if ("fx", i) not in cross:
            for key in (("cx", 1),) if i else (("hx", 0), ("hx", 1)):
                need(key)
            cross_send(
                ("fx", i), cols_x.at[0, i], cols_x.at[1, i], col_x_recv, (1, i), sibling
            )

    def pass_col_y(k):
        need(("cy", k))
        cross_send(
            ("fy", k), cols_y.at[0, k], cols_y.at[1, k], col_y_recv, (1, k), sibling
        )

    def start_x(unit):
        left, right = UNITS[unit][0]
        n = left - 8
        sem = row_x_recv
        source = row_views(left).at[:, 1 - x, core]
        cross_send(("rx", n, 0), source, rows_x.at[0, n], sem, (0, n), x_mate)
        pass_col_x(right // 2)
        need(left, row_copies)
        cross_send(
            ("rx", n, 1), rows_sib.at[left, :, 1 - x], rows_x.at[1, n], sem, (1, n), x_mate
        )

    def product_x(unit):
        left, right = UNITS[unit][0]
        n, i = left - 8, right // 2
        need(right, col_copies)
        need(("fx", i))
        flat = (4 * PIECE, tokens)
        total = matmul(row_half(left, x), col_ref(right)[...])
        total += matmul(rows_sib[left, :, x].reshape(flat), cols_sib[right])
        for k in range(2):
            need(("rx", n, k))
            total += matmul(rows_x[k, n].reshape(flat), cols_x[k, i])
        total = total.astype(low).reshape(2, 2, PIECE, width)
        part[unit, 0, x] = total[..., :half_width]
        part[unit, 1, x] = total[..., half_width:]

    def start_y(unit):
        if ("ry", 0) not in cross:
            sem = row_y_recv
            cross_send(("ry", 0), rows.at[6, :, :, core], rows_y.at[0], sem, 0, y_mate)
            for k in range(4):
                pass_col_y(k)
            need(6, row_copies)
            cross_send(("ry", 1), rows_sib.at[6], rows_y.at[1], sem, 1, y_mate)

    def product_y(unit):
        left, right = UNITS[unit][0]
        k = right - 3
        need(right, col_copies)
        need(("fy", k))
        flat = (4 * PIECE, tokens)
        for i in range(2):
            need(("ry", i))
        for side in range(2):
            total = matmul(row_half(left, side), cols[2 + k, :, lanes_of[0]])
            total += matmul(
                rows_sib[left, :, side].reshape(flat), cols_sib[right, :, lanes_of[0]]
            )
            for i in range(2):
                total += matmul(rows_y[i, :, side].reshape(flat), cols_y[i, k])
            part[unit, y, side] = total.astype(low).reshape(2, 2, PIECE, half_width)

    axes = ("y", "x", "h", "l")
    recvs = (recv_one, recv_two, recv_three, recv_four)
    copies, last = {}, {}
    units = len(UNITS)

    def half(unit, side):
        total = None
        for left, right in UNITS[unit]:
            need(left, row_copies)
            need(right, col_copies)
            term = matmul(row_half(left, side), col_ref(right)[...])
            term += matmul(
                rows_sib[left, :, side].reshape(4 * PIECE, tokens), cols_sib[right]
            )
            total = term if total is None else total + term
        total = total.astype(low).reshape(2, 2, PIECE, width)
        part[unit, 0, side] = total[..., :half_width]
        part[unit, 1, side] = total[..., half_width:]

    def place(done, axis, index):
        fixed = {name: own[name] for name in done}
        fixed[axis] = index
        left = [name for name in axes if name not in done]
        inside = tuple(index if name == axis else slice(None) for name in left)
        return tuple(fixed.get(name, slice(None)) for name in axes), inside

    def landing(unit, stage):
        return WHOLE.index(unit) if stage == 0 else unit

    def push(unit, stage):
        order = ORDERS[unit]
        axis = order[stage]
        where, _ = place(order[:stage], axis, 1 - own[axis])
        copies[unit, stage] = send(
            part.at[(unit, *where)],
            recvs[stage].at[landing(unit, stage)],
            stage_recv.at[stage, unit],
            mates[axis],
        )

    def start(unit):
        if unit in CROSS_X:
            start_x(unit)
        elif unit in CROSS_Y:
            start_y(unit)
        elif ORDERS[unit][0] == "x":
            half(unit, 1 - x)
            push(unit, 0)
            half(unit, x)
        else:
            half(unit, 0)
            half(unit, 1)
            push(unit, 0)

    def add(unit, stage, axis, index):
        where, inside = place(ORDERS[unit][: stage + 1], axis, index)
        mine = part[(unit, *where)].astype(jnp.float32)
        part[(unit, *where)] = (mine + recvs[stage][(landing(unit, stage), *inside)].astype(jnp.float32)).astype(low)

    def advance(unit, stage):
        if stage == 0 and unit not in WHOLE:
            if unit in CROSS_X:
                product_x(unit)
            else:
                product_y(unit)
            push(unit, 1)
            return
        copies[unit, stage].wait_recv()
        axis = ORDERS[unit][stage + 1]
        add(unit, stage, axis, 1 - own[axis])
        push(unit, stage + 1)
        add(unit, stage, axis, own[axis])

    def close(unit):
        copies[unit, 3].wait_recv()
        total = part[(unit, *(own[name] for name in axes))].astype(jnp.float32)
        sums[unit, core] = (total + recv_four[unit].astype(jnp.float32)).astype(low)
        last[unit] = send(
            sums.at[unit, core],
            sums.at[unit, core],
            last_recv.at[unit],
            sibling,
        )

    step_rows = tokens

    def over_rows(body, init=0):
        return body(slice(None), 0, init)

    def over_pieces(body, init=0):
        for p in range(blocks):
            init = body(p, init)
        return init

    def spot(p):
        return p // 4, (p // 2) % 2, p % 2

    def put_t(index, value):
        rows[index] = value.reshape(4, 2, 2, PIECE, tokens)

    def get_t(index):
        return rows[index].reshape(width, tokens)

    def fold(value):
        return value.reshape(PIECE // 8, 8, tokens).sum(0)

    banks_in = (adapt_down, adapt_up)
    half_bank = width // 8
    far = flip(bn, 2)

    def bank_half(bank, side):
        return bank.at[pl.ds(pl.multiple_of(side * half_bank, half_bank), half_bank), :]

    bank_y, bank_x, bank_sib = [], [], [[], []]

    def send_bank(source, i, where, kind, mate):
        return send(
            source, banks.at[(i, *where)], bank_recv.at[i, kind], mate
        )

    def pass_from_y(i):
        bank_y[i].wait_recv()
        source = banks.at[i, far, x]
        bank_x.append(send_bank(source, i, (far, x), 3, x_mate))
        bank_sib[i].append(send_bank(source, i, (far, x), 4, sibling))

    def pass_from_x(i):
        bank_x[i].wait_recv()
        source = banks.at[i, far, 1 - x]
        bank_sib[i].append(send_bank(source, i, (far, 1 - x), 5, sibling))

    def open_links():
        pl.semaphore_wait(barrier, 1 + len(mates))
        for i in range(2):
            bank_y.append(send_bank(bank_half(banks_in[i], x), i, (bn, x), 0, y_mate))
        for i in range(2):
            for side in range(2):
                source = bank_half(banks_in[i], side)
                bank_sib[i].append(send_bank(source, i, (bn, side), 1 + side, sibling))
        share_col(0)
        half_hidden_over_x(0)

    length = lengths[0]
    for k in range(3):
        slot = take()
        value = matmul(hidden[...], ring[slot])
        release(slot)
        if k == 0:
            value = value * 0.125
        qkv_t[pl.ds(k * width, width), :] = value.astype(low).T
        if k == 0:
            open_links()
    size = width // heads

    def head_rows(k, head):
        return pl.ds(pl.multiple_of(k * width + head * size, size), size)

    valid_keys = lax.broadcasted_iota(jnp.int32, (tokens, tokens), 0) < length

    def head_forward(head, carry):
        scores = matmul_tn(qkv_t[head_rows(1, head), :], qkv_t[head_rows(0, head), :])
        scores = jnp.where(valid_keys, scores, masked_value)
        scores = jnp.exp(scores - jnp.max(scores, 0, keepdims=True))
        share = (scores * (1.0 / jnp.sum(scores, 0, keepdims=True))).astype(low)
        probs[head] = share
        context = matmul(qkv_t[head_rows(2, head), :], share)
        low_tmp_two[pl.ds(pl.multiple_of(head * size, size), size), :] = context.astype(low)
        return carry

    lax.fori_loop(0, heads, head_forward, 0, unroll=3)
    pass_from_y(0)
    cols[0] = low_tmp_two[...].T
    share_col(1)
    slot = take()
    acc[...] = matmul(cols[0], ring[slot])
    release(slot)

    def norm_rows(total):
        center = total - jnp.mean(total, -1, keepdims=True)
        rstd = lax.rsqrt(jnp.mean(center * center, -1, keepdims=True) + epsilon)
        return center * rstd, rstd

    def norm_first(r, i, carry):
        normed, rstd = norm_rows(hidden[r, :].astype(jnp.float32) + acc[r, :])
        stat[r, :] = jnp.broadcast_to(rstd, (step_rows, 128))
        low_tmp[r, :] = normed.astype(low)
        one_rows = normed * gain_attn
        wide[r, :] = one_rows
        cols[1, r, :] = one_rows.astype(low)
        return carry

    over_rows(norm_first)
    share_col(2)
    norm_one[...] = low_tmp[...].T.reshape(blocks, PIECE, tokens)
    stat_one[...] = stat[...].T[:8]

    for k in range(4):
        slot = take()
        acc[...] = matmul(cols[1], ring[slot])
        release(slot)
        unit_base = 2 + (k % 2) * 2
        lanes = lanes_of[1 - k // 2]

        def gelu_rows(r, i, carry):
            before = acc[r, :]
            cdf, density = normal_parts(before)
            act = (before * cdf).astype(low)
            low_tmp[r, :] = act
            cols[unit_base, r, lanes] = act[:, :half_width]
            cols[unit_base + 1, r, lanes] = act[:, half_width:]
            cols[9, r, :] = (cdf + before * density).astype(low)
            return carry

        over_rows(gelu_rows)
        slope[pl.ds(ff_blocks[k] * blocks, blocks)] = cols[9].T.reshape(blocks, PIECE, tokens)
        slot = take()
        value = matmul(low_tmp[...], ring[slot])
        release(slot)
        acc_two[...] = value if k == 0 else acc_two[...] + value
        if k == 0:
            pass_from_y(1)
            half_hidden_over_x(1)
            col_over_x(1)
        if k < 2:
            col_over_y(2 * k)
            col_over_y(2 * k + 1)
        if k == 2:
            pass_from_x(0)
    for index in range(3, 7):
        share_col(index)

    def norm_second(r, i, carry):
        normed, rstd = norm_rows(wide[r, :] + acc_two[r, :])
        stat[r, :] = jnp.broadcast_to(rstd, (step_rows, 128))
        low_tmp[r, :] = normed.astype(low)
        two_rows = normed * gain_ff
        wide[r, :] = two_rows
        cols[6, r, :] = two_rows.astype(low)
        return carry

    over_rows(norm_second)
    share_col(7)
    norm_two[...] = low_tmp[...].T.reshape(blocks, PIECE, tokens)
    stat_two[...] = stat[...].T[:8]
    put_t(3, cols[6].T)
    share_row(3)

    slot_query = take()
    low_tmp[...] = matmul(cols[6], ring[slot_query]).astype(low)
    put_t(4, low_tmp[...].T)
    share_row(4)
    slot_key = take()
    put_t(2, matmul(ring[slot_key], get_t(4)).astype(low))
    share_row(2)

    def bank_ready(i):
        for side in range(2):
            bank_own[2 * i + side].wait()
        for copy in bank_sib[i]:
            copy.wait_recv()

    bank_ready(0)
    acc_t[...] = matmul(banks[0].reshape(width, width), get_t(3)).reshape(blocks, PIECE, tokens)
    pass_from_x(1)
    bank_ready(1)
    acc_t_two[...] = matmul(banks[1].reshape(width, width), get_t(2)).reshape(
        blocks, PIECE, tokens
    )
    score_scale = 1.0 / math.sqrt(width)
    groups = PIECE // adapters

    def grouped(value):
        return value.reshape(groups, adapters, tokens)

    def adapter_rows(p, logits):
        inner = acc_t[p]
        cdf, density = normal_parts(inner)
        act = inner * cdf
        active[p] = act
        bank_slope[p] = (cdf + inner * density).astype(low)
        return logits + grouped(act * acc_t_two[p]).sum(0)

    logits = over_pieces(adapter_rows, jnp.zeros((adapters, tokens), jnp.float32)) * score_scale
    logits = jnp.exp(logits - jnp.max(logits, 0, keepdims=True))
    shares = logits / jnp.sum(logits, 0, keepdims=True)

    def spread(value):
        return jnp.concatenate([value] * groups, 0)

    wide_shares = spread(shares)

    def mixing_rows(p, carry):
        low_tmp_two[pl.ds(p * PIECE, PIECE), :] = (
            wide_shares * active[p]
        ).astype(low)
        return carry

    over_pieces(mixing_rows)
    cols[8] = low_tmp_two[...].T
    share_col(9)
    acc[...] = matmul(cols[8], banks[1].reshape(width, width))

    def joined_rows(r, i, carry):
        cols[7, r, :] = (wide[r, :] + acc[r, :]).astype(low)
        return carry

    over_rows(joined_rows)
    share_col(8)
    slot_value = take()
    acc[...] = matmul(cols[7], ring[slot_value])

    upstream_copy.wait()

    def norm_third(r, i, gain_part):
        normed, rstd = norm_rows(wide[r, :] + acc[r, :])
        gain = gain_out
        acc_two[r, :] = normed * gain
        token = lax.broadcasted_iota(jnp.int32, (step_rows, 1), 0) + i * step_rows
        upstream = jnp.where(token < length, cotangent[r, :].astype(jnp.float32), 0.0)
        product = upstream * normed
        gained = upstream * gain
        third = rstd * (
            gained
            - jnp.mean(gained, -1, keepdims=True)
            - normed * jnp.mean(gained * normed, -1, keepdims=True)
        )
        low_tmp[r, :] = third.astype(low)
        return gain_part + product.reshape(step_rows // 8, 8, width).sum(0)

    gain_part = over_rows(norm_third, jnp.zeros((8, width), jnp.float32))
    out_copy = pltpu.make_async_copy(acc_two, output, local_sem.at[0])
    out_copy.start()
    gain_sum[0] = jnp.broadcast_to(jnp.sum(gain_part, 0, keepdims=True), (8, width))
    put_t(0, low_tmp[...].T)
    share_row(0)

    state = {}

    def value_back():
        second[...] = matmul(ring[slot_value], get_t(0)).reshape(blocks, PIECE, tokens)
        release(slot_value)

        def mix_rows(p, carry):
            zz, xx, cc = spot(p)
            rows[1, zz, xx, cc] = second[p].astype(low)
            return carry

        over_pieces(mix_rows)
        share_row(1)
        acc_t[...] = matmul(banks[1].reshape(width, width), get_t(1)).reshape(blocks, PIECE, tokens)

    def adapter_grads():
        def share_rows(p, total):
            return total + grouped(acc_t[p] * active[p]).sum(0)

        share_grad = over_pieces(share_rows, jnp.zeros((adapters, tokens), jnp.float32))
        logit_grad = shares * (share_grad - jnp.sum(shares * share_grad, 0, keepdims=True))
        wide_logit = spread(logit_grad * score_scale)

        def adapter_back(p, carry):
            act_grad = acc_t[p] * wide_shares + wide_logit * acc_t_two[p]
            where = pl.ds(p * PIECE, PIECE)
            low_tmp_two[where, :] = (wide_logit * active[p]).astype(low)
            bank_slope[p] = (bank_slope[p].astype(jnp.float32) * act_grad).astype(low)
            return carry

        over_pieces(adapter_back)
        cols[9] = low_tmp_two[...].T
        share_col(10)
        cols[10] = bank_slope[...].reshape(width, tokens).T
        share_col(11)

    def probe_back():
        cols[11] = matmul(cols[9], banks[1].reshape(width, width)).astype(low)
        share_col(12)
        low_tmp[...] = matmul(cols[11], ring[slot_key]).astype(low)
        release(slot_key)
        put_t(5, low_tmp[...].T)
        share_row(5)
        low_tmp[...] = matmul(cols[10], banks[0].reshape(width, width)).astype(low)
        low_tmp_two[...] = low_tmp[...].T
        acc_t[...] = matmul(ring[slot_query], get_t(5)).reshape(blocks, PIECE, tokens)
        release(slot_query)

    def norm_back(index, gain, normed_ref, stat_ref, upstream_of, factor):
        gain_col[...] = jnp.broadcast_to(gain, (128, width)).T.reshape(blocks, PIECE, 128)

        def gained(p):
            column = gain_col[p]
            return acc_t[p] * jnp.concatenate([column] * (tokens // 128), 1)

        def first_pass(p, carry):
            upstream = upstream_of(p)
            acc_t[p] = upstream
            normed = normed_ref[p].astype(jnp.float32)
            gain_of = jnp.sum(upstream * normed, -1, keepdims=True)
            weighted = gained(p)
            gain_col[p] = jnp.broadcast_to(gain_of, (PIECE, 128))
            acc_t[p] = weighted
            return carry[0] + fold(weighted), carry[1] + fold(weighted * normed)

        zeros = jnp.zeros((8, tokens), jnp.float32)
        plain, tilted = over_pieces(first_pass, (zeros, zeros))
        mean_plain = jnp.sum(plain, 0, keepdims=True) * (1.0 / width)
        mean_tilted = jnp.sum(tilted, 0, keepdims=True) * (1.0 / width)
        rstd = stat_ref[0:1, :]

        def second_pass(p, carry):
            value = rstd * (acc_t[p] - mean_plain - normed_ref[p].astype(jnp.float32) * mean_tilted)
            second[p] = value
            zz, xx, cc = spot(p)
            rows[factor, zz, xx, cc] = value.astype(low)
            return carry

        over_pieces(second_pass)
        gain_sum[0, index : index + 1, :] = gain_col[...].reshape(width, 128).T[:1]

    def upstream_two(p):
        zz, xx, cc = spot(p)
        where = pl.ds(p * PIECE, PIECE)
        total = rows[0, zz, xx, cc].astype(jnp.float32) + second[p]
        return total + low_tmp_two[where, :].astype(jnp.float32) + acc_t[p]

    def norm_two_back():
        norm_back(1, gain_ff, norm_two, stat_two, upstream_two, 6)
        share_row(6)

    def ff_back(k):
        slot = take()
        acc_t_two[...] = matmul(ring[slot], get_t(6)).reshape(blocks, PIECE, tokens)
        release(slot)

        def slope_rows(p, carry):
            value = acc_t_two[p] * slope[k * blocks + p].astype(jnp.float32)
            rows_ff[k, p // 8, (p % 8) // 2, p % 2] = value.astype(low)
            return carry

        over_pieces(slope_rows)
        slot = take()
        value = matmul(ring[slot], rows_ff[k].reshape(width, tokens))
        value = value.reshape(blocks, PIECE, tokens)
        release(slot)
        acc_t[...] = value if k == 0 else acc_t[...] + value
        if k == 3:
            for index in range(8, 12):
                share_row(index)

    def upstream_one(p):
        return second[p] + acc_t[p]

    def norm_one_back():
        norm_back(0, gain_attn, norm_one, stat_one, upstream_one, 7)
        share_row(7)
        slot = take()
        low_tmp_two[...] = matmul(ring[slot], get_t(7)).astype(low)
        release(slot)

    heads_step = 3
    step_pieces = heads_step * size // PIECE

    def head_backward(group, carry):
        grads = [[], [], []]
        for i in range(heads_step):
            head = group * heads_step + i
            query, key, value = [qkv_t[head_rows(k, head), :] for k in range(3)]
            upstream = low_tmp_two[pl.ds(pl.multiple_of(head * size, size), size), :]
            share = probs[head]
            share_wide = share.astype(jnp.float32)
            prob_grad = matmul_tn(value, upstream)
            delta = jnp.sum(share_wide * prob_grad, 0, keepdims=True)
            score_grad = (share_wide * (prob_grad - delta)).astype(low)
            grads[0].append((matmul(key, score_grad) * 0.125).astype(low))
            grads[1].append(matmul_t(query, score_grad).astype(low))
            grads[2].append(matmul_t(upstream, share).astype(low))
        for k in range(3):
            stacked = jnp.concatenate(grads[k], 0).reshape(step_pieces, PIECE, tokens)
            for i in range(step_pieces):
                p = k * blocks + group * step_pieces + i
                rows_qkv[p // 12, (p // 6) % 2, (p % 6) // 2, p % 2] = stacked[i]
        return carry

    def attention_back():
        lax.fori_loop(0, heads // heads_step, head_backward, 0)
        for index in range(12, 15):
            share_row(index)

    def input_back():
        for k in range(3):
            slot = take()
            block = rows_qkv[...].reshape(3 * blocks, PIECE, tokens)[k * blocks : (k + 1) * blocks]
            value = matmul(ring[slot], block.reshape(width, tokens)).reshape(blocks, PIECE, tokens)
            release(slot)
            second[...] = second[...] + value
        acc[...] = second[...].reshape(width, tokens).T
        state["in"] = pltpu.make_async_copy(acc, grad_in, local_sem.at[1])
        state["in"].start()

    gain_mates = (sibling, x_mate, y_mate, mates["l"], mates["h"])

    def gain_step(stage):
        if stage > 0:
            state["gain"].wait_recv()
            total = gain_sum[stage - 1] + gain_from[stage - 1]
            if stage == 5:
                gain_sums[...] = total
                return
            gain_sum[stage] = total
        state["gain"] = send(
            gain_sum.at[stage],
            gain_from.at[stage],
            gain_recv.at[stage],
            gain_mates[stage],
        )

    chain = [value_back, adapter_grads, probe_back, norm_two_back]
    chain += [functools.partial(ff_back, k) for k in range(4)]
    chain += [norm_one_back, attention_back, input_back]
    progress = [0] * units
    since_chain, gain_stage = 0, 0
    for action in SEQUENCE:
        if action < 0:
            chain.pop(0)()
        elif progress[action] == 0:
            start(action)
        elif progress[action] < 4:
            advance(action, progress[action] - 1)
        else:
            close(action)
        if action >= 0:
            progress[action] += 1
        if not chain:
            if since_chain % 4 == 0 and gain_stage < 6:
                gain_step(gain_stage)
                gain_stage += 1
            since_chain += 1
    for stage in range(gain_stage, 6):
        gain_step(stage)
    for unit in range(units):
        last[unit].wait_recv()
    for copy in started[-SENDS:]:
        copy.wait_send()
    out_copy.wait()
    state["in"].wait()


def run_layer(heads, adapters, arrays):
    hidden = arrays[0]
    tokens, width = hidden.shape
    low, wide = jnp.bfloat16, jnp.float32
    blocks = width // PIECE
    units = len(UNITS)
    dma = pltpu.SemaphoreType.DMA
    vmem = pl.BlockSpec(memory_space=pltpu.VMEM)
    smem = pl.BlockSpec(memory_space=pltpu.SMEM)
    far = pl.BlockSpec(memory_space=pl.ANY)
    half_width = width // 2
    return pl.pallas_call(
        functools.partial(layer_kernel, heads, adapters),
        out_shape=(
            jax.ShapeDtypeStruct((tokens, width), wide),
            jax.ShapeDtypeStruct((tokens, width), wide),
            jax.ShapeDtypeStruct((units, 2, PIECE, half_width), low),
            jax.ShapeDtypeStruct((8, width), wide),
        ),
        in_specs=[
            vmem, smem, far, far, far, vmem, far, far, vmem, far, far, far, far, far, vmem,
        ],
        out_specs=[far, far, vmem, vmem],
        scratch_shapes=[
            pltpu.VMEM((8, 4, 2, 2, PIECE, tokens), low),
            pltpu.VMEM((4, 2, 4, 2, PIECE, tokens), low),
            pltpu.VMEM((4, 2, 3, 2, PIECE, tokens), low),
            pltpu.VMEM((15, 4, 2, PIECE, tokens), low),
            pltpu.VMEM((12, tokens, width), low),
            pltpu.VMEM((13, tokens, width), low),
            pltpu.VMEM((2, 7, 4, PIECE, tokens), low),
            pltpu.VMEM((2, 2, tokens, width), low),
            pltpu.VMEM((2, 4, 2, PIECE, tokens), low),
            pltpu.VMEM((2, 4, tokens, half_width), low),
            pltpu.VMEM((SLOTS, width, width), low),
            pltpu.VMEM((2, 4, 2, width // 8, width), low),
            pltpu.VMEM((tokens, width), wide),
            pltpu.VMEM((tokens, width), wide),
            pltpu.VMEM((tokens, width), wide),
            pltpu.VMEM((blocks, PIECE, tokens), wide),
            pltpu.VMEM((blocks, PIECE, tokens), wide),
            pltpu.VMEM((blocks, PIECE, tokens), wide),
            pltpu.VMEM((blocks, PIECE, tokens), low),
            pltpu.VMEM((blocks, PIECE, tokens), wide),
            pltpu.VMEM((blocks, PIECE, tokens), low),
            pltpu.VMEM((blocks, PIECE, tokens), low),
            pltpu.VMEM((4 * blocks, PIECE, tokens), low),
            pltpu.VMEM((3 * width, tokens), low),
            pltpu.VMEM((heads, tokens, tokens), low),
            pltpu.VMEM((tokens, width), low),
            pltpu.VMEM((width, tokens), low),
            pltpu.VMEM((tokens, 128), wide),
            pltpu.VMEM((8, tokens), wide),
            pltpu.VMEM((8, tokens), wide),
            pltpu.VMEM((blocks, PIECE, 128), wide),
            pltpu.VMEM((tokens, width), low),
            pltpu.VMEM((units, 2, 2, 2, 2, PIECE, half_width), low),
            pltpu.VMEM((len(WHOLE), 2, 2, 2, PIECE, half_width), low),
            pltpu.VMEM((units, 2, 2, PIECE, half_width), low),
            pltpu.VMEM((units, 2, PIECE, half_width), low),
            pltpu.VMEM((units, PIECE, half_width), low),
            pltpu.VMEM((5, 8, width), wide),
            pltpu.VMEM((5, 8, width), wide),
            dma((SLOTS,)),
            dma((7,)),
            dma((SENDS,)),
            dma((2, 6)),
            dma((15,)),
            dma((13,)),
            dma((2, 7)),
            dma((2, 2)),
            dma((2,)),
            dma((2,)),
            dma((2, 4)),
            dma((4, units)),
            dma((units,)),
            dma((5,)),
        ],
        compiler_params=pltpu.CompilerParams(
            collective_id=0, has_side_effects=True, vmem_limit_bytes=63 * 2**20
        ),
    )(*arrays)


def finish_kernel(
    sums_far,
    gain_sums_far,
    output,
    grad_in,
    out_output,
    out_grad_in,
    out_qkv,
    out_proj,
    out_gain_attn,
    out_ff_in,
    out_ff_out,
    out_gain_ff,
    out_query,
    out_key,
    out_value,
    out_down,
    out_up,
    out_gain_out,
    turned,
    sums,
    gain_sums,
    held,
    copy_sem,
):
    fetched = [
        pltpu.make_async_copy(sums_far, sums, copy_sem.at[2]),
        pltpu.make_async_copy(gain_sums_far, gain_sums, copy_sem.at[3]),
    ]
    through = [
        pltpu.make_async_copy(output, held.at[0], copy_sem.at[0]),
        pltpu.make_async_copy(grad_in, held.at[1], copy_sem.at[1]),
    ]
    for copy in fetched + through:
        copy.start()
    for copy in fetched:
        copy.wait()
    ad = lax.axis_index("ad")
    core = lax.axis_index("bn") % 2
    width = sums.shape[3]
    own = pl.ds(pl.multiple_of(core * (width // 2), width // 2), width // 2)

    def columns(out, slot, first, count):
        value = sums[first : first + count].reshape(count * 2 * PIECE, width)
        extent = pl.ds(0, count * 2 * PIECE)
        turned[slot, :, extent] = value.astype(jnp.float32).T
        out[...] = turned[slot, own, extent]

    columns(out_value, 0, 0, 1)
    columns(out_up, 1, 1, 1)
    columns(out_down, 2, 2, 1)
    columns(out_key, 0, 3, 1)
    columns(out_query, 1, 4, 1)
    for copy in through:
        copy.wait()
    passed = [
        pltpu.make_async_copy(held.at[0], out_output, copy_sem.at[0]),
        pltpu.make_async_copy(held.at[1], out_grad_in, copy_sem.at[1]),
    ]
    for copy in passed:
        copy.start()
    columns(out_ff_in, 2, 9, 4)
    columns(out_proj, 0, 13, 1)
    columns(out_qkv, 1, 14, 3)
    for i in range(2):
        value = sums[5 + 2 * core + i].reshape(2 * PIECE, width)
        out_ff_out[:, pl.ds(i * width, width)] = value.astype(jnp.float32)
    total = gain_sums.shape[1]
    piece = out_gain_attn.shape[0]
    rolled = pltpu.roll(gain_sums[...], lax.rem(total - ad * piece, total), 1)[:, :piece]
    for index, out in enumerate((out_gain_attn, out_gain_ff, out_gain_out)):
        out[...] = rolled[index : index + 1].reshape(piece)
    for copy in passed:
        copy.wait()


def finish(sums, gain_sums, output, grad_in, width):
    quarter, eighth = width // 4, width // 8
    far = pl.BlockSpec(memory_space=pl.ANY)
    shapes = [
        output.shape,
        grad_in.shape,
        (quarter, 3 * eighth),
        (quarter, eighth),
        (eighth,),
        (quarter, 4 * eighth),
        (eighth, 4 * quarter),
        (eighth,),
    ]
    shapes += [(quarter, eighth)] * 5 + [(eighth,)]
    return pl.pallas_call(
        finish_kernel,
        out_shape=tuple(jax.ShapeDtypeStruct(shape, jnp.float32) for shape in shapes),
        in_specs=[far] * 4,
        out_specs=[far] * 2 + [pl.BlockSpec(memory_space=pltpu.VMEM)] * 12,
        scratch_shapes=[
            pltpu.VMEM((3, width // 2, 4 * eighth), jnp.float32),
            pltpu.VMEM(sums.shape, sums.dtype),
            pltpu.VMEM(gain_sums.shape, gain_sums.dtype),
            pltpu.VMEM((2, *output.shape), output.dtype),
            pltpu.SemaphoreType.DMA((4,)),
        ],
        compiler_params=pltpu.CompilerParams(vmem_limit_bytes=62 * 2**20),
    )(sums, gain_sums, output, grad_in)


def fast_local(*arrays):
    arrays = list(arrays)
    width = arrays[0].shape[1]
    adapters = arrays[12].shape[1]
    bank_shape = arrays[12].shape[:2] + (-1,)
    for i in (12, 13):
        arrays[i] = arrays[i].reshape(-1, width)
    output, grad_in, sums, gain_sums = run_layer(H, adapters, arrays)
    results = list(finish(sums, gain_sums, output, grad_in, width))
    results[6] = results[6].T
    for i in (11, 12):
        results[i] = results[i].reshape(bank_shape)
    return tuple(results)


def local(
    hidden_in,
    lengths,
    cotangent,
    w_qkv,
    w_out,
    gain_attn,
    w_ff_in,
    w_ff_out,
    gain_ff,
    join_query,
    join_key,
    join_value,
    adapt_down,
    adapt_up,
    gain_out,
):
    seq_count = lengths.shape[0]
    tok_rows, model_width = hidden_in.shape
    slot_len = tok_rows // seq_count
    head_count = H
    head_size = model_width // head_count
    score_scale = 1.0 / math.sqrt(head_size)
    adapters = adapt_down.shape[1]
    down_flat = lax.all_gather(adapt_down.reshape(-1, model_width), "bn", axis=0, tiled=True)
    up_flat = lax.all_gather(adapt_up.reshape(-1, model_width), "bn", axis=0, tiled=True)
    valid = lax.broadcasted_iota(jnp.int32, (seq_count, slot_len), 1) < lengths[:, None]
    row_ok = valid.reshape(tok_rows, 1).astype(jnp.float32)
    tokens_wide = hidden_in.astype(jnp.float32)
    qkv = matmul(hidden_in, w_qkv).astype(jnp.bfloat16)
    queries = qkv[:, :model_width].reshape(seq_count, slot_len, head_count, head_size)
    key_rows = qkv[:, model_width : 2 * model_width].reshape(
        seq_count, slot_len, head_count, head_size
    )
    values = qkv[:, 2 * model_width :].reshape(seq_count, slot_len, head_count, head_size)

    def attend_scores():
        raw_scores = (
            jnp.einsum("sqhe,skhe->shqk", queries, key_rows, preferred_element_type=jnp.float32)
            * score_scale
        )
        return jnp.where(valid[:, None, None, :], raw_scores, masked_value)

    scores = attend_scores()
    row_max = jnp.max(scores, -1, keepdims=True)
    log_total = row_max + jnp.log(jnp.sum(jnp.exp(scores - row_max), -1, keepdims=True))
    probs = jnp.exp(scores - log_total).astype(jnp.bfloat16)
    context = (
        jnp.einsum("shqk,skhe->sqhe", probs, values, preferred_element_type=jnp.float32)
        .reshape(tok_rows, model_width)
        .astype(jnp.bfloat16)
    )
    attn_out = matmul(context, w_out)
    hidden_one, norm_one_back = jax.vjp(layer_norm, tokens_wide + attn_out, gain_attn)
    hidden_one_low = hidden_one.astype(jnp.bfloat16)
    ff_pre = matmul(hidden_one_low, w_ff_in)
    ff_act, gelu_ff_back = jax.vjp(gelu_exact, ff_pre)
    ff_low = ff_act.astype(jnp.bfloat16)
    ff_out = matmul(ff_low, w_ff_out)
    hidden_two, norm_two_back = jax.vjp(layer_norm, hidden_one + ff_out, gain_ff)
    hidden_low = hidden_two.astype(jnp.bfloat16)
    query_join = matmul(hidden_low, join_query).astype(jnp.bfloat16)
    probe = matmul_t(query_join, join_key).astype(jnp.bfloat16)
    mixing, kept_state = adapter_forward(hidden_low, probe, down_flat, up_flat, adapters)
    joined_in = (hidden_two + matmul(mixing, up_flat)).astype(jnp.bfloat16)
    joined = matmul(joined_in, join_value)
    output, norm_out_back = jax.vjp(layer_norm, hidden_two + joined, gain_out)
    out_grad = cotangent.astype(jnp.float32) * row_ok
    sum_three, gain_out_grad = norm_out_back(out_grad)
    joined_grad = sum_three.astype(jnp.bfloat16)
    into_joined = matmul_t(joined_grad, join_value)
    mix_grad = into_joined.astype(jnp.bfloat16)
    inner_grad, weigh_grad = adapter_backward(kept_state, up_flat, mix_grad, adapters)
    hidden_back = matmul(inner_grad, down_flat)
    probe_grad = matmul(weigh_grad, up_flat).astype(jnp.bfloat16)
    query_in = matmul(probe_grad, join_key).astype(jnp.bfloat16)
    grad_two = sum_three + into_joined + hidden_back + matmul_t(query_in, join_query)
    sum_two, gain_ff_grad = norm_two_back(grad_two)
    ff_out_grad = sum_two.astype(jnp.bfloat16)
    ff_pre_grad = gelu_ff_back(matmul_t(ff_out_grad, w_ff_out))[0].astype(jnp.bfloat16)
    grad_one = sum_two + matmul_t(ff_pre_grad, w_ff_in)
    sum_one, gain_attn_grad = norm_one_back(grad_one)
    attn_grad = sum_one.astype(jnp.bfloat16)
    context_grad = (
        matmul_t(attn_grad, w_out)
        .astype(jnp.bfloat16)
        .reshape(seq_count, slot_len, head_count, head_size)
    )
    probs_wide = jnp.exp(attend_scores() - log_total)
    prob_grad = jnp.einsum(
        "sqhe,skhe->shqk", context_grad, values, preferred_element_type=jnp.float32
    )
    row_delta = jnp.sum(probs_wide * prob_grad, -1, keepdims=True)
    score_grad = (probs_wide * (prob_grad - row_delta)).astype(jnp.bfloat16)
    query_back = (
        jnp.einsum("shqk,skhe->sqhe", score_grad, key_rows, preferred_element_type=jnp.float32)
        * score_scale
    )
    key_back = (
        jnp.einsum("shqk,sqhe->skhe", score_grad, queries, preferred_element_type=jnp.float32)
        * score_scale
    )
    value_back = jnp.einsum(
        "shqk,sqhe->skhe", probs, context_grad, preferred_element_type=jnp.float32
    )
    qkv_grad = jnp.concatenate(
        [
            query_back.reshape(tok_rows, model_width),
            key_back.reshape(tok_rows, model_width),
            value_back.reshape(tok_rows, model_width),
        ],
        1,
    ).astype(jnp.bfloat16)
    grad_in = sum_one + matmul_t(qkv_grad, w_qkv)
    def shared_sum(gradient):
        columns = lax.psum_scatter(gradient, "ad", scatter_dimension=1, tiled=True)
        return lax.psum_scatter(
            columns.astype(jnp.bfloat16), "bn", scatter_dimension=0, tiled=True
        ).astype(jnp.float32)

    gains = lax.psum(
        lax.psum_scatter(
            jnp.stack([gain_attn_grad, gain_ff_grad, gain_out_grad]),
            "ad",
            scatter_dimension=1,
            tiled=True,
        ),
        "bn",
    )
    down_grad = shared_sum(matmul_tn(inner_grad, hidden_low))
    up_grad = shared_sum(matmul_tn(mixing, mix_grad) + matmul_tn(weigh_grad, probe))
    bank = adapt_down.shape[:2] + (-1,)
    return (
        output,
        grad_in,
        shared_sum(matmul_tn(hidden_in, qkv_grad)),
        shared_sum(matmul_tn(context, attn_grad)),
        gains[0],
        shared_sum(matmul_tn(hidden_one_low, ff_pre_grad)),
        shared_sum(matmul_tn(ff_low, ff_out_grad)),
        gains[1],
        shared_sum(matmul_tn(hidden_low, query_in)),
        shared_sum(matmul_tn(probe_grad, query_join)),
        shared_sum(matmul_tn(joined_in, joined_grad)),
        down_grad.reshape(bank),
        up_grad.reshape(bank),
        gains[2],
    )


def solution(mesh):
    placed = (
        P(("ad", "bn"), None),
        P(("ad", "bn")),
        P(("ad", "bn"), None),
        P(),
        P(),
        P(),
        P(),
        P(),
        P(),
        P(),
        P(),
        P(),
        P("bn", None, None),
        P("bn", None, None),
        P(),
    )
    sizes = (mesh.shape["ad"], mesh.shape["bn"])
    return jax.shard_map(
        fast_local if sizes == (8, 4) else local,
        mesh=mesh,
        in_specs=placed,
        out_specs=(
            P(("ad", "bn"), None),
            P(("ad", "bn"), None),
            P("bn", "ad"),
            P("bn", "ad"),
            P("ad"),
            P("bn", "ad"),
            P("bn", "ad"),
            P("ad"),
            P("bn", "ad"),
            P("bn", "ad"),
            P("bn", "ad"),
            P("bn", None, "ad"),
            P("bn", None, "ad"),
            P("ad"),
        ),
        check_vma=False,
    )
```

```python
import functools
import math

import jax
import jax.numpy as jnp
from jax import lax
from jax.experimental import pallas as pl
from jax.experimental.pallas import tpu as pltpu
from jax.sharding import PartitionSpec as P

H = 12


epsilon = 1e-06
masked_value = -1000000000.0
MESH = pl.DeviceIdType.MESH


def layer_norm(values, gain):
    center = values - jnp.mean(values, -1, keepdims=True)
    spread = jnp.mean(center * center, -1, keepdims=True)
    return center * lax.rsqrt(spread + epsilon) * gain


def gelu_exact(values):
    return jax.nn.gelu(values, approximate=False)


def matmul(left, right):
    return jnp.dot(left, right, preferred_element_type=jnp.float32)


def matmul_t(left, right):
    return lax.dot_general(
        left, right, (((1,), (1,)), ((), ())), preferred_element_type=jnp.float32
    )


def matmul_tn(left, right):
    return lax.dot_general(
        left, right, (((0,), (0,)), ((), ())), preferred_element_type=jnp.float32
    )


def adapter_forward(hidden, probe_rows, down_flat, up_flat, adapters):
    row_count, model_width = hidden.shape
    inner_pre = matmul_t(hidden, down_flat)
    active = gelu_exact(inner_pre)
    weigh_rows = matmul_t(probe_rows, up_flat)
    logits = jnp.sum((active * weigh_rows).reshape(row_count, -1, adapters), 1) / math.sqrt(
        model_width
    )
    shares = jax.nn.softmax(logits, -1)
    mixing = (
        (shares[:, None, :] * active.reshape(row_count, -1, adapters))
        .reshape(row_count, -1)
        .astype(jnp.bfloat16)
    )
    return (mixing, (inner_pre, active, weigh_rows, shares))


def adapter_backward(kept_state, up_flat, mix_grad, adapters):
    inner_pre, active, weigh_rows, shares = kept_state
    row_count, model_width = mix_grad.shape
    score_scale = 1.0 / math.sqrt(model_width)
    mix_in = matmul_t(mix_grad, up_flat).reshape(row_count, -1, adapters)
    active_three = active.reshape(row_count, -1, adapters)
    weigh_three = weigh_rows.reshape(row_count, -1, adapters)
    share_grad = jnp.sum(mix_in * active_three, 1)
    logit_grad = shares * (share_grad - jnp.sum(shares * share_grad, -1, keepdims=True))
    act_grad = mix_in * shares[:, None, :] + logit_grad[:, None, :] * score_scale * weigh_three
    weigh_grad = (
        (logit_grad[:, None, :] * score_scale * active_three)
        .reshape(row_count, -1)
        .astype(jnp.bfloat16)
    )
    unused, gelu_back = jax.vjp(gelu_exact, inner_pre)
    inner_grad = gelu_back(act_grad.reshape(row_count, -1))[0].astype(jnp.bfloat16)
    return (inner_grad, weigh_grad)


PIECE = 48
SLOTS = 5
SENDS = 48
UNITS = (
    ((0, 8),),
    ((1, 9), (2, 10)),
    ((3, 11),),
    ((4, 12),),
    ((5, 7),),
    ((6, 3),),
    ((6, 4),),
    ((6, 5),),
    ((6, 6),),
    ((8, 2),),
    ((9, 2),),
    ((10, 2),),
    ((11, 2),),
    ((7, 1),),
    ((12, 0),),
    ((13, 0),),
    ((14, 0),),
)


CROSS_X = (9, 10, 11, 12, 14, 15, 16)
CROSS_Y = (5, 6, 7, 8)
WHOLE = tuple(unit for unit in range(len(UNITS)) if unit not in CROSS_X + CROSS_Y)
ORDERS = (
    ("l", "y", "x", "h"),
    ("y", "l", "x", "h"),
    ("l", "y", "x", "h"),
    ("x", "l", "y", "h"),
    ("l", "x", "y", "h"),
    ("y", "l", "x", "h"),
    ("y", "l", "x", "h"),
    ("y", "x", "l", "h"),
    ("y", "x", "l", "h"),
    ("x", "y", "l", "h"),
    ("x", "l", "y", "h"),
    ("x", "y", "l", "h"),
    ("x", "y", "l", "h"),
    ("y", "l", "x", "h"),
    ("x", "y", "l", "h"),
    ("x", "y", "l", "h"),
    ("x", "y", "l", "h"),
)
SEQUENCE = (
    -1, -1, -1, 0, 1, -1, 3, 2, -1, 6, 7, 5, 8, -1, -1, -1, 4, -1, 9, 12, -1, 0, 11, -1,
    1, 9, 16, 3, 13, 6, 14, 5, 10, 12, 9, 3, 15, 16, 13, 11, 1, 12, 9, 6, 14, 3, 10, 0,
    13, 2, 16, 12, 5, 9, 3, 7, 15, 1, 11, 6, 4, 10, 0, 14, 16, 12, 13, 1, 8, 5, 11, 6,
    0, 2, 7, 15, 14, 16, 10, 13, 5, 4, 11, 7, 8, 15, 4, 14, 2, 10, 7, 8, 15, 4, 2, 8,
)

def flip(index, bit):
    return index + bit - 2 * bit * ((index // bit) % 2)


def normal_parts(values):
    cdf = 0.5 * (1.0 + lax.erf(values * (1.0 / math.sqrt(2.0))))
    density = jnp.exp(values * values * -0.5) * (1.0 / math.sqrt(2.0 * math.pi))
    return cdf, density


def layer_kernel(
    heads,
    adapters,
    hidden,
    lengths,
    cotangent_far,
    w_qkv,
    w_out,
    gain_attn,
    w_ff_in,
    w_ff_out,
    gain_ff,
    join_query,
    join_key,
    join_value,
    adapt_down,
    adapt_up,
    gain_out,
    output,
    grad_in,
    sums,
    gain_sums,
    rows,
    rows_ff,
    rows_qkv,
    rows_sib,
    cols,
    cols_sib,
    rows_x,
    cols_x,
    rows_y,
    cols_y,
    ring,
    banks,
    acc,
    acc_two,
    wide,
    acc_t,
    acc_t_two,
    active,
    bank_slope,
    second,
    norm_one,
    norm_two,
    slope,
    qkv_t,
    probs,
    low_tmp,
    low_tmp_two,
    stat,
    stat_one,
    stat_two,
    gain_col,
    cotangent,
    part,
    recv_one,
    recv_two,
    recv_three,
    recv_four,
    gain_sum,
    gain_from,
    ring_sem,
    local_sem,
    send_sem,
    bank_recv,
    row_recv,
    col_recv,
    row_x_recv,
    col_x_recv,
    hidden_x_recv,
    row_y_recv,
    col_y_recv,
    stage_recv,
    last_recv,
    gain_recv,
):
    low = jnp.bfloat16
    tokens, width = hidden.shape
    half_width = width // 2
    gain_attn, gain_ff, gain_out = [
        gain[...].reshape(1, width) for gain in (gain_attn, gain_ff, gain_out)
    ]
    blocks = rows.shape[1] * rows.shape[2] * rows.shape[3]
    ad = lax.axis_index("ad")
    bn = lax.axis_index("bn")
    x, z = ad % 2, ad // 2
    core, y = bn % 2, bn // 2
    sibling = (ad, flip(bn, 1))
    x_mate = (flip(ad, 1), bn)
    y_mate = (ad, flip(bn, 2))
    own = {"y": y, "x": x, "h": z // 2, "l": z % 2}
    mates = {"y": y_mate, "x": x_mate, "h": (flip(ad, 4), bn), "l": (flip(ad, 2), bn)}
    other_core = 1 - core

    loads = [(w_qkv.at[:, pl.ds(k * width, width)]) for k in range(3)] + [w_out]
    ff_blocks = [2 * (1 - y), 2 * (1 - y) + 1, 2 * y, 2 * y + 1]
    for block in ff_blocks:
        where = pl.ds(pl.multiple_of(block * width, width), width)
        loads.append(w_ff_in.at[:, where])
        loads.append(w_ff_out.at[where, :])
    loads += [join_query, join_key, join_value]
    for k in range(4):
        loads.append(w_ff_out.at[pl.ds(k * width, width), :])
        loads.append(w_ff_in.at[:, pl.ds(k * width, width)])
    loads += [w_out] + [w_qkv.at[:, pl.ds(k * width, width)] for k in range(3)]
    free_slots = list(range(SLOTS))
    in_flight = []
    next_load = [0]

    def fill():
        while free_slots and next_load[0] < len(loads):
            slot = free_slots.pop(0)
            copy = pltpu.make_async_copy(loads[next_load[0]], ring.at[slot], ring_sem.at[slot])
            copy.start()
            in_flight.append((slot, copy))
            next_load[0] += 1

    def take():
        slot, copy = in_flight.pop(0)
        copy.wait()
        return slot

    def release(slot):
        free_slots.append(slot)
        fill()

    fill()
    upstream_copy = pltpu.make_async_copy(cotangent_far, cotangent, local_sem.at[6])
    upstream_copy.start()
    bank_own = []
    for i, bank in enumerate((adapt_down, adapt_up)):
        for side in range(2):
            bank_own.append(
                pltpu.make_async_copy(
                    bank.at[pl.ds(side * (width // 8), width // 8), :],
                    banks.at[i, bn, side],
                    local_sem.at[2 + 2 * i + side],
                )
            )
            bank_own[-1].start()

    barrier = pltpu.get_barrier_semaphore()
    for mate in [sibling, *mates.values()]:
        pl.semaphore_signal(barrier, inc=1, device_id=mate, device_id_type=MESH)

    started = []

    def send(source, target, recv_sem, mate):
        slot = len(started) % SENDS
        if len(started) >= SENDS:
            started[-SENDS].wait_send()
        copy = pltpu.make_async_remote_copy(
            src_ref=source,
            dst_ref=target,
            send_sem=send_sem.at[slot],
            recv_sem=recv_sem,
            device_id=mate,
            device_id_type=MESH,
        )
        copy.start()
        started.append(copy)
        return copy

    def row_views(index):
        if index < 8:
            return rows.at[index]
        if index < 12:
            return rows_ff.at[:, :, index - 8]
        return rows_qkv.at[:, :, index - 12]

    def row_half(index, side):
        if index < 8:
            piece = rows[index, :, side, core]
        elif index < 12:
            piece = rows_ff[:, side, index - 8, core]
        else:
            piece = rows_qkv[:, side, index - 12, core]
        return piece.reshape(4 * PIECE, tokens)

    def col_ref(index):
        return hidden if index == 0 else cols.at[index - 1]

    row_copies, col_copies = {}, {}
    arrived = set()

    def share_row(index):
        row_copies[index] = send(
            row_views(index).at[:, :, other_core],
            rows_sib.at[index],
            row_recv.at[index],
            sibling,
        )

    def share_col(index):
        col_copies[index] = send(
            col_ref(index),
            cols_sib.at[index],
            col_recv.at[index],
            sibling,
        )

    cross = {}
    lanes_of = [
        pl.ds(pl.multiple_of(side * half_width, half_width), half_width) for side in (y, 1 - y)
    ]

    def cross_send(key, source, target, sem, index, mate):
        cross[key] = send(source, target, sem.at[index], mate)

    def col_over_x(i):
        cross_send(("cx", i), col_ref(2 * i), cols_x.at[0, i], col_x_recv, (0, i), x_mate)

    def half_hidden_over_x(side):
        where = pl.ds(side * (tokens // 2), tokens // 2)
        cross_send(
            ("hx", side), hidden.at[where], cols_x.at[0, 0, where], hidden_x_recv, side, x_mate
        )

    def col_over_y(k):
        source = cols.at[2 + k, :, lanes_of[1]]
        cross_send(("cy", k), source, cols_y.at[0, k], col_y_recv, (0, k), y_mate)

    def need(copy_key, table=cross):
        if (id(table), copy_key) not in arrived:
            table[copy_key].wait_recv()
            arrived.add((id(table), copy_key))

    def pass_col_x(i):
        if ("fx", i) not in cross:
            for key in (("cx", 1),) if i else (("hx", 0), ("hx", 1)):
                need(key)
            cross_send(
                ("fx", i), cols_x.at[0, i], cols_x.at[1, i], col_x_recv, (1, i), sibling
            )

    def pass_col_y(k):
        need(("cy", k))
        cross_send(
            ("fy", k), cols_y.at[0, k], cols_y.at[1, k], col_y_recv, (1, k), sibling
        )

    def start_x(unit):
        left, right = UNITS[unit][0]
        n = left - 8
        sem = row_x_recv
        source = row_views(left).at[:, 1 - x, core]
        cross_send(("rx", n, 0), source, rows_x.at[0, n], sem, (0, n), x_mate)
        pass_col_x(right // 2)
        need(left, row_copies)
        cross_send(
            ("rx", n, 1), rows_sib.at[left, :, 1 - x], rows_x.at[1, n], sem, (1, n), x_mate
        )

    def product_x(unit):
        left, right = UNITS[unit][0]
        n, i = left - 8, right // 2
        need(right, col_copies)
        need(("fx", i))
        flat = (4 * PIECE, tokens)
        total = matmul(row_half(left, x), col_ref(right)[...])
        total += matmul(rows_sib[left, :, x].reshape(flat), cols_sib[right])
        for k in range(2):
            need(("rx", n, k))
            total += matmul(rows_x[k, n].reshape(flat), cols_x[k, i])
        total = total.astype(low).reshape(2, 2, PIECE, width)
        part[unit, 0, x] = total[..., :half_width]
        part[unit, 1, x] = total[..., half_width:]

    def start_y(unit):
        if ("ry", 0) not in cross:
            sem = row_y_recv
            cross_send(("ry", 0), rows.at[6, :, :, core], rows_y.at[0], sem, 0, y_mate)
            for k in range(4):
                pass_col_y(k)
            need(6, row_copies)
            cross_send(("ry", 1), rows_sib.at[6], rows_y.at[1], sem, 1, y_mate)

    def product_y(unit):
        left, right = UNITS[unit][0]
        k = right - 3
        need(right, col_copies)
        need(("fy", k))
        flat = (4 * PIECE, tokens)
        for i in range(2):
            need(("ry", i))
        for side in range(2):
            total = matmul(row_half(left, side), cols[2 + k, :, lanes_of[0]])
            total += matmul(
                rows_sib[left, :, side].reshape(flat), cols_sib[right, :, lanes_of[0]]
            )
            for i in range(2):
                total += matmul(rows_y[i, :, side].reshape(flat), cols_y[i, k])
            part[unit, y, side] = total.astype(low).reshape(2, 2, PIECE, half_width)

    axes = ("y", "x", "h", "l")
    recvs = (recv_one, recv_two, recv_three, recv_four)
    copies, last = {}, {}
    units = len(UNITS)

    def half(unit, side):
        total = None
        for left, right in UNITS[unit]:
            need(left, row_copies)
            need(right, col_copies)
            term = matmul(row_half(left, side), col_ref(right)[...])
            term += matmul(
                rows_sib[left, :, side].reshape(4 * PIECE, tokens), cols_sib[right]
            )
            total = term if total is None else total + term
        total = total.astype(low).reshape(2, 2, PIECE, width)
        part[unit, 0, side] = total[..., :half_width]
        part[unit, 1, side] = total[..., half_width:]

    def place(done, axis, index):
        fixed = {name: own[name] for name in done}
        fixed[axis] = index
        left = [name for name in axes if name not in done]
        inside = tuple(index if name == axis else slice(None) for name in left)
        return tuple(fixed.get(name, slice(None)) for name in axes), inside

    def landing(unit, stage):
        return WHOLE.index(unit) if stage == 0 else unit

    def push(unit, stage):
        order = ORDERS[unit]
        axis = order[stage]
        where, _ = place(order[:stage], axis, 1 - own[axis])
        copies[unit, stage] = send(
            part.at[(unit, *where)],
            recvs[stage].at[landing(unit, stage)],
            stage_recv.at[stage, unit],
            mates[axis],
        )

    def start(unit):
        if unit in CROSS_X:
            start_x(unit)
        elif unit in CROSS_Y:
            start_y(unit)
        elif ORDERS[unit][0] == "x":
            half(unit, 1 - x)
            push(unit, 0)
            half(unit, x)
        else:
            half(unit, 0)
            half(unit, 1)
            push(unit, 0)

    def add(unit, stage, axis, index):
        where, inside = place(ORDERS[unit][: stage + 1], axis, index)
        mine = part[(unit, *where)].astype(jnp.float32)
        part[(unit, *where)] = (mine + recvs[stage][(landing(unit, stage), *inside)].astype(jnp.float32)).astype(low)

    def advance(unit, stage):
        if stage == 0 and unit not in WHOLE:
            if unit in CROSS_X:
                product_x(unit)
            else:
                product_y(unit)
            push(unit, 1)
            return
        copies[unit, stage].wait_recv()
        axis = ORDERS[unit][stage + 1]
        add(unit, stage, axis, 1 - own[axis])
        push(unit, stage + 1)
        add(unit, stage, axis, own[axis])

    def close(unit):
        copies[unit, 3].wait_recv()
        total = part[(unit, *(own[name] for name in axes))].astype(jnp.float32)
        sums[unit, core] = (total + recv_four[unit].astype(jnp.float32)).astype(low)
        last[unit] = send(
            sums.at[unit, core],
            sums.at[unit, core],
            last_recv.at[unit],
            sibling,
        )

    step_rows = tokens

    def over_rows(body, init=0):
        return body(slice(None), 0, init)

    def over_pieces(body, init=0):
        for p in range(blocks):
            init = body(p, init)
        return init

    def spot(p):
        return p // 4, (p // 2) % 2, p % 2

    def put_t(index, value):
        rows[index] = value.reshape(4, 2, 2, PIECE, tokens)

    def get_t(index):
        return rows[index].reshape(width, tokens)

    def fold(value):
        return value.reshape(PIECE // 8, 8, tokens).sum(0)

    banks_in = (adapt_down, adapt_up)
    half_bank = width // 8
    far = flip(bn, 2)

    def bank_half(bank, side):
        return bank.at[pl.ds(pl.multiple_of(side * half_bank, half_bank), half_bank), :]

    bank_y, bank_x, bank_sib = [], [], [[], []]

    def send_bank(source, i, where, kind, mate):
        return send(
            source, banks.at[(i, *where)], bank_recv.at[i, kind], mate
        )

    def pass_from_y(i):
        bank_y[i].wait_recv()
        source = banks.at[i, far, x]
        bank_x.append(send_bank(source, i, (far, x), 3, x_mate))
        bank_sib[i].append(send_bank(source, i, (far, x), 4, sibling))

    def pass_from_x(i):
        bank_x[i].wait_recv()
        source = banks.at[i, far, 1 - x]
        bank_sib[i].append(send_bank(source, i, (far, 1 - x), 5, sibling))

    def open_links():
        pl.semaphore_wait(barrier, 1 + len(mates))
        for i in range(2):
            bank_y.append(send_bank(bank_half(banks_in[i], x), i, (bn, x), 0, y_mate))
        for i in range(2):
            for side in range(2):
                source = bank_half(banks_in[i], side)
                bank_sib[i].append(send_bank(source, i, (bn, side), 1 + side, sibling))
        share_col(0)
        half_hidden_over_x(0)

    length = lengths[0]
    for k in range(3):
        slot = take()
        value = matmul(hidden[...], ring[slot])
        release(slot)
        if k == 0:
            value = value * 0.125
        qkv_t[pl.ds(k * width, width), :] = value.astype(low).T
        if k == 0:
            open_links()
    size = width // heads

    def head_rows(k, head):
        return pl.ds(pl.multiple_of(k * width + head * size, size), size)

    valid_keys = lax.broadcasted_iota(jnp.int32, (tokens, tokens), 0) < length

    def head_forward(head, carry):
        scores = matmul_tn(qkv_t[head_rows(1, head), :], qkv_t[head_rows(0, head), :])
        scores = jnp.where(valid_keys, scores, masked_value)
        scores = jnp.exp(scores - jnp.max(scores, 0, keepdims=True))
        share = (scores * (1.0 / jnp.sum(scores, 0, keepdims=True))).astype(low)
        probs[head] = share
        context = matmul(qkv_t[head_rows(2, head), :], share)
        low_tmp_two[pl.ds(pl.multiple_of(head * size, size), size), :] = context.astype(low)
        return carry

    lax.fori_loop(0, heads, head_forward, 0, unroll=12)
    pass_from_y(0)
    cols[0] = low_tmp_two[...].T
    share_col(1)
    slot = take()
    acc[...] = matmul(cols[0], ring[slot])
    release(slot)

    def norm_rows(total):
        center = total - jnp.mean(total, -1, keepdims=True)
        rstd = lax.rsqrt(jnp.mean(center * center, -1, keepdims=True) + epsilon)
        return center * rstd, rstd

    def norm_first(r, i, carry):
        normed, rstd = norm_rows(hidden[r, :].astype(jnp.float32) + acc[r, :])
        stat[r, :] = jnp.broadcast_to(rstd, (step_rows, 128))
        low_tmp[r, :] = normed.astype(low)
        one_rows = normed * gain_attn
        wide[r, :] = one_rows
        cols[1, r, :] = one_rows.astype(low)
        return carry

    over_rows(norm_first)
    share_col(2)
    norm_one[...] = low_tmp[...].T.reshape(blocks, PIECE, tokens)
    stat_one[...] = stat[...].T[:8]

    for k in range(4):
        slot, slot_two = take(), take()
        acc[...] = matmul(cols[1], ring[slot])
        unit_base = 2 + (k % 2) * 2
        lanes = lanes_of[1 - k // 2]

        def gelu_rows(r, i, carry):
            before = acc[r, :]
            cdf, density = normal_parts(before)
            act = (before * cdf).astype(low)
            low_tmp[r, :] = act
            cols[unit_base, r, lanes] = act[:, :half_width]
            cols[unit_base + 1, r, lanes] = act[:, half_width:]
            cols[9, r, :] = (cdf + before * density).astype(low)
            return carry

        over_rows(gelu_rows)
        slope[pl.ds(ff_blocks[k] * blocks, blocks)] = cols[9].T.reshape(blocks, PIECE, tokens)
        value = matmul(low_tmp[...], ring[slot_two])
        acc_two[...] = value if k == 0 else acc_two[...] + value
        release(slot)
        release(slot_two)
        if k == 0:
            pass_from_y(1)
            half_hidden_over_x(1)
            col_over_x(1)
        if k < 2:
            col_over_y(2 * k)
            col_over_y(2 * k + 1)
        if k == 2:
            pass_from_x(0)
    for index in range(3, 7):
        share_col(index)

    def norm_second(r, i, carry):
        normed, rstd = norm_rows(wide[r, :] + acc_two[r, :])
        stat[r, :] = jnp.broadcast_to(rstd, (step_rows, 128))
        low_tmp[r, :] = normed.astype(low)
        two_rows = normed * gain_ff
        wide[r, :] = two_rows
        cols[6, r, :] = two_rows.astype(low)
        return carry

    over_rows(norm_second)
    share_col(7)
    norm_two[...] = low_tmp[...].T.reshape(blocks, PIECE, tokens)
    stat_two[...] = stat[...].T[:8]
    put_t(3, cols[6].T)
    share_row(3)

    slot_query = take()
    low_tmp[...] = matmul(cols[6], ring[slot_query]).astype(low)
    put_t(4, low_tmp[...].T)
    share_row(4)
    slot_key = take()
    put_t(2, matmul(ring[slot_key], get_t(4)).astype(low))
    share_row(2)

    def bank_ready(i):
        for side in range(2):
            bank_own[2 * i + side].wait()
        for copy in bank_sib[i]:
            copy.wait_recv()

    bank_ready(0)
    acc_t[...] = matmul(banks[0].reshape(width, width), get_t(3)).reshape(blocks, PIECE, tokens)
    pass_from_x(1)
    bank_ready(1)
    acc_t_two[...] = matmul(banks[1].reshape(width, width), get_t(2)).reshape(
        blocks, PIECE, tokens
    )
    score_scale = 1.0 / math.sqrt(width)
    groups = PIECE // adapters

    def grouped(value):
        return value.reshape(groups, adapters, tokens)

    def adapter_rows(p, logits):
        inner = acc_t[p]
        cdf, density = normal_parts(inner)
        act = inner * cdf
        active[p] = act
        bank_slope[p] = (cdf + inner * density).astype(low)
        return logits + grouped(act * acc_t_two[p]).sum(0)

    logits = over_pieces(adapter_rows, jnp.zeros((adapters, tokens), jnp.float32)) * score_scale
    logits = jnp.exp(logits - jnp.max(logits, 0, keepdims=True))
    shares = logits / jnp.sum(logits, 0, keepdims=True)

    def spread(value):
        return jnp.concatenate([value] * groups, 0)

    wide_shares = spread(shares)

    def mixing_rows(p, carry):
        low_tmp_two[pl.ds(p * PIECE, PIECE), :] = (
            wide_shares * active[p]
        ).astype(low)
        return carry

    over_pieces(mixing_rows)
    cols[8] = low_tmp_two[...].T
    share_col(9)
    acc[...] = matmul(cols[8], banks[1].reshape(width, width))

    def joined_rows(r, i, carry):
        cols[7, r, :] = (wide[r, :] + acc[r, :]).astype(low)
        return carry

    over_rows(joined_rows)
    share_col(8)
    slot_value = take()
    acc[...] = matmul(cols[7], ring[slot_value])

    upstream_copy.wait()

    def norm_third(r, i, gain_part):
        normed, rstd = norm_rows(wide[r, :] + acc[r, :])
        gain = gain_out
        acc_two[r, :] = normed * gain
        token = lax.broadcasted_iota(jnp.int32, (step_rows, 1), 0) + i * step_rows
        upstream = jnp.where(token < length, cotangent[r, :].astype(jnp.float32), 0.0)
        product = upstream * normed
        gained = upstream * gain
        third = rstd * (
            gained
            - jnp.mean(gained, -1, keepdims=True)
            - normed * jnp.mean(gained * normed, -1, keepdims=True)
        )
        low_tmp[r, :] = third.astype(low)
        return gain_part + product.reshape(step_rows // 8, 8, width).sum(0)

    gain_part = over_rows(norm_third, jnp.zeros((8, width), jnp.float32))
    out_copy = pltpu.make_async_copy(acc_two, output, local_sem.at[0])
    out_copy.start()
    gain_sum[0] = jnp.broadcast_to(jnp.sum(gain_part, 0, keepdims=True), (8, width))
    put_t(0, low_tmp[...].T)
    share_row(0)

    state = {}

    def value_back():
        second[...] = matmul(ring[slot_value], get_t(0)).reshape(blocks, PIECE, tokens)
        release(slot_value)

        def mix_rows(p, carry):
            zz, xx, cc = spot(p)
            rows[1, zz, xx, cc] = second[p].astype(low)
            return carry

        over_pieces(mix_rows)
        share_row(1)
        acc_t[...] = matmul(banks[1].reshape(width, width), get_t(1)).reshape(blocks, PIECE, tokens)

    def adapter_grads():
        def share_rows(p, total):
            return total + grouped(acc_t[p] * active[p]).sum(0)

        share_grad = over_pieces(share_rows, jnp.zeros((adapters, tokens), jnp.float32))
        logit_grad = shares * (share_grad - jnp.sum(shares * share_grad, 0, keepdims=True))
        wide_logit = spread(logit_grad * score_scale)

        def adapter_back(p, carry):
            act_grad = acc_t[p] * wide_shares + wide_logit * acc_t_two[p]
            where = pl.ds(p * PIECE, PIECE)
            low_tmp_two[where, :] = (wide_logit * active[p]).astype(low)
            bank_slope[p] = (bank_slope[p].astype(jnp.float32) * act_grad).astype(low)
            return carry

        over_pieces(adapter_back)
        cols[9] = low_tmp_two[...].T
        share_col(10)
        cols[10] = bank_slope[...].reshape(width, tokens).T
        share_col(11)

    def probe_back():
        cols[11] = matmul(cols[9], banks[1].reshape(width, width)).astype(low)
        share_col(12)
        low_tmp[...] = matmul(cols[11], ring[slot_key]).astype(low)
        release(slot_key)
        put_t(5, low_tmp[...].T)
        share_row(5)
        low_tmp[...] = matmul(cols[10], banks[0].reshape(width, width)).astype(low)
        low_tmp_two[...] = low_tmp[...].T
        acc_t[...] = matmul(ring[slot_query], get_t(5)).reshape(blocks, PIECE, tokens)
        release(slot_query)

    def norm_back(index, gain, normed_ref, stat_ref, upstream_of, factor):
        gain_col[...] = jnp.broadcast_to(gain, (128, width)).T.reshape(blocks, PIECE, 128)

        def gained(p):
            column = gain_col[p]
            return acc_t[p] * jnp.concatenate([column] * (tokens // 128), 1)

        def first_pass(p, carry):
            upstream = upstream_of(p)
            acc_t[p] = upstream
            normed = normed_ref[p].astype(jnp.float32)
            gain_of = jnp.sum(upstream * normed, -1, keepdims=True)
            weighted = gained(p)
            gain_col[p] = jnp.broadcast_to(gain_of, (PIECE, 128))
            acc_t[p] = weighted
            return carry[0] + fold(weighted), carry[1] + fold(weighted * normed)

        zeros = jnp.zeros((8, tokens), jnp.float32)
        plain, tilted = over_pieces(first_pass, (zeros, zeros))
        mean_plain = jnp.sum(plain, 0, keepdims=True) * (1.0 / width)
        mean_tilted = jnp.sum(tilted, 0, keepdims=True) * (1.0 / width)
        rstd = stat_ref[0:1, :]

        def second_pass(p, carry):
            value = rstd * (acc_t[p] - mean_plain - normed_ref[p].astype(jnp.float32) * mean_tilted)
            second[p] = value
            zz, xx, cc = spot(p)
            rows[factor, zz, xx, cc] = value.astype(low)
            return carry

        over_pieces(second_pass)
        gain_sum[0, index : index + 1, :] = gain_col[...].reshape(width, 128).T[:1]

    def upstream_two(p):
        zz, xx, cc = spot(p)
        where = pl.ds(p * PIECE, PIECE)
        total = rows[0, zz, xx, cc].astype(jnp.float32) + second[p]
        return total + low_tmp_two[where, :].astype(jnp.float32) + acc_t[p]

    def norm_two_back():
        norm_back(1, gain_ff, norm_two, stat_two, upstream_two, 6)
        share_row(6)

    def ff_back(k):
        slot, slot_two = take(), take()
        acc_t_two[...] = matmul(ring[slot], get_t(6)).reshape(blocks, PIECE, tokens)

        def slope_rows(p, carry):
            value = acc_t_two[p] * slope[k * blocks + p].astype(jnp.float32)
            rows_ff[k, p // 8, (p % 8) // 2, p % 2] = value.astype(low)
            return carry

        over_pieces(slope_rows)
        value = matmul(ring[slot_two], rows_ff[k].reshape(width, tokens))
        value = value.reshape(blocks, PIECE, tokens)
        release(slot)
        release(slot_two)
        acc_t[...] = value if k == 0 else acc_t[...] + value
        if k == 3:
            for index in range(8, 12):
                share_row(index)

    def upstream_one(p):
        return second[p] + acc_t[p]

    def norm_one_back():
        norm_back(0, gain_attn, norm_one, stat_one, upstream_one, 7)
        share_row(7)
        slot = take()
        low_tmp_two[...] = matmul(ring[slot], get_t(7)).astype(low)
        release(slot)

    heads_step = 3
    step_pieces = heads_step * size // PIECE

    def head_backward(group, carry):
        grads = [[], [], []]
        for i in range(heads_step):
            head = group * heads_step + i
            query, key, value = [qkv_t[head_rows(k, head), :] for k in range(3)]
            upstream = low_tmp_two[pl.ds(pl.multiple_of(head * size, size), size), :]
            share = probs[head]
            share_wide = share.astype(jnp.float32)
            prob_grad = matmul_tn(value, upstream)
            delta = jnp.sum(share_wide * prob_grad, 0, keepdims=True)
            score_grad = (share_wide * (prob_grad - delta)).astype(low)
            grads[0].append((matmul(key, score_grad) * 0.125).astype(low))
            grads[1].append(matmul_t(query, score_grad).astype(low))
            grads[2].append(matmul_t(upstream, share).astype(low))
        for k in range(3):
            stacked = jnp.concatenate(grads[k], 0).reshape(step_pieces, PIECE, tokens)
            for i in range(step_pieces):
                p = k * blocks + group * step_pieces + i
                rows_qkv[p // 12, (p // 6) % 2, (p % 6) // 2, p % 2] = stacked[i]
        return carry

    def attention_back():
        lax.fori_loop(0, heads // heads_step, head_backward, 0)
        for index in range(12, 15):
            share_row(index)

    def input_back():
        for k in range(3):
            slot = take()
            block = rows_qkv[...].reshape(3 * blocks, PIECE, tokens)[k * blocks : (k + 1) * blocks]
            value = matmul(ring[slot], block.reshape(width, tokens)).reshape(blocks, PIECE, tokens)
            release(slot)
            second[...] = second[...] + value
        acc[...] = second[...].reshape(width, tokens).T
        state["in"] = pltpu.make_async_copy(acc, grad_in, local_sem.at[1])
        state["in"].start()

    gain_mates = (sibling, x_mate, y_mate, mates["l"], mates["h"])

    def gain_step(stage):
        if stage > 0:
            state["gain"].wait_recv()
            total = gain_sum[stage - 1] + gain_from[stage - 1]
            if stage == 5:
                gain_sums[...] = total
                return
            gain_sum[stage] = total
        state["gain"] = send(
            gain_sum.at[stage],
            gain_from.at[stage],
            gain_recv.at[stage],
            gain_mates[stage],
        )

    chain = [value_back, adapter_grads, probe_back, norm_two_back]
    chain += [functools.partial(ff_back, k) for k in range(4)]
    chain += [norm_one_back, attention_back, input_back]
    progress = [0] * units
    since_chain, gain_stage = 0, 0
    for action in SEQUENCE:
        if action < 0:
            chain.pop(0)()
        elif progress[action] == 0:
            start(action)
        elif progress[action] < 4:
            advance(action, progress[action] - 1)
        else:
            close(action)
        if action >= 0:
            progress[action] += 1
        if not chain:
            if since_chain % 4 == 0 and gain_stage < 6:
                gain_step(gain_stage)
                gain_stage += 1
            since_chain += 1
    for stage in range(gain_stage, 6):
        gain_step(stage)
    for unit in range(units):
        last[unit].wait_recv()
    for copy in started[-SENDS:]:
        copy.wait_send()
    out_copy.wait()
    state["in"].wait()


def run_layer(heads, adapters, arrays):
    hidden = arrays[0]
    tokens, width = hidden.shape
    low, wide = jnp.bfloat16, jnp.float32
    blocks = width // PIECE
    units = len(UNITS)
    dma = pltpu.SemaphoreType.DMA
    vmem = pl.BlockSpec(memory_space=pltpu.VMEM)
    smem = pl.BlockSpec(memory_space=pltpu.SMEM)
    far = pl.BlockSpec(memory_space=pl.ANY)
    half_width = width // 2
    return pl.pallas_call(
        functools.partial(layer_kernel, heads, adapters),
        out_shape=(
            jax.ShapeDtypeStruct((tokens, width), wide),
            jax.ShapeDtypeStruct((tokens, width), wide),
            jax.ShapeDtypeStruct((units, 2, PIECE, half_width), low),
            jax.ShapeDtypeStruct((8, width), wide),
        ),
        in_specs=[
            vmem, smem, far, far, far, vmem, far, far, vmem, far, far, far, far, far, vmem,
        ],
        out_specs=[far, far, vmem, vmem],
        scratch_shapes=[
            pltpu.VMEM((8, 4, 2, 2, PIECE, tokens), low),
            pltpu.VMEM((4, 2, 4, 2, PIECE, tokens), low),
            pltpu.VMEM((4, 2, 3, 2, PIECE, tokens), low),
            pltpu.VMEM((15, 4, 2, PIECE, tokens), low),
            pltpu.VMEM((12, tokens, width), low),
            pltpu.VMEM((13, tokens, width), low),
            pltpu.VMEM((2, 7, 4, PIECE, tokens), low),
            pltpu.VMEM((2, 2, tokens, width), low),
            pltpu.VMEM((2, 4, 2, PIECE, tokens), low),
            pltpu.VMEM((2, 4, tokens, half_width), low),
            pltpu.VMEM((SLOTS, width, width), low),
            pltpu.VMEM((2, 4, 2, width // 8, width), low),
            pltpu.VMEM((tokens, width), wide),
            pltpu.VMEM((tokens, width), wide),
            pltpu.VMEM((tokens, width), wide),
            pltpu.VMEM((blocks, PIECE, tokens), wide),
            pltpu.VMEM((blocks, PIECE, tokens), wide),
            pltpu.VMEM((blocks, PIECE, tokens), wide),
            pltpu.VMEM((blocks, PIECE, tokens), low),
            pltpu.VMEM((blocks, PIECE, tokens), wide),
            pltpu.VMEM((blocks, PIECE, tokens), low),
            pltpu.VMEM((blocks, PIECE, tokens), low),
            pltpu.VMEM((4 * blocks, PIECE, tokens), low),
            pltpu.VMEM((3 * width, tokens), low),
            pltpu.VMEM((heads, tokens, tokens), low),
            pltpu.VMEM((tokens, width), low),
            pltpu.VMEM((width, tokens), low),
            pltpu.VMEM((tokens, 128), wide),
            pltpu.VMEM((8, tokens), wide),
            pltpu.VMEM((8, tokens), wide),
            pltpu.VMEM((blocks, PIECE, 128), wide),
            pltpu.VMEM((tokens, width), low),
            pltpu.VMEM((units, 2, 2, 2, 2, PIECE, half_width), low),
            pltpu.VMEM((len(WHOLE), 2, 2, 2, PIECE, half_width), low),
            pltpu.VMEM((units, 2, 2, PIECE, half_width), low),
            pltpu.VMEM((units, 2, PIECE, half_width), low),
            pltpu.VMEM((units, PIECE, half_width), low),
            pltpu.VMEM((5, 8, width), wide),
            pltpu.VMEM((5, 8, width), wide),
            dma((SLOTS,)),
            dma((7,)),
            dma((SENDS,)),
            dma((2, 6)),
            dma((15,)),
            dma((13,)),
            dma((2, 7)),
            dma((2, 2)),
            dma((2,)),
            dma((2,)),
            dma((2, 4)),
            dma((4, units)),
            dma((units,)),
            dma((5,)),
        ],
        compiler_params=pltpu.CompilerParams(
            collective_id=0, has_side_effects=True, vmem_limit_bytes=63 * 2**20
        ),
    )(*arrays)


def finish_kernel(
    sums_far,
    gain_sums_far,
    output,
    grad_in,
    out_output,
    out_grad_in,
    out_qkv,
    out_proj,
    out_gain_attn,
    out_ff_in,
    out_ff_out,
    out_gain_ff,
    out_query,
    out_key,
    out_value,
    out_down,
    out_up,
    out_gain_out,
    turned,
    sums,
    gain_sums,
    held,
    copy_sem,
):
    fetched = [
        pltpu.make_async_copy(sums_far, sums, copy_sem.at[2]),
        pltpu.make_async_copy(gain_sums_far, gain_sums, copy_sem.at[3]),
    ]
    through = [
        pltpu.make_async_copy(output, held.at[0], copy_sem.at[0]),
        pltpu.make_async_copy(grad_in, held.at[1], copy_sem.at[1]),
    ]
    for copy in fetched + through:
        copy.start()
    for copy in fetched:
        copy.wait()
    ad = lax.axis_index("ad")
    core = lax.axis_index("bn") % 2
    width = sums.shape[3]
    own = pl.ds(pl.multiple_of(core * (width // 2), width // 2), width // 2)

    def columns(out, slot, first, count):
        value = sums[first : first + count].reshape(count * 2 * PIECE, width)
        extent = pl.ds(0, count * 2 * PIECE)
        turned[slot, :, extent] = value.astype(jnp.float32).T
        out[...] = turned[slot, own, extent]

    columns(out_value, 0, 0, 1)
    columns(out_up, 1, 1, 1)
    columns(out_down, 2, 2, 1)
    columns(out_key, 0, 3, 1)
    columns(out_query, 1, 4, 1)
    for copy in through:
        copy.wait()
    passed = [
        pltpu.make_async_copy(held.at[0], out_output, copy_sem.at[0]),
        pltpu.make_async_copy(held.at[1], out_grad_in, copy_sem.at[1]),
    ]
    for copy in passed:
        copy.start()
    columns(out_ff_in, 2, 9, 4)
    columns(out_proj, 0, 13, 1)
    columns(out_qkv, 1, 14, 3)
    for i in range(2):
        value = sums[5 + 2 * core + i].reshape(2 * PIECE, width)
        out_ff_out[:, pl.ds(i * width, width)] = value.astype(jnp.float32)
    total = gain_sums.shape[1]
    piece = out_gain_attn.shape[0]
    rolled = pltpu.roll(gain_sums[...], lax.rem(total - ad * piece, total), 1)[:, :piece]
    for index, out in enumerate((out_gain_attn, out_gain_ff, out_gain_out)):
        out[...] = rolled[index : index + 1].reshape(piece)
    for copy in passed:
        copy.wait()


def finish(sums, gain_sums, output, grad_in, width):
    quarter, eighth = width // 4, width // 8
    far = pl.BlockSpec(memory_space=pl.ANY)
    shapes = [
        output.shape,
        grad_in.shape,
        (quarter, 3 * eighth),
        (quarter, eighth),
        (eighth,),
        (quarter, 4 * eighth),
        (eighth, 4 * quarter),
        (eighth,),
    ]
    shapes += [(quarter, eighth)] * 5 + [(eighth,)]
    return pl.pallas_call(
        finish_kernel,
        out_shape=tuple(jax.ShapeDtypeStruct(shape, jnp.float32) for shape in shapes),
        in_specs=[far] * 4,
        out_specs=[far] * 2 + [pl.BlockSpec(memory_space=pltpu.VMEM)] * 12,
        scratch_shapes=[
            pltpu.VMEM((3, width // 2, 4 * eighth), jnp.float32),
            pltpu.VMEM(sums.shape, sums.dtype),
            pltpu.VMEM(gain_sums.shape, gain_sums.dtype),
            pltpu.VMEM((2, *output.shape), output.dtype),
            pltpu.SemaphoreType.DMA((4,)),
        ],
        compiler_params=pltpu.CompilerParams(vmem_limit_bytes=62 * 2**20),
    )(sums, gain_sums, output, grad_in)


def fast_local(*arrays):
    arrays = list(arrays)
    width = arrays[0].shape[1]
    adapters = arrays[12].shape[1]
    bank_shape = arrays[12].shape[:2] + (-1,)
    for i in (12, 13):
        arrays[i] = arrays[i].reshape(-1, width)
    output, grad_in, sums, gain_sums = run_layer(H, adapters, arrays)
    results = list(finish(sums, gain_sums, output, grad_in, width))
    results[6] = results[6].T
    for i in (11, 12):
        results[i] = results[i].reshape(bank_shape)
    return tuple(results)


def local(
    hidden_in,
    lengths,
    cotangent,
    w_qkv,
    w_out,
    gain_attn,
    w_ff_in,
    w_ff_out,
    gain_ff,
    join_query,
    join_key,
    join_value,
    adapt_down,
    adapt_up,
    gain_out,
):
    seq_count = lengths.shape[0]
    tok_rows, model_width = hidden_in.shape
    slot_len = tok_rows // seq_count
    head_count = H
    head_size = model_width // head_count
    score_scale = 1.0 / math.sqrt(head_size)
    adapters = adapt_down.shape[1]
    down_flat = lax.all_gather(adapt_down.reshape(-1, model_width), "bn", axis=0, tiled=True)
    up_flat = lax.all_gather(adapt_up.reshape(-1, model_width), "bn", axis=0, tiled=True)
    valid = lax.broadcasted_iota(jnp.int32, (seq_count, slot_len), 1) < lengths[:, None]
    row_ok = valid.reshape(tok_rows, 1).astype(jnp.float32)
    tokens_wide = hidden_in.astype(jnp.float32)
    qkv = matmul(hidden_in, w_qkv).astype(jnp.bfloat16)
    queries = qkv[:, :model_width].reshape(seq_count, slot_len, head_count, head_size)
    key_rows = qkv[:, model_width : 2 * model_width].reshape(
        seq_count, slot_len, head_count, head_size
    )
    values = qkv[:, 2 * model_width :].reshape(seq_count, slot_len, head_count, head_size)

    def attend_scores():
        raw_scores = (
            jnp.einsum("sqhe,skhe->shqk", queries, key_rows, preferred_element_type=jnp.float32)
            * score_scale
        )
        return jnp.where(valid[:, None, None, :], raw_scores, masked_value)

    scores = attend_scores()
    row_max = jnp.max(scores, -1, keepdims=True)
    log_total = row_max + jnp.log(jnp.sum(jnp.exp(scores - row_max), -1, keepdims=True))
    probs = jnp.exp(scores - log_total).astype(jnp.bfloat16)
    context = (
        jnp.einsum("shqk,skhe->sqhe", probs, values, preferred_element_type=jnp.float32)
        .reshape(tok_rows, model_width)
        .astype(jnp.bfloat16)
    )
    attn_out = matmul(context, w_out)
    hidden_one, norm_one_back = jax.vjp(layer_norm, tokens_wide + attn_out, gain_attn)
    hidden_one_low = hidden_one.astype(jnp.bfloat16)
    ff_pre = matmul(hidden_one_low, w_ff_in)
    ff_act, gelu_ff_back = jax.vjp(gelu_exact, ff_pre)
    ff_low = ff_act.astype(jnp.bfloat16)
    ff_out = matmul(ff_low, w_ff_out)
    hidden_two, norm_two_back = jax.vjp(layer_norm, hidden_one + ff_out, gain_ff)
    hidden_low = hidden_two.astype(jnp.bfloat16)
    query_join = matmul(hidden_low, join_query).astype(jnp.bfloat16)
    probe = matmul_t(query_join, join_key).astype(jnp.bfloat16)
    mixing, kept_state = adapter_forward(hidden_low, probe, down_flat, up_flat, adapters)
    joined_in = (hidden_two + matmul(mixing, up_flat)).astype(jnp.bfloat16)
    joined = matmul(joined_in, join_value)
    output, norm_out_back = jax.vjp(layer_norm, hidden_two + joined, gain_out)
    out_grad = cotangent.astype(jnp.float32) * row_ok
    sum_three, gain_out_grad = norm_out_back(out_grad)
    joined_grad = sum_three.astype(jnp.bfloat16)
    into_joined = matmul_t(joined_grad, join_value)
    mix_grad = into_joined.astype(jnp.bfloat16)
    inner_grad, weigh_grad = adapter_backward(kept_state, up_flat, mix_grad, adapters)
    hidden_back = matmul(inner_grad, down_flat)
    probe_grad = matmul(weigh_grad, up_flat).astype(jnp.bfloat16)
    query_in = matmul(probe_grad, join_key).astype(jnp.bfloat16)
    grad_two = sum_three + into_joined + hidden_back + matmul_t(query_in, join_query)
    sum_two, gain_ff_grad = norm_two_back(grad_two)
    ff_out_grad = sum_two.astype(jnp.bfloat16)
    ff_pre_grad = gelu_ff_back(matmul_t(ff_out_grad, w_ff_out))[0].astype(jnp.bfloat16)
    grad_one = sum_two + matmul_t(ff_pre_grad, w_ff_in)
    sum_one, gain_attn_grad = norm_one_back(grad_one)
    attn_grad = sum_one.astype(jnp.bfloat16)
    context_grad = (
        matmul_t(attn_grad, w_out)
        .astype(jnp.bfloat16)
        .reshape(seq_count, slot_len, head_count, head_size)
    )
    probs_wide = jnp.exp(attend_scores() - log_total)
    prob_grad = jnp.einsum(
        "sqhe,skhe->shqk", context_grad, values, preferred_element_type=jnp.float32
    )
    row_delta = jnp.sum(probs_wide * prob_grad, -1, keepdims=True)
    score_grad = (probs_wide * (prob_grad - row_delta)).astype(jnp.bfloat16)
    query_back = (
        jnp.einsum("shqk,skhe->sqhe", score_grad, key_rows, preferred_element_type=jnp.float32)
        * score_scale
    )
    key_back = (
        jnp.einsum("shqk,sqhe->skhe", score_grad, queries, preferred_element_type=jnp.float32)
        * score_scale
    )
    value_back = jnp.einsum(
        "shqk,sqhe->skhe", probs, context_grad, preferred_element_type=jnp.float32
    )
    qkv_grad = jnp.concatenate(
        [
            query_back.reshape(tok_rows, model_width),
            key_back.reshape(tok_rows, model_width),
            value_back.reshape(tok_rows, model_width),
        ],
        1,
    ).astype(jnp.bfloat16)
    grad_in = sum_one + matmul_t(qkv_grad, w_qkv)
    def shared_sum(gradient):
        columns = lax.psum_scatter(gradient, "ad", scatter_dimension=1, tiled=True)
        return lax.psum_scatter(
            columns.astype(jnp.bfloat16), "bn", scatter_dimension=0, tiled=True
        ).astype(jnp.float32)

    gains = lax.psum(
        lax.psum_scatter(
            jnp.stack([gain_attn_grad, gain_ff_grad, gain_out_grad]),
            "ad",
            scatter_dimension=1,
            tiled=True,
        ),
        "bn",
    )
    down_grad = shared_sum(matmul_tn(inner_grad, hidden_low))
    up_grad = shared_sum(matmul_tn(mixing, mix_grad) + matmul_tn(weigh_grad, probe))
    bank = adapt_down.shape[:2] + (-1,)
    return (
        output,
        grad_in,
        shared_sum(matmul_tn(hidden_in, qkv_grad)),
        shared_sum(matmul_tn(context, attn_grad)),
        gains[0],
        shared_sum(matmul_tn(hidden_one_low, ff_pre_grad)),
        shared_sum(matmul_tn(ff_low, ff_out_grad)),
        gains[1],
        shared_sum(matmul_tn(hidden_low, query_in)),
        shared_sum(matmul_tn(probe_grad, query_join)),
        shared_sum(matmul_tn(joined_in, joined_grad)),
        down_grad.reshape(bank),
        up_grad.reshape(bank),
        gains[2],
    )


def solution(mesh):
    placed = (
        P(("ad", "bn"), None),
        P(("ad", "bn")),
        P(("ad", "bn"), None),
        P(),
        P(),
        P(),
        P(),
        P(),
        P(),
        P(),
        P(),
        P(),
        P("bn", None, None),
        P("bn", None, None),
        P(),
    )
    sizes = (mesh.shape["ad"], mesh.shape["bn"])
    return jax.shard_map(
        fast_local if sizes == (8, 4) else local,
        mesh=mesh,
        in_specs=placed,
        out_specs=(
            P(("ad", "bn"), None),
            P(("ad", "bn"), None),
            P("bn", "ad"),
            P("bn", "ad"),
            P("ad"),
            P("bn", "ad"),
            P("bn", "ad"),
            P("ad"),
            P("bn", "ad"),
            P("bn", "ad"),
            P("bn", "ad"),
            P("bn", None, "ad"),
            P("bn", None, "ad"),
            P("ad"),
        ),
        check_vma=False,
    )
```

```python
import functools
import math

import jax
import jax.numpy as jnp
from jax import lax
from jax.experimental import pallas as pl
from jax.experimental.pallas import tpu as pltpu
from jax.sharding import PartitionSpec as P

H = 12


epsilon = 1e-06
masked_value = -1000000000.0
MESH = pl.DeviceIdType.MESH


def layer_norm(values, gain):
    center = values - jnp.mean(values, -1, keepdims=True)
    spread = jnp.mean(center * center, -1, keepdims=True)
    return center * lax.rsqrt(spread + epsilon) * gain


def gelu_exact(values):
    return jax.nn.gelu(values, approximate=False)


def matmul(left, right):
    return jnp.dot(left, right, preferred_element_type=jnp.float32)


def matmul_t(left, right):
    return lax.dot_general(
        left, right, (((1,), (1,)), ((), ())), preferred_element_type=jnp.float32
    )


def matmul_tn(left, right):
    return lax.dot_general(
        left, right, (((0,), (0,)), ((), ())), preferred_element_type=jnp.float32
    )


def adapter_forward(hidden, probe_rows, down_flat, up_flat, adapters):
    row_count, model_width = hidden.shape
    inner_pre = matmul_t(hidden, down_flat)
    active = gelu_exact(inner_pre)
    weigh_rows = matmul_t(probe_rows, up_flat)
    logits = jnp.sum((active * weigh_rows).reshape(row_count, -1, adapters), 1) / math.sqrt(
        model_width
    )
    shares = jax.nn.softmax(logits, -1)
    mixing = (
        (shares[:, None, :] * active.reshape(row_count, -1, adapters))
        .reshape(row_count, -1)
        .astype(jnp.bfloat16)
    )
    return (mixing, (inner_pre, active, weigh_rows, shares))


def adapter_backward(kept_state, up_flat, mix_grad, adapters):
    inner_pre, active, weigh_rows, shares = kept_state
    row_count, model_width = mix_grad.shape
    score_scale = 1.0 / math.sqrt(model_width)
    mix_in = matmul_t(mix_grad, up_flat).reshape(row_count, -1, adapters)
    active_three = active.reshape(row_count, -1, adapters)
    weigh_three = weigh_rows.reshape(row_count, -1, adapters)
    share_grad = jnp.sum(mix_in * active_three, 1)
    logit_grad = shares * (share_grad - jnp.sum(shares * share_grad, -1, keepdims=True))
    act_grad = mix_in * shares[:, None, :] + logit_grad[:, None, :] * score_scale * weigh_three
    weigh_grad = (
        (logit_grad[:, None, :] * score_scale * active_three)
        .reshape(row_count, -1)
        .astype(jnp.bfloat16)
    )
    unused, gelu_back = jax.vjp(gelu_exact, inner_pre)
    inner_grad = gelu_back(act_grad.reshape(row_count, -1))[0].astype(jnp.bfloat16)
    return (inner_grad, weigh_grad)


PIECE = 48
SLOTS = 5
SENDS = 32
UNITS = (
    ((0, 8),),
    ((1, 9), (2, 10)),
    ((3, 11),),
    ((4, 12),),
    ((5, 7),),
    ((6, 3),),
    ((6, 4),),
    ((6, 5),),
    ((6, 6),),
    ((8, 2),),
    ((9, 2),),
    ((10, 2),),
    ((11, 2),),
    ((7, 1),),
    ((12, 0),),
    ((13, 0),),
    ((14, 0),),
)


CROSS_X = (9, 10, 11, 12, 14, 15, 16)
CROSS_Y = (5, 6, 7, 8)
WHOLE = tuple(unit for unit in range(len(UNITS)) if unit not in CROSS_X + CROSS_Y)
ORDERS = (
    ("l", "y", "x", "h"),
    ("y", "l", "x", "h"),
    ("l", "y", "x", "h"),
    ("x", "l", "y", "h"),
    ("l", "x", "y", "h"),
    ("y", "l", "x", "h"),
    ("y", "l", "x", "h"),
    ("y", "x", "l", "h"),
    ("y", "x", "l", "h"),
    ("x", "y", "l", "h"),
    ("x", "l", "y", "h"),
    ("x", "y", "l", "h"),
    ("x", "y", "l", "h"),
    ("y", "l", "x", "h"),
    ("x", "y", "l", "h"),
    ("x", "y", "l", "h"),
    ("x", "y", "l", "h"),
)
SEQUENCE = (
    -1, -1, -1, 0, 1, -1, 3, 2, -1, 6, 7, 5, 8, -1, -1, -1, 4, -1, 9, 12, -1, 0, 11, -1,
    1, 9, 16, 3, 13, 6, 14, 5, 10, 12, 9, 3, 15, 16, 13, 11, 1, 12, 9, 6, 14, 3, 10, 0,
    13, 2, 16, 12, 5, 9, 3, 7, 15, 1, 11, 6, 4, 10, 0, 14, 16, 12, 13, 1, 8, 5, 11, 6,
    0, 2, 7, 15, 14, 16, 10, 13, 5, 4, 11, 7, 8, 15, 4, 14, 2, 10, 7, 8, 15, 4, 2, 8,
)

def flip(index, bit):
    return index + bit - 2 * bit * ((index // bit) % 2)


def normal_parts(values):
    cdf = 0.5 * (1.0 + lax.erf(values * (1.0 / math.sqrt(2.0))))
    density = jnp.exp(values * values * -0.5) * (1.0 / math.sqrt(2.0 * math.pi))
    return cdf, density


def layer_kernel(
    heads,
    adapters,
    hidden,
    lengths,
    cotangent_far,
    w_qkv,
    w_out,
    gain_attn,
    w_ff_in,
    w_ff_out,
    gain_ff,
    join_query,
    join_key,
    join_value,
    adapt_down,
    adapt_up,
    gain_out,
    output,
    grad_in,
    sums,
    gain_sums,
    rows,
    rows_ff,
    rows_qkv,
    rows_sib,
    cols,
    cols_sib,
    rows_x,
    cols_x,
    rows_y,
    cols_y,
    ring,
    banks,
    acc,
    acc_two,
    wide,
    acc_t,
    acc_t_two,
    active,
    bank_slope,
    second,
    norm_one,
    norm_two,
    slope,
    qkv_t,
    probs,
    low_tmp,
    low_tmp_two,
    stat,
    stat_one,
    stat_two,
    gain_col,
    cotangent,
    part,
    recv_one,
    recv_two,
    recv_three,
    recv_four,
    gain_sum,
    gain_from,
    ring_sem,
    local_sem,
    send_sem,
    bank_recv,
    row_recv,
    col_recv,
    row_x_recv,
    col_x_recv,
    hidden_x_recv,
    row_y_recv,
    col_y_recv,
    stage_recv,
    last_recv,
    gain_recv,
):
    low = jnp.bfloat16
    tokens, width = hidden.shape
    half_width = width // 2
    gain_attn, gain_ff, gain_out = [
        gain[...].reshape(1, width) for gain in (gain_attn, gain_ff, gain_out)
    ]
    blocks = rows.shape[1] * rows.shape[2] * rows.shape[3]
    ad = lax.axis_index("ad")
    bn = lax.axis_index("bn")
    x, z = ad % 2, ad // 2
    core, y = bn % 2, bn // 2
    sibling = (ad, flip(bn, 1))
    x_mate = (flip(ad, 1), bn)
    y_mate = (ad, flip(bn, 2))
    own = {"y": y, "x": x, "h": z // 2, "l": z % 2}
    mates = {"y": y_mate, "x": x_mate, "h": (flip(ad, 4), bn), "l": (flip(ad, 2), bn)}
    other_core = 1 - core

    loads = [(w_qkv.at[:, pl.ds(k * width, width)]) for k in range(3)] + [w_out]
    ff_blocks = [2 * (1 - y), 2 * (1 - y) + 1, 2 * y, 2 * y + 1]
    for block in ff_blocks:
        where = pl.ds(pl.multiple_of(block * width, width), width)
        loads.append(w_ff_in.at[:, where])
        loads.append(w_ff_out.at[where, :])
    loads += [join_query, join_key, join_value]
    for k in range(4):
        loads.append(w_ff_out.at[pl.ds(k * width, width), :])
        loads.append(w_ff_in.at[:, pl.ds(k * width, width)])
    loads += [w_out] + [w_qkv.at[:, pl.ds(k * width, width)] for k in range(3)]
    free_slots = list(range(SLOTS))
    in_flight = []
    next_load = [0]

    def fill():
        while free_slots and next_load[0] < len(loads):
            slot = free_slots.pop(0)
            copy = pltpu.make_async_copy(loads[next_load[0]], ring.at[slot], ring_sem.at[slot])
            copy.start()
            in_flight.append((slot, copy))
            next_load[0] += 1

    def take():
        slot, copy = in_flight.pop(0)
        copy.wait()
        return slot

    def release(slot):
        free_slots.append(slot)
        fill()

    fill()
    upstream_copy = pltpu.make_async_copy(cotangent_far, cotangent, local_sem.at[6])
    upstream_copy.start()
    bank_own = []
    for i, bank in enumerate((adapt_down, adapt_up)):
        for side in range(2):
            bank_own.append(
                pltpu.make_async_copy(
                    bank.at[pl.ds(side * (width // 8), width // 8), :],
                    banks.at[i, bn, side],
                    local_sem.at[2 + 2 * i + side],
                )
            )
            bank_own[-1].start()

    barrier = pltpu.get_barrier_semaphore()
    for mate in [sibling, *mates.values()]:
        pl.semaphore_signal(barrier, inc=1, device_id=mate, device_id_type=MESH)

    started = []

    def send(source, target, recv_sem, mate):
        slot = len(started) % SENDS
        if len(started) >= SENDS:
            started[-SENDS].wait_send()
        copy = pltpu.make_async_remote_copy(
            src_ref=source,
            dst_ref=target,
            send_sem=send_sem.at[slot],
            recv_sem=recv_sem,
            device_id=mate,
            device_id_type=MESH,
        )
        copy.start()
        started.append(copy)
        return copy

    def row_views(index):
        if index < 8:
            return rows.at[index]
        if index < 12:
            return rows_ff.at[:, :, index - 8]
        return rows_qkv.at[:, :, index - 12]

    def row_half(index, side):
        if index < 8:
            piece = rows[index, :, side, core]
        elif index < 12:
            piece = rows_ff[:, side, index - 8, core]
        else:
            piece = rows_qkv[:, side, index - 12, core]
        return piece.reshape(4 * PIECE, tokens)

    def col_ref(index):
        return hidden if index == 0 else cols.at[index - 1]

    row_copies, col_copies = {}, {}
    arrived = set()

    def share_row(index):
        row_copies[index] = send(
            row_views(index).at[:, :, other_core],
            rows_sib.at[index],
            row_recv.at[index],
            sibling,
        )

    def share_col(index):
        col_copies[index] = send(
            col_ref(index),
            cols_sib.at[index],
            col_recv.at[index],
            sibling,
        )

    cross = {}
    lanes_of = [
        pl.ds(pl.multiple_of(side * half_width, half_width), half_width) for side in (y, 1 - y)
    ]

    def cross_send(key, source, target, sem, index, mate):
        cross[key] = send(source, target, sem.at[index], mate)

    def col_over_x(i):
        cross_send(("cx", i), col_ref(2 * i), cols_x.at[0, i], col_x_recv, (0, i), x_mate)

    def half_hidden_over_x(side):
        where = pl.ds(side * (tokens // 2), tokens // 2)
        cross_send(
            ("hx", side), hidden.at[where], cols_x.at[0, 0, where], hidden_x_recv, side, x_mate
        )

    def col_over_y(k):
        source = cols.at[2 + k, :, lanes_of[1]]
        cross_send(("cy", k), source, cols_y.at[0, k], col_y_recv, (0, k), y_mate)

    def need(copy_key, table=cross):
        if (id(table), copy_key) not in arrived:
            table[copy_key].wait_recv()
            arrived.add((id(table), copy_key))

    def pass_col_x(i):
        if ("fx", i) not in cross:
            for key in (("cx", 1),) if i else (("hx", 0), ("hx", 1)):
                need(key)
            cross_send(
                ("fx", i), cols_x.at[0, i], cols_x.at[1, i], col_x_recv, (1, i), sibling
            )

    def pass_col_y(k):
        need(("cy", k))
        cross_send(
            ("fy", k), cols_y.at[0, k], cols_y.at[1, k], col_y_recv, (1, k), sibling
        )

    def start_x(unit):
        left, right = UNITS[unit][0]
        n = left - 8
        sem = row_x_recv
        source = row_views(left).at[:, 1 - x, core]
        cross_send(("rx", n, 0), source, rows_x.at[0, n], sem, (0, n), x_mate)
        pass_col_x(right // 2)
        need(left, row_copies)
        cross_send(
            ("rx", n, 1), rows_sib.at[left, :, 1 - x], rows_x.at[1, n], sem, (1, n), x_mate
        )

    def product_x(unit):
        left, right = UNITS[unit][0]
        n, i = left - 8, right // 2
        need(right, col_copies)
        need(("fx", i))
        flat = (4 * PIECE, tokens)
        total = matmul(row_half(left, x), col_ref(right)[...])
        total += matmul(rows_sib[left, :, x].reshape(flat), cols_sib[right])
        for k in range(2):
            need(("rx", n, k))
            total += matmul(rows_x[k, n].reshape(flat), cols_x[k, i])
        total = total.astype(low).reshape(2, 2, PIECE, width)
        part[unit, 0, x] = total[..., :half_width]
        part[unit, 1, x] = total[..., half_width:]

    def start_y(unit):
        if ("ry", 0) not in cross:
            sem = row_y_recv
            cross_send(("ry", 0), rows.at[6, :, :, core], rows_y.at[0], sem, 0, y_mate)
            for k in range(4):
                pass_col_y(k)
            need(6, row_copies)
            cross_send(("ry", 1), rows_sib.at[6], rows_y.at[1], sem, 1, y_mate)

    def product_y(unit):
        left, right = UNITS[unit][0]
        k = right - 3
        need(right, col_copies)
        need(("fy", k))
        flat = (4 * PIECE, tokens)
        for i in range(2):
            need(("ry", i))
        for side in range(2):
            total = matmul(row_half(left, side), cols[2 + k, :, lanes_of[0]])
            total += matmul(
                rows_sib[left, :, side].reshape(flat), cols_sib[right, :, lanes_of[0]]
            )
            for i in range(2):
                total += matmul(rows_y[i, :, side].reshape(flat), cols_y[i, k])
            part[unit, y, side] = total.astype(low).reshape(2, 2, PIECE, half_width)

    axes = ("y", "x", "h", "l")
    recvs = (recv_one, recv_two, recv_three, recv_four)
    copies, last = {}, {}
    units = len(UNITS)

    def half(unit, side):
        total = None
        for left, right in UNITS[unit]:
            need(left, row_copies)
            need(right, col_copies)
            term = matmul(row_half(left, side), col_ref(right)[...])
            term += matmul(
                rows_sib[left, :, side].reshape(4 * PIECE, tokens), cols_sib[right]
            )
            total = term if total is None else total + term
        total = total.astype(low).reshape(2, 2, PIECE, width)
        part[unit, 0, side] = total[..., :half_width]
        part[unit, 1, side] = total[..., half_width:]

    def place(done, axis, index):
        fixed = {name: own[name] for name in done}
        fixed[axis] = index
        left = [name for name in axes if name not in done]
        inside = tuple(index if name == axis else slice(None) for name in left)
        return tuple(fixed.get(name, slice(None)) for name in axes), inside

    def landing(unit, stage):
        return WHOLE.index(unit) if stage == 0 else unit

    def push(unit, stage):
        order = ORDERS[unit]
        axis = order[stage]
        where, _ = place(order[:stage], axis, 1 - own[axis])
        copies[unit, stage] = send(
            part.at[(unit, *where)],
            recvs[stage].at[landing(unit, stage)],
            stage_recv.at[stage, unit],
            mates[axis],
        )

    def start(unit):
        if unit in CROSS_X:
            start_x(unit)
        elif unit in CROSS_Y:
            start_y(unit)
        elif ORDERS[unit][0] == "x":
            half(unit, 1 - x)
            push(unit, 0)
            half(unit, x)
        else:
            half(unit, 0)
            half(unit, 1)
            push(unit, 0)

    def add(unit, stage, axis, index):
        where, inside = place(ORDERS[unit][: stage + 1], axis, index)
        mine = part[(unit, *where)].astype(jnp.float32)
        part[(unit, *where)] = (mine + recvs[stage][(landing(unit, stage), *inside)].astype(jnp.float32)).astype(low)

    def advance(unit, stage):
        if stage == 0 and unit not in WHOLE:
            if unit in CROSS_X:
                product_x(unit)
            else:
                product_y(unit)
            push(unit, 1)
            return
        copies[unit, stage].wait_recv()
        axis = ORDERS[unit][stage + 1]
        add(unit, stage, axis, 1 - own[axis])
        push(unit, stage + 1)
        add(unit, stage, axis, own[axis])

    def close(unit):
        copies[unit, 3].wait_recv()
        total = part[(unit, *(own[name] for name in axes))].astype(jnp.float32)
        sums[unit, core] = (total + recv_four[unit].astype(jnp.float32)).astype(low)
        last[unit] = send(
            sums.at[unit, core],
            sums.at[unit, core],
            last_recv.at[unit],
            sibling,
        )

    step_rows = tokens

    def over_rows(body, init=0):
        return body(slice(None), 0, init)

    def over_pieces(body, init=0):
        for p in range(blocks):
            init = body(p, init)
        return init

    def spot(p):
        return p // 4, (p // 2) % 2, p % 2

    def put_t(index, value):
        rows[index] = value.reshape(4, 2, 2, PIECE, tokens)

    def get_t(index):
        return rows[index].reshape(width, tokens)

    def fold(value):
        return value.reshape(PIECE // 8, 8, tokens).sum(0)

    banks_in = (adapt_down, adapt_up)
    half_bank = width // 8
    far = flip(bn, 2)

    def bank_half(bank, side):
        return bank.at[pl.ds(pl.multiple_of(side * half_bank, half_bank), half_bank), :]

    bank_y, bank_x, bank_sib = [], [], [[], []]

    def send_bank(source, i, where, kind, mate):
        return send(
            source, banks.at[(i, *where)], bank_recv.at[i, kind], mate
        )

    def pass_from_y(i):
        bank_y[i].wait_recv()
        source = banks.at[i, far, x]
        bank_x.append(send_bank(source, i, (far, x), 3, x_mate))
        bank_sib[i].append(send_bank(source, i, (far, x), 4, sibling))

    def pass_from_x(i):
        bank_x[i].wait_recv()
        source = banks.at[i, far, 1 - x]
        bank_sib[i].append(send_bank(source, i, (far, 1 - x), 5, sibling))

    def open_links():
        pl.semaphore_wait(barrier, 1 + len(mates))
        for i in range(2):
            bank_y.append(send_bank(bank_half(banks_in[i], x), i, (bn, x), 0, y_mate))
        for i in range(2):
            for side in range(2):
                source = bank_half(banks_in[i], side)
                bank_sib[i].append(send_bank(source, i, (bn, side), 1 + side, sibling))
        share_col(0)
        half_hidden_over_x(0)

    length = lengths[0]
    for k in range(3):
        slot = take()
        value = matmul(hidden[...], ring[slot])
        release(slot)
        if k == 0:
            value = value * 0.125
        qkv_t[pl.ds(k * width, width), :] = value.astype(low).T
        if k == 0:
            open_links()
    size = width // heads

    def head_rows(k, head):
        return pl.ds(pl.multiple_of(k * width + head * size, size), size)

    valid_keys = lax.broadcasted_iota(jnp.int32, (tokens, tokens), 0) < length

    def head_forward(head, carry):
        scores = matmul_tn(qkv_t[head_rows(1, head), :], qkv_t[head_rows(0, head), :])
        scores = jnp.where(valid_keys, scores, masked_value)
        scores = jnp.exp(scores - jnp.max(scores, 0, keepdims=True))
        share = (scores * (1.0 / jnp.sum(scores, 0, keepdims=True))).astype(low)
        probs[head] = share
        context = matmul(qkv_t[head_rows(2, head), :], share)
        low_tmp_two[pl.ds(pl.multiple_of(head * size, size), size), :] = context.astype(low)
        return carry

    lax.fori_loop(0, heads, head_forward, 0, unroll=12)
    pass_from_y(0)
    cols[0] = low_tmp_two[...].T
    share_col(1)
    slot = take()
    acc[...] = matmul(cols[0], ring[slot])
    release(slot)

    def norm_rows(total):
        center = total - jnp.mean(total, -1, keepdims=True)
        rstd = lax.rsqrt(jnp.mean(center * center, -1, keepdims=True) + epsilon)
        return center * rstd, rstd

    def norm_first(r, i, carry):
        normed, rstd = norm_rows(hidden[r, :].astype(jnp.float32) + acc[r, :])
        stat[r, :] = jnp.broadcast_to(rstd, (step_rows, 128))
        low_tmp[r, :] = normed.astype(low)
        one_rows = normed * gain_attn
        wide[r, :] = one_rows
        cols[1, r, :] = one_rows.astype(low)
        return carry

    over_rows(norm_first)
    share_col(2)
    norm_one[...] = low_tmp[...].T.reshape(blocks, PIECE, tokens)
    stat_one[...] = stat[...].T[:8]

    for k in range(4):
        slot, slot_two = take(), take()
        acc[...] = matmul(cols[1], ring[slot])
        unit_base = 2 + (k % 2) * 2
        lanes = lanes_of[1 - k // 2]

        def gelu_rows(r, i, carry):
            before = acc[r, :]
            cdf, density = normal_parts(before)
            act = (before * cdf).astype(low)
            low_tmp[r, :] = act
            cols[unit_base, r, lanes] = act[:, :half_width]
            cols[unit_base + 1, r, lanes] = act[:, half_width:]
            cols[9, r, :] = (cdf + before * density).astype(low)
            return carry

        over_rows(gelu_rows)
        slope[pl.ds(ff_blocks[k] * blocks, blocks)] = cols[9].T.reshape(blocks, PIECE, tokens)
        value = matmul(low_tmp[...], ring[slot_two])
        acc_two[...] = value if k == 0 else acc_two[...] + value
        release(slot)
        release(slot_two)
        if k == 0:
            pass_from_y(1)
            half_hidden_over_x(1)
            col_over_x(1)
        if k < 2:
            col_over_y(2 * k)
            col_over_y(2 * k + 1)
        if k == 2:
            pass_from_x(0)
    for index in range(3, 7):
        share_col(index)

    def norm_second(r, i, carry):
        normed, rstd = norm_rows(wide[r, :] + acc_two[r, :])
        stat[r, :] = jnp.broadcast_to(rstd, (step_rows, 128))
        low_tmp[r, :] = normed.astype(low)
        two_rows = normed * gain_ff
        wide[r, :] = two_rows
        cols[6, r, :] = two_rows.astype(low)
        return carry

    over_rows(norm_second)
    share_col(7)
    norm_two[...] = low_tmp[...].T.reshape(blocks, PIECE, tokens)
    stat_two[...] = stat[...].T[:8]
    put_t(3, cols[6].T)
    share_row(3)

    slot_query, slot_key, slot_value = take(), take(), take()
    low_tmp[...] = matmul(cols[6], ring[slot_query]).astype(low)
    put_t(4, low_tmp[...].T)
    share_row(4)
    put_t(2, matmul(ring[slot_key], get_t(4)).astype(low))
    share_row(2)

    def bank_ready(i):
        for side in range(2):
            bank_own[2 * i + side].wait()
        for copy in bank_sib[i]:
            copy.wait_recv()

    bank_ready(0)
    acc_t[...] = matmul(banks[0].reshape(width, width), get_t(3)).reshape(blocks, PIECE, tokens)
    pass_from_x(1)
    bank_ready(1)
    acc_t_two[...] = matmul(banks[1].reshape(width, width), get_t(2)).reshape(
        blocks, PIECE, tokens
    )
    score_scale = 1.0 / math.sqrt(width)
    groups = PIECE // adapters

    def grouped(value):
        return value.reshape(groups, adapters, tokens)

    def adapter_rows(p, logits):
        inner = acc_t[p]
        cdf, density = normal_parts(inner)
        act = inner * cdf
        active[p] = act
        bank_slope[p] = (cdf + inner * density).astype(low)
        return logits + grouped(act * acc_t_two[p]).sum(0)

    logits = over_pieces(adapter_rows, jnp.zeros((adapters, tokens), jnp.float32)) * score_scale
    logits = jnp.exp(logits - jnp.max(logits, 0, keepdims=True))
    shares = logits / jnp.sum(logits, 0, keepdims=True)

    def spread(value):
        return jnp.concatenate([value] * groups, 0)

    wide_shares = spread(shares)

    def mixing_rows(p, carry):
        low_tmp_two[pl.ds(p * PIECE, PIECE), :] = (
            wide_shares * active[p]
        ).astype(low)
        return carry

    over_pieces(mixing_rows)
    cols[8] = low_tmp_two[...].T
    share_col(9)
    acc[...] = matmul(cols[8], banks[1].reshape(width, width))

    def joined_rows(r, i, carry):
        cols[7, r, :] = (wide[r, :] + acc[r, :]).astype(low)
        return carry

    over_rows(joined_rows)
    share_col(8)
    acc[...] = matmul(cols[7], ring[slot_value])

    upstream_copy.wait()

    def norm_third(r, i, gain_part):
        normed, rstd = norm_rows(wide[r, :] + acc[r, :])
        gain = gain_out
        acc_two[r, :] = normed * gain
        token = lax.broadcasted_iota(jnp.int32, (step_rows, 1), 0) + i * step_rows
        upstream = jnp.where(token < length, cotangent[r, :].astype(jnp.float32), 0.0)
        product = upstream * normed
        gained = upstream * gain
        third = rstd * (
            gained
            - jnp.mean(gained, -1, keepdims=True)
            - normed * jnp.mean(gained * normed, -1, keepdims=True)
        )
        low_tmp[r, :] = third.astype(low)
        return gain_part + product.reshape(step_rows // 8, 8, width).sum(0)

    gain_part = over_rows(norm_third, jnp.zeros((8, width), jnp.float32))
    out_copy = pltpu.make_async_copy(acc_two, output, local_sem.at[0])
    out_copy.start()
    gain_sum[0] = jnp.broadcast_to(jnp.sum(gain_part, 0, keepdims=True), (8, width))
    put_t(0, low_tmp[...].T)
    share_row(0)

    state = {}

    def value_back():
        second[...] = matmul(ring[slot_value], get_t(0)).reshape(blocks, PIECE, tokens)
        release(slot_value)

        def mix_rows(p, carry):
            zz, xx, cc = spot(p)
            rows[1, zz, xx, cc] = second[p].astype(low)
            return carry

        over_pieces(mix_rows)
        share_row(1)
        acc_t[...] = matmul(banks[1].reshape(width, width), get_t(1)).reshape(blocks, PIECE, tokens)

    def adapter_grads():
        def share_rows(p, total):
            return total + grouped(acc_t[p] * active[p]).sum(0)

        share_grad = over_pieces(share_rows, jnp.zeros((adapters, tokens), jnp.float32))
        logit_grad = shares * (share_grad - jnp.sum(shares * share_grad, 0, keepdims=True))
        wide_logit = spread(logit_grad * score_scale)

        def adapter_back(p, carry):
            act_grad = acc_t[p] * wide_shares + wide_logit * acc_t_two[p]
            where = pl.ds(p * PIECE, PIECE)
            low_tmp_two[where, :] = (wide_logit * active[p]).astype(low)
            bank_slope[p] = (bank_slope[p].astype(jnp.float32) * act_grad).astype(low)
            return carry

        over_pieces(adapter_back)
        cols[9] = low_tmp_two[...].T
        share_col(10)
        cols[10] = bank_slope[...].reshape(width, tokens).T
        share_col(11)

    def probe_back():
        cols[11] = matmul(cols[9], banks[1].reshape(width, width)).astype(low)
        share_col(12)
        low_tmp[...] = matmul(cols[11], ring[slot_key]).astype(low)
        release(slot_key)
        put_t(5, low_tmp[...].T)
        share_row(5)
        low_tmp[...] = matmul(cols[10], banks[0].reshape(width, width)).astype(low)
        low_tmp_two[...] = low_tmp[...].T
        acc_t[...] = matmul(ring[slot_query], get_t(5)).reshape(blocks, PIECE, tokens)
        release(slot_query)

    def norm_back(index, gain, normed_ref, stat_ref, upstream_of, factor):
        gain_col[...] = jnp.broadcast_to(gain, (128, width)).T.reshape(blocks, PIECE, 128)

        def gained(p):
            column = gain_col[p]
            return acc_t[p] * jnp.concatenate([column] * (tokens // 128), 1)

        def first_pass(p, carry):
            upstream = upstream_of(p)
            acc_t[p] = upstream
            normed = normed_ref[p].astype(jnp.float32)
            gain_of = jnp.sum(upstream * normed, -1, keepdims=True)
            weighted = gained(p)
            gain_col[p] = jnp.broadcast_to(gain_of, (PIECE, 128))
            acc_t[p] = weighted
            return carry[0] + fold(weighted), carry[1] + fold(weighted * normed)

        zeros = jnp.zeros((8, tokens), jnp.float32)
        plain, tilted = over_pieces(first_pass, (zeros, zeros))
        mean_plain = jnp.sum(plain, 0, keepdims=True) * (1.0 / width)
        mean_tilted = jnp.sum(tilted, 0, keepdims=True) * (1.0 / width)
        rstd = stat_ref[0:1, :]

        def second_pass(p, carry):
            value = rstd * (acc_t[p] - mean_plain - normed_ref[p].astype(jnp.float32) * mean_tilted)
            second[p] = value
            zz, xx, cc = spot(p)
            rows[factor, zz, xx, cc] = value.astype(low)
            return carry

        over_pieces(second_pass)
        gain_sum[0, index : index + 1, :] = gain_col[...].reshape(width, 128).T[:1]

    def upstream_two(p):
        zz, xx, cc = spot(p)
        where = pl.ds(p * PIECE, PIECE)
        total = rows[0, zz, xx, cc].astype(jnp.float32) + second[p]
        return total + low_tmp_two[where, :].astype(jnp.float32) + acc_t[p]

    def norm_two_back():
        norm_back(1, gain_ff, norm_two, stat_two, upstream_two, 6)
        share_row(6)

    def ff_back(k):
        slot, slot_two = take(), take()
        acc_t_two[...] = matmul(ring[slot], get_t(6)).reshape(blocks, PIECE, tokens)

        def slope_rows(p, carry):
            value = acc_t_two[p] * slope[k * blocks + p].astype(jnp.float32)
            rows_ff[k, p // 8, (p % 8) // 2, p % 2] = value.astype(low)
            return carry

        over_pieces(slope_rows)
        value = matmul(ring[slot_two], rows_ff[k].reshape(width, tokens))
        value = value.reshape(blocks, PIECE, tokens)
        release(slot)
        release(slot_two)
        acc_t[...] = value if k == 0 else acc_t[...] + value
        if k == 3:
            for index in range(8, 12):
                share_row(index)

    def upstream_one(p):
        return second[p] + acc_t[p]

    def norm_one_back():
        norm_back(0, gain_attn, norm_one, stat_one, upstream_one, 7)
        share_row(7)
        slot = take()
        low_tmp_two[...] = matmul(ring[slot], get_t(7)).astype(low)
        release(slot)

    heads_step = 3
    step_pieces = heads_step * size // PIECE

    def head_backward(group, carry):
        grads = [[], [], []]
        for i in range(heads_step):
            head = group * heads_step + i
            query, key, value = [qkv_t[head_rows(k, head), :] for k in range(3)]
            upstream = low_tmp_two[pl.ds(pl.multiple_of(head * size, size), size), :]
            share = probs[head]
            share_wide = share.astype(jnp.float32)
            prob_grad = matmul_tn(value, upstream)
            delta = jnp.sum(share_wide * prob_grad, 0, keepdims=True)
            score_grad = (share_wide * (prob_grad - delta)).astype(low)
            grads[0].append((matmul(key, score_grad) * 0.125).astype(low))
            grads[1].append(matmul_t(query, score_grad).astype(low))
            grads[2].append(matmul_t(upstream, share).astype(low))
        for k in range(3):
            stacked = jnp.concatenate(grads[k], 0).reshape(step_pieces, PIECE, tokens)
            for i in range(step_pieces):
                p = k * blocks + group * step_pieces + i
                rows_qkv[p // 12, (p // 6) % 2, (p % 6) // 2, p % 2] = stacked[i]
        return carry

    def attention_back():
        lax.fori_loop(0, heads // heads_step, head_backward, 0)
        for index in range(12, 15):
            share_row(index)

    def input_back():
        for k in range(3):
            slot = take()
            block = rows_qkv[...].reshape(3 * blocks, PIECE, tokens)[k * blocks : (k + 1) * blocks]
            value = matmul(ring[slot], block.reshape(width, tokens)).reshape(blocks, PIECE, tokens)
            release(slot)
            second[...] = second[...] + value
        acc[...] = second[...].reshape(width, tokens).T
        state["in"] = pltpu.make_async_copy(acc, grad_in, local_sem.at[1])
        state["in"].start()

    gain_mates = (sibling, x_mate, y_mate, mates["l"], mates["h"])

    def gain_step(stage):
        if stage > 0:
            state["gain"].wait_recv()
            total = gain_sum[stage - 1] + gain_from[stage - 1]
            if stage == 5:
                gain_sums[...] = total
                return
            gain_sum[stage] = total
        state["gain"] = send(
            gain_sum.at[stage],
            gain_from.at[stage],
            gain_recv.at[stage],
            gain_mates[stage],
        )

    chain = [value_back, adapter_grads, probe_back, norm_two_back]
    chain += [functools.partial(ff_back, k) for k in range(4)]
    chain += [norm_one_back, attention_back, input_back]
    progress = [0] * units
    since_chain, gain_stage = 0, 0
    for action in SEQUENCE:
        if action < 0:
            chain.pop(0)()
        elif progress[action] == 0:
            start(action)
        elif progress[action] < 4:
            advance(action, progress[action] - 1)
        else:
            close(action)
        if action >= 0:
            progress[action] += 1
        if not chain:
            if since_chain % 4 == 0 and gain_stage < 6:
                gain_step(gain_stage)
                gain_stage += 1
            since_chain += 1
    for stage in range(gain_stage, 6):
        gain_step(stage)
    for unit in range(units):
        last[unit].wait_recv()
    for copy in started[-SENDS:]:
        copy.wait_send()
    out_copy.wait()
    state["in"].wait()


def run_layer(heads, adapters, arrays):
    hidden = arrays[0]
    tokens, width = hidden.shape
    low, wide = jnp.bfloat16, jnp.float32
    blocks = width // PIECE
    units = len(UNITS)
    dma = pltpu.SemaphoreType.DMA
    vmem = pl.BlockSpec(memory_space=pltpu.VMEM)
    smem = pl.BlockSpec(memory_space=pltpu.SMEM)
    far = pl.BlockSpec(memory_space=pl.ANY)
    half_width = width // 2
    return pl.pallas_call(
        functools.partial(layer_kernel, heads, adapters),
        out_shape=(
            jax.ShapeDtypeStruct((tokens, width), wide),
            jax.ShapeDtypeStruct((tokens, width), wide),
            jax.ShapeDtypeStruct((units, 2, PIECE, half_width), low),
            jax.ShapeDtypeStruct((8, width), wide),
        ),
        in_specs=[
            vmem, smem, far, far, far, vmem, far, far, vmem, far, far, far, far, far, vmem,
        ],
        out_specs=[far, far, vmem, vmem],
        scratch_shapes=[
            pltpu.VMEM((8, 4, 2, 2, PIECE, tokens), low),
            pltpu.VMEM((4, 2, 4, 2, PIECE, tokens), low),
            pltpu.VMEM((4, 2, 3, 2, PIECE, tokens), low),
            pltpu.VMEM((15, 4, 2, PIECE, tokens), low),
            pltpu.VMEM((12, tokens, width), low),
            pltpu.VMEM((13, tokens, width), low),
            pltpu.VMEM((2, 7, 4, PIECE, tokens), low),
            pltpu.VMEM((2, 2, tokens, width), low),
            pltpu.VMEM((2, 4, 2, PIECE, tokens), low),
            pltpu.VMEM((2, 4, tokens, half_width), low),
            pltpu.VMEM((SLOTS, width, width), low),
            pltpu.VMEM((2, 4, 2, width // 8, width), low),
            pltpu.VMEM((tokens, width), wide),
            pltpu.VMEM((tokens, width), wide),
            pltpu.VMEM((tokens, width), wide),
            pltpu.VMEM((blocks, PIECE, tokens), wide),
            pltpu.VMEM((blocks, PIECE, tokens), wide),
            pltpu.VMEM((blocks, PIECE, tokens), wide),
            pltpu.VMEM((blocks, PIECE, tokens), low),
            pltpu.VMEM((blocks, PIECE, tokens), wide),
            pltpu.VMEM((blocks, PIECE, tokens), low),
            pltpu.VMEM((blocks, PIECE, tokens), low),
            pltpu.VMEM((4 * blocks, PIECE, tokens), low),
            pltpu.VMEM((3 * width, tokens), low),
            pltpu.VMEM((heads, tokens, tokens), low),
            pltpu.VMEM((tokens, width), low),
            pltpu.VMEM((width, tokens), low),
            pltpu.VMEM((tokens, 128), wide),
            pltpu.VMEM((8, tokens), wide),
            pltpu.VMEM((8, tokens), wide),
            pltpu.VMEM((blocks, PIECE, 128), wide),
            pltpu.VMEM((tokens, width), low),
            pltpu.VMEM((units, 2, 2, 2, 2, PIECE, half_width), low),
            pltpu.VMEM((len(WHOLE), 2, 2, 2, PIECE, half_width), low),
            pltpu.VMEM((units, 2, 2, PIECE, half_width), low),
            pltpu.VMEM((units, 2, PIECE, half_width), low),
            pltpu.VMEM((units, PIECE, half_width), low),
            pltpu.VMEM((5, 8, width), wide),
            pltpu.VMEM((5, 8, width), wide),
            dma((SLOTS,)),
            dma((7,)),
            dma((SENDS,)),
            dma((2, 6)),
            dma((15,)),
            dma((13,)),
            dma((2, 7)),
            dma((2, 2)),
            dma((2,)),
            dma((2,)),
            dma((2, 4)),
            dma((4, units)),
            dma((units,)),
            dma((5,)),
        ],
        compiler_params=pltpu.CompilerParams(
            collective_id=0, has_side_effects=True, vmem_limit_bytes=63 * 2**20
        ),
    )(*arrays)


def finish_kernel(
    sums_far,
    gain_sums_far,
    output,
    grad_in,
    out_output,
    out_grad_in,
    out_qkv,
    out_proj,
    out_gain_attn,
    out_ff_in,
    out_ff_out,
    out_gain_ff,
    out_query,
    out_key,
    out_value,
    out_down,
    out_up,
    out_gain_out,
    turned,
    sums,
    gain_sums,
    held,
    copy_sem,
):
    fetched = [
        pltpu.make_async_copy(sums_far, sums, copy_sem.at[2]),
        pltpu.make_async_copy(gain_sums_far, gain_sums, copy_sem.at[3]),
    ]
    through = [
        pltpu.make_async_copy(output, held.at[0], copy_sem.at[0]),
        pltpu.make_async_copy(grad_in, held.at[1], copy_sem.at[1]),
    ]
    for copy in fetched + through:
        copy.start()
    for copy in fetched:
        copy.wait()
    ad = lax.axis_index("ad")
    core = lax.axis_index("bn") % 2
    width = sums.shape[3]
    own = pl.ds(pl.multiple_of(core * (width // 2), width // 2), width // 2)

    def columns(out, slot, first, count):
        value = sums[first : first + count].reshape(count * 2 * PIECE, width)
        extent = pl.ds(0, count * 2 * PIECE)
        turned[slot, :, extent] = value.astype(jnp.float32).T
        out[...] = turned[slot, own, extent]

    columns(out_value, 0, 0, 1)
    columns(out_up, 1, 1, 1)
    columns(out_down, 2, 2, 1)
    columns(out_key, 0, 3, 1)
    columns(out_query, 1, 4, 1)
    for copy in through:
        copy.wait()
    passed = [
        pltpu.make_async_copy(held.at[0], out_output, copy_sem.at[0]),
        pltpu.make_async_copy(held.at[1], out_grad_in, copy_sem.at[1]),
    ]
    for copy in passed:
        copy.start()
    columns(out_ff_in, 2, 9, 4)
    columns(out_proj, 0, 13, 1)
    columns(out_qkv, 1, 14, 3)
    for i in range(2):
        value = sums[5 + 2 * core + i].reshape(2 * PIECE, width)
        out_ff_out[:, pl.ds(i * width, width)] = value.astype(jnp.float32)
    total = gain_sums.shape[1]
    piece = out_gain_attn.shape[0]
    rolled = pltpu.roll(gain_sums[...], lax.rem(total - ad * piece, total), 1)[:, :piece]
    for index, out in enumerate((out_gain_attn, out_gain_ff, out_gain_out)):
        out[...] = rolled[index : index + 1].reshape(piece)
    for copy in passed:
        copy.wait()


def finish(sums, gain_sums, output, grad_in, width):
    quarter, eighth = width // 4, width // 8
    far = pl.BlockSpec(memory_space=pl.ANY)
    shapes = [
        output.shape,
        grad_in.shape,
        (quarter, 3 * eighth),
        (quarter, eighth),
        (eighth,),
        (quarter, 4 * eighth),
        (eighth, 4 * quarter),
        (eighth,),
    ]
    shapes += [(quarter, eighth)] * 5 + [(eighth,)]
    return pl.pallas_call(
        finish_kernel,
        out_shape=tuple(jax.ShapeDtypeStruct(shape, jnp.float32) for shape in shapes),
        in_specs=[far] * 4,
        out_specs=[far] * 2 + [pl.BlockSpec(memory_space=pltpu.VMEM)] * 12,
        scratch_shapes=[
            pltpu.VMEM((3, width // 2, 4 * eighth), jnp.float32),
            pltpu.VMEM(sums.shape, sums.dtype),
            pltpu.VMEM(gain_sums.shape, gain_sums.dtype),
            pltpu.VMEM((2, *output.shape), output.dtype),
            pltpu.SemaphoreType.DMA((4,)),
        ],
        compiler_params=pltpu.CompilerParams(vmem_limit_bytes=62 * 2**20),
    )(sums, gain_sums, output, grad_in)


def fast_local(*arrays):
    arrays = list(arrays)
    width = arrays[0].shape[1]
    adapters = arrays[12].shape[1]
    bank_shape = arrays[12].shape[:2] + (-1,)
    for i in (12, 13):
        arrays[i] = arrays[i].reshape(-1, width)
    output, grad_in, sums, gain_sums = run_layer(H, adapters, arrays)
    results = list(finish(sums, gain_sums, output, grad_in, width))
    results[6] = results[6].T
    for i in (11, 12):
        results[i] = results[i].reshape(bank_shape)
    return tuple(results)


def local(
    hidden_in,
    lengths,
    cotangent,
    w_qkv,
    w_out,
    gain_attn,
    w_ff_in,
    w_ff_out,
    gain_ff,
    join_query,
    join_key,
    join_value,
    adapt_down,
    adapt_up,
    gain_out,
):
    seq_count = lengths.shape[0]
    tok_rows, model_width = hidden_in.shape
    slot_len = tok_rows // seq_count
    head_count = H
    head_size = model_width // head_count
    score_scale = 1.0 / math.sqrt(head_size)
    adapters = adapt_down.shape[1]
    down_flat = lax.all_gather(adapt_down.reshape(-1, model_width), "bn", axis=0, tiled=True)
    up_flat = lax.all_gather(adapt_up.reshape(-1, model_width), "bn", axis=0, tiled=True)
    valid = lax.broadcasted_iota(jnp.int32, (seq_count, slot_len), 1) < lengths[:, None]
    row_ok = valid.reshape(tok_rows, 1).astype(jnp.float32)
    tokens_wide = hidden_in.astype(jnp.float32)
    qkv = matmul(hidden_in, w_qkv).astype(jnp.bfloat16)
    queries = qkv[:, :model_width].reshape(seq_count, slot_len, head_count, head_size)
    key_rows = qkv[:, model_width : 2 * model_width].reshape(
        seq_count, slot_len, head_count, head_size
    )
    values = qkv[:, 2 * model_width :].reshape(seq_count, slot_len, head_count, head_size)

    def attend_scores():
        raw_scores = (
            jnp.einsum("sqhe,skhe->shqk", queries, key_rows, preferred_element_type=jnp.float32)
            * score_scale
        )
        return jnp.where(valid[:, None, None, :], raw_scores, masked_value)

    scores = attend_scores()
    row_max = jnp.max(scores, -1, keepdims=True)
    log_total = row_max + jnp.log(jnp.sum(jnp.exp(scores - row_max), -1, keepdims=True))
    probs = jnp.exp(scores - log_total).astype(jnp.bfloat16)
    context = (
        jnp.einsum("shqk,skhe->sqhe", probs, values, preferred_element_type=jnp.float32)
        .reshape(tok_rows, model_width)
        .astype(jnp.bfloat16)
    )
    attn_out = matmul(context, w_out)
    hidden_one, norm_one_back = jax.vjp(layer_norm, tokens_wide + attn_out, gain_attn)
    hidden_one_low = hidden_one.astype(jnp.bfloat16)
    ff_pre = matmul(hidden_one_low, w_ff_in)
    ff_act, gelu_ff_back = jax.vjp(gelu_exact, ff_pre)
    ff_low = ff_act.astype(jnp.bfloat16)
    ff_out = matmul(ff_low, w_ff_out)
    hidden_two, norm_two_back = jax.vjp(layer_norm, hidden_one + ff_out, gain_ff)
    hidden_low = hidden_two.astype(jnp.bfloat16)
    query_join = matmul(hidden_low, join_query).astype(jnp.bfloat16)
    probe = matmul_t(query_join, join_key).astype(jnp.bfloat16)
    mixing, kept_state = adapter_forward(hidden_low, probe, down_flat, up_flat, adapters)
    joined_in = (hidden_two + matmul(mixing, up_flat)).astype(jnp.bfloat16)
    joined = matmul(joined_in, join_value)
    output, norm_out_back = jax.vjp(layer_norm, hidden_two + joined, gain_out)
    out_grad = cotangent.astype(jnp.float32) * row_ok
    sum_three, gain_out_grad = norm_out_back(out_grad)
    joined_grad = sum_three.astype(jnp.bfloat16)
    into_joined = matmul_t(joined_grad, join_value)
    mix_grad = into_joined.astype(jnp.bfloat16)
    inner_grad, weigh_grad = adapter_backward(kept_state, up_flat, mix_grad, adapters)
    hidden_back = matmul(inner_grad, down_flat)
    probe_grad = matmul(weigh_grad, up_flat).astype(jnp.bfloat16)
    query_in = matmul(probe_grad, join_key).astype(jnp.bfloat16)
    grad_two = sum_three + into_joined + hidden_back + matmul_t(query_in, join_query)
    sum_two, gain_ff_grad = norm_two_back(grad_two)
    ff_out_grad = sum_two.astype(jnp.bfloat16)
    ff_pre_grad = gelu_ff_back(matmul_t(ff_out_grad, w_ff_out))[0].astype(jnp.bfloat16)
    grad_one = sum_two + matmul_t(ff_pre_grad, w_ff_in)
    sum_one, gain_attn_grad = norm_one_back(grad_one)
    attn_grad = sum_one.astype(jnp.bfloat16)
    context_grad = (
        matmul_t(attn_grad, w_out)
        .astype(jnp.bfloat16)
        .reshape(seq_count, slot_len, head_count, head_size)
    )
    probs_wide = jnp.exp(attend_scores() - log_total)
    prob_grad = jnp.einsum(
        "sqhe,skhe->shqk", context_grad, values, preferred_element_type=jnp.float32
    )
    row_delta = jnp.sum(probs_wide * prob_grad, -1, keepdims=True)
    score_grad = (probs_wide * (prob_grad - row_delta)).astype(jnp.bfloat16)
    query_back = (
        jnp.einsum("shqk,skhe->sqhe", score_grad, key_rows, preferred_element_type=jnp.float32)
        * score_scale
    )
    key_back = (
        jnp.einsum("shqk,sqhe->skhe", score_grad, queries, preferred_element_type=jnp.float32)
        * score_scale
    )
    value_back = jnp.einsum(
        "shqk,sqhe->skhe", probs, context_grad, preferred_element_type=jnp.float32
    )
    qkv_grad = jnp.concatenate(
        [
            query_back.reshape(tok_rows, model_width),
            key_back.reshape(tok_rows, model_width),
            value_back.reshape(tok_rows, model_width),
        ],
        1,
    ).astype(jnp.bfloat16)
    grad_in = sum_one + matmul_t(qkv_grad, w_qkv)
    def shared_sum(gradient):
        columns = lax.psum_scatter(gradient, "ad", scatter_dimension=1, tiled=True)
        return lax.psum_scatter(
            columns.astype(jnp.bfloat16), "bn", scatter_dimension=0, tiled=True
        ).astype(jnp.float32)

    gains = lax.psum(
        lax.psum_scatter(
            jnp.stack([gain_attn_grad, gain_ff_grad, gain_out_grad]),
            "ad",
            scatter_dimension=1,
            tiled=True,
        ),
        "bn",
    )
    down_grad = shared_sum(matmul_tn(inner_grad, hidden_low))
    up_grad = shared_sum(matmul_tn(mixing, mix_grad) + matmul_tn(weigh_grad, probe))
    bank = adapt_down.shape[:2] + (-1,)
    return (
        output,
        grad_in,
        shared_sum(matmul_tn(hidden_in, qkv_grad)),
        shared_sum(matmul_tn(context, attn_grad)),
        gains[0],
        shared_sum(matmul_tn(hidden_one_low, ff_pre_grad)),
        shared_sum(matmul_tn(ff_low, ff_out_grad)),
        gains[1],
        shared_sum(matmul_tn(hidden_low, query_in)),
        shared_sum(matmul_tn(probe_grad, query_join)),
        shared_sum(matmul_tn(joined_in, joined_grad)),
        down_grad.reshape(bank),
        up_grad.reshape(bank),
        gains[2],
    )


def solution(mesh):
    placed = (
        P(("ad", "bn"), None),
        P(("ad", "bn")),
        P(("ad", "bn"), None),
        P(),
        P(),
        P(),
        P(),
        P(),
        P(),
        P(),
        P(),
        P(),
        P("bn", None, None),
        P("bn", None, None),
        P(),
    )
    sizes = (mesh.shape["ad"], mesh.shape["bn"])
    return jax.shard_map(
        fast_local if sizes == (8, 4) else local,
        mesh=mesh,
        in_specs=placed,
        out_specs=(
            P(("ad", "bn"), None),
            P(("ad", "bn"), None),
            P("bn", "ad"),
            P("bn", "ad"),
            P("ad"),
            P("bn", "ad"),
            P("bn", "ad"),
            P("ad"),
            P("bn", "ad"),
            P("bn", "ad"),
            P("bn", "ad"),
            P("bn", None, "ad"),
            P("bn", None, "ad"),
            P("ad"),
        ),
        check_vma=False,
    )
```
